128 devices in a mesh: fsdp: 8 (over y, x_lo), ctx: 4 (over x_hi, core), tp: 4 (over z).
Axes of the slice: x: 4 (x_hi: 2, x_lo: 2; x = x_hi * 2 + x_lo), y: 4, z: 4, core: 2. Of those that a mesh axis runs over, the one named last changes fastest.
Arguments:
- block_input: bfloat16 [8192, 1024], P(('fsdp', 'ctx')), may hold values from -6 to 6
- cotangent: bfloat16 [8192, 1024], P(('fsdp', 'ctx')), may hold values from -6 to 6
- sequence_starts: int32 [8, 2], P('fsdp'), may hold values from 1 to 1023, as said below
- attention_weight: float32 [2, 1024, 4, 1024], P(None, ('fsdp', 'ctx'), None, 'tp')
- attention_first: float32 [2, 1024, 4, 1024], P(None, ('fsdp', 'ctx'), None, 'tp'), may hold values from -32 to 32
- attention_second: float32 [2, 1024, 4, 1024], P(None, ('fsdp', 'ctx'), None, 'tp'), may hold values from 106.496 to 425.984
- feedforward_weight: float32 [2, 1024, 2, 4096], P(None, ('fsdp', 'ctx'), None, 'tp'), may hold values from -0.1875 to 0.1875
- feedforward_first: float32 [2, 1024, 2, 4096], P(None, ('fsdp', 'ctx'), None, 'tp'), may hold values from -32 to 32
- feedforward_second: float32 [2, 1024, 2, 4096], P(None, ('fsdp', 'ctx'), None, 'tp'), may hold values from 147.456 to 589.824
- vector_weight: float32 [2, 12, 1024], P(None, None, ('fsdp', 'ctx', 'tp'))
- vector_first: float32 [2, 12, 1024], P(None, None, ('fsdp', 'ctx', 'tp')), may hold values from -64 to 64
- vector_second: float32 [2, 12, 1024], P(None, None, ('fsdp', 'ctx', 'tp')), may hold values from 409.6 to 1638.4
Outputs:
- block_output: float32 [8192, 1024], P(('fsdp', 'ctx'))
- input_gradient: float32 [8192, 1024], P(('fsdp', 'ctx'))
- attention_moment: float32 [2, 1024, 4, 1024], P(None, ('fsdp', 'ctx'), None, 'tp')
- attention_square: float32 [2, 1024, 4, 1024], P(None, ('fsdp', 'ctx'), None, 'tp')
- attention_updated: float32 [2, 1024, 4, 1024], P(None, ('fsdp', 'ctx'), None, 'tp')
- feedforward_moment: float32 [2, 1024, 2, 4096], P(None, ('fsdp', 'ctx'), None, 'tp')
- feedforward_square: float32 [2, 1024, 2, 4096], P(None, ('fsdp', 'ctx'), None, 'tp')
- feedforward_updated: float32 [2, 1024, 2, 4096], P(None, ('fsdp', 'ctx'), None, 'tp')
- vector_moment: float32 [2, 12, 1024], P(None, None, ('fsdp', 'ctx', 'tp'))
- vector_square: float32 [2, 12, 1024], P(None, None, ('fsdp', 'ctx', 'tp'))
- vector_updated: float32 [2, 12, 1024], P(None, None, ('fsdp', 'ctx', 'tp'))
The draws below stay inside these ranges and needn't reach their ends.
Inputs may be any that keep to these rules, and one draw needn't show every extreme that they name: `sequence_starts`: A group's sequences run from 0 to its first start, between the starts, and from the second start to 1024; the first start is below 256, the second above 768.
All inputs are finite; a program needn't handle non-finite values.
Results may differ from the reference program's by a relative error of at most 0.04.
Values may be sent and summed in bfloat16 or wider, within the bound.
No kernel may reach another device: no remote copies, remote signals or barrier semaphores. Data moves between devices by JAX's collectives and lax.ppermute only.
A program may use at most 128 MiB of HBM per device.

```python
import math
import jax
import jax.numpy as jnp
from jax import lax

D = 1024
H = 16
HD = 64
FF = 4096
LAYERS = 2
STEP = 10
TOK_DEV = 256
GROUP_TOK = 1024
TOKENS = 8192
VROWS = 12
N_FSDP = 8


def draw_sequence_starts(key, part):
    key = jax.random.fold_in(key, 11)
    first_key, second_key = jax.random.split(key)
    first_start = jax.random.randint(first_key, (N_FSDP,), 1, TOK_DEV)
    second_start = jax.random.randint(second_key, (N_FSDP,), GROUP_TOK - TOK_DEV + 1, GROUP_TOK)
    first_start = first_start.at[0].set(1)
    second_start = second_start.at[N_FSDP - 1].set(GROUP_TOK - 1)
    return jnp.stack([first_start, second_start], axis=1).astype(jnp.int32)


def draw_attention_weight(key, part):
    key = jax.random.fold_in(key, 23)
    slot_scale = jnp.array([1.0, 1.0, 1.0, 2.0], jnp.float32).reshape(1, 1, 4, 1) * D ** (-0.5)
    noise = jax.random.truncated_normal(key, -4.0, 4.0, (LAYERS, D, 4, D), jnp.float32)
    return noise * slot_scale


def draw_vector_weight(key, part):
    key = jax.random.fold_in(key, 37)
    row_index = jnp.arange(VROWS)
    gain_rows = (row_index == 0) | (row_index == 5)
    noise = jax.random.truncated_normal(key, -4.0, 4.0, (LAYERS, VROWS, D), jnp.float32)
    return jnp.where(gain_rows[None, :, None], 1.0 + 0.15 * noise, 0.3 * noise)


def steps_of(rng, dims, cuts, low, high):
    loudness = 1.0
    for dim, shards_of in cuts:
        steps = jax.random.uniform(jax.random.fold_in(jax.random.fold_in(rng, 6), dim), (shards_of,), jnp.float32, low / len(cuts), high / len(cuts))
        loudness = loudness * jnp.repeat(jnp.exp(steps), dims[dim] // shards_of).reshape((-1,) + (1,) * (len(dims) - 1 - dim))
    return loudness


def scatter_about(stream_key, extent, scale, limit, cuts=(), kind=jnp.bfloat16):
    entries = jax.random.normal(stream_key, extent, jnp.float32) * scale
    if len(cuts) > 0:
        entries = steps_of(stream_key, extent, cuts, -0.22, 0.18) * entries
    return jnp.clip(entries, min=-limit, max=limit).astype(kind)


def setup_inputs(seed: int = 0) -> dict:
    splits = jax.random.split(jax.random.key(seed), 13)
    return {
        "block_input": scatter_about(splits[0], (TOKENS, D), 1.0, 6.0, ((0, 32),)),
        "cotangent": scatter_about(splits[1], (TOKENS, D), 1.0, 6.0, ((0, 32),)),
        "sequence_starts": draw_sequence_starts(jax.random.fold_in(splits[12], 71), 0),
        "attention_weight": draw_attention_weight(jax.random.fold_in(splits[12], 71), 0),
        "attention_first": scatter_about(splits[4], (LAYERS, D, 4, D), (0.055 * TOKENS ** 0.5), 32.0, ((1, 32), (3, 4)), jnp.float32),
        "attention_second": jnp.clip(jnp.exp(math.log(425.984) - 1.3862944 * jax.random.uniform(splits[5], (LAYERS, D, 4, D), jnp.float32) ** steps_of(splits[5], (LAYERS, D, 4, D), ((1, 32), (3, 4)), -0.2, 0.2)), 106.496, 425.984),
        "feedforward_weight": scatter_about(splits[6], (LAYERS, D, 2, FF), D ** -0.5, 0.1875, ((1, 32), (3, 4)), jnp.float32),
        "feedforward_first": scatter_about(splits[7], (LAYERS, D, 2, FF), (0.067 * TOKENS ** 0.5), 32.0, ((1, 32), (3, 4)), jnp.float32),
        "feedforward_second": jnp.clip(jnp.exp(math.log(589.824) - 1.3862944 * jax.random.uniform(splits[8], (LAYERS, D, 2, FF), jnp.float32) ** steps_of(splits[8], (LAYERS, D, 2, FF), ((1, 32), (3, 4)), -0.2, 0.2)), 147.456, 589.824),
        "vector_weight": draw_vector_weight(jax.random.fold_in(splits[12], 71), 0),
        "vector_first": scatter_about(splits[10], (LAYERS, VROWS, D), (0.11 * TOKENS ** 0.5), 64.0, ((2, 128),), jnp.float32),
        "vector_second": jnp.clip(jnp.exp(math.log(1638.4) - 1.3862944 * jax.random.uniform(splits[11], (LAYERS, VROWS, D), jnp.float32) ** steps_of(splits[11], (LAYERS, VROWS, D), ((2, 128),), -0.2, 0.2)), 409.6, 1638.4),
    }


@jax.custom_vjp
def low(v):
    return lax.optimization_barrier(v.astype(jnp.bfloat16)).astype(jnp.float32)

@jax.custom_vjp
def low_back(v):
    return v

def low_keep(v):
    return (low(v), None)

def low_pass(kept, grad):
    return (grad,)

def back_keep(v):
    return (v, None)

def back_low(kept, grad):
    return (low(grad),)
low.defvjp(low_keep, low_pass)
low_back.defvjp(back_keep, back_low)
highest = lax.Precision.HIGHEST
norm_eps = 1e-05
gelu_factor = 0.7978845608028654
matrix_rate = 0.05
vector_rate = 0.3
weight_decay = 0.1

def layer_norm(values, gain_row, shift_row):
    centre = values - lax.optimization_barrier(jnp.mean(values, axis=-1, keepdims=True))
    spread = lax.optimization_barrier(jnp.mean(centre * centre, axis=-1, keepdims=True))
    return centre * lax.rsqrt(spread + norm_eps) * gain_row + shift_row

def gelu_tanh(values):
    return 0.5 * values * (1.0 + jnp.tanh(gelu_factor * (values + 0.044715 * values * values * values)))

def segment_of(position, bounds):
    return (position >= bounds[0]).astype(jnp.int32) + (position >= bounds[1]).astype(jnp.int32)

def attend_group(operands):
    queries, key_rows, value_rows, bounds = operands
    length = queries.shape[0]
    block_rows = min(512, length)
    slopes = jnp.exp2(-8.0 * (jnp.arange(H).astype(jnp.float32) + 1.0) / H)
    key_place = jnp.arange(length).astype(jnp.int32)
    key_segment = segment_of(key_place, bounds)

    def one_block(row_start):
        query_rows = lax.dynamic_slice_in_dim(queries, row_start, block_rows, 0)
        row_place = row_start + jnp.arange(block_rows).astype(jnp.int32)
        distance = (row_place[:, None] - key_place[None, :]).astype(jnp.float32)
        raw_scores = jnp.einsum('qhe,khe->hqk', query_rows, key_rows, precision=highest) * 0.125 - slopes[:, None, None] * distance[None]
        scores = low_back(raw_scores)
        allowed = (segment_of(row_place, bounds)[:, None] == key_segment[None, :]) & (row_place[:, None] >= key_place[None, :])
        scores = jnp.where(allowed[None], scores, -1e+30)
        exponent = jnp.exp(scores - lax.optimization_barrier(jnp.max(scores, axis=-1, keepdims=True)))
        softmax_rows = exponent / lax.optimization_barrier(jnp.sum(exponent, axis=-1, keepdims=True))
        return jnp.einsum('hqk,khe->qhe', low(softmax_rows), value_rows, precision=highest)
    starts = jnp.arange(length // block_rows).astype(jnp.int32) * block_rows
    return lax.map(jax.checkpoint(one_block), starts).reshape(length, H, HD)

def forward(stream, attention_weight, feedforward_weight, vector_weight, sequence_starts):
    shape_heads = (N_FSDP, GROUP_TOK, H, HD)
    for layer_index in range(LAYERS):
        attention_low = low(attention_weight[layer_index])
        feedforward_low = low(feedforward_weight[layer_index])
        vector = vector_weight[layer_index]
        normed = low(layer_norm(stream, vector[0], vector[1]))
        project = jnp.einsum('ntd,dkf->ntkf', normed, attention_low[:, :3], precision=highest)
        queries = low_back(low(project[:, :, 0] + vector[2]))
        key_rows = low_back(low(project[:, :, 1]))
        value_rows = low_back(low(project[:, :, 2] + vector[3]))
        mixed = lax.map(attend_group, (queries.reshape(shape_heads), key_rows.reshape(shape_heads), value_rows.reshape(shape_heads), sequence_starts))
        mixed = low_back(low(mixed.reshape(N_FSDP, GROUP_TOK, D)))
        branch = low_back(jnp.einsum('ntf,ef->nte', mixed, attention_low[:, 3], precision=highest) + vector[4])
        stream = stream + branch
        normed_two = low(layer_norm(stream, vector[5], vector[6]))
        hidden = low_back(jnp.einsum('ntd,df->ntf', normed_two, feedforward_low[:, 0], precision=highest) + vector[8:].reshape(FF))
        active = low(gelu_tanh(hidden))
        branch = low_back(jnp.einsum('ntf,ef->nte', active, feedforward_low[:, 1], precision=highest) + vector[7])
        stream = stream + branch
    return stream

def adamw_step(weight, moment, second, gradient, step_rate, decay_rate):
    moment = 0.9 * moment + 0.1 * gradient
    second = 0.95 * second + 0.05 * gradient * gradient
    first_fix = 1.0 - 0.9 ** STEP
    second_fix = 1.0 - 0.95 ** STEP
    update = moment / first_fix / (jnp.sqrt(second / second_fix) + 1e-08) + decay_rate * weight
    return (moment, second, weight - step_rate * update)

def reference(block_input, cotangent, sequence_starts, attention_weight, attention_first, attention_second, feedforward_weight, feedforward_first, feedforward_second, vector_weight, vector_first, vector_second):
    stream = block_input.astype(jnp.float32).reshape(N_FSDP, GROUP_TOK, D)

    def run_layers(stream_in, attention_in, feedforward_in, vector_in):
        return forward(stream_in, attention_in, feedforward_in, vector_in, sequence_starts)
    output, pull_back = jax.vjp(run_layers, stream, attention_weight, feedforward_weight, vector_weight)
    back_input, back_attention, back_feedforward, back_vector = pull_back(cotangent.astype(jnp.float32).reshape(N_FSDP, GROUP_TOK, D))
    attention_moment, attention_square, attention_updated = adamw_step(attention_weight, attention_first, attention_second, back_attention, matrix_rate, weight_decay)
    feedforward_moment, feedforward_square, feedforward_updated = adamw_step(feedforward_weight, feedforward_first, feedforward_second, back_feedforward, matrix_rate, weight_decay)
    vector_moment, vector_square, vector_updated = adamw_step(vector_weight, vector_first, vector_second, back_vector, vector_rate, 0.0)
    return (output.reshape(TOKENS, D), back_input.reshape(TOKENS, D), attention_moment, attention_square, attention_updated, feedforward_moment, feedforward_square, feedforward_updated, vector_moment, vector_square, vector_updated)
```

```python
import jax
import jax.numpy as jnp
from jax import lax
from jax.experimental import pallas as pl
from jax.experimental.pallas import tpu as pltpu
from jax.sharding import PartitionSpec as P

H = 16
HD = 64
STEP = 10
FC = ("fsdp", "ctx")
NY = 4
NX = 4
TP = 4

norm_eps = 1e-05
gelu_factor = 0.7978845608028654
matrix_rate = 0.05
vector_rate = 0.3
weight_decay = 0.1

f32 = jnp.float32
bf16 = jnp.bfloat16
VMEM_LIMIT = 48 * 1024 * 1024


def place(y, x, core):
    return (y * 2 + (x & 1)) * 4 + (x >> 1) * 2 + core


def shift_perm(dy=0, dx=0, dc=0):
    return [
        (place(y, x, c), place((y + dy) % NY, (x + dx) % NX, (c + dc) % 2))
        for y in range(NY)
        for x in range(NX)
        for c in range(2)
    ]


def move(value, dy=0, dx=0, dc=0):
    return lax.ppermute(value, FC, shift_perm(dy, dx, dc))


def move_tp(value, k):
    return lax.ppermute(value, "tp", [(i, (i + k) % TP) for i in range(TP)])


def tp_gather(own):
    return jnp.concatenate([own] + [move_tp(own, k) for k in (1, 2, 3)], axis=0)


def tp_scatter(partial):
    rows = partial.shape[0] // TP
    total = partial[:rows].astype(f32)
    for k in (1, 2, 3):
        total = total + move_tp(partial[k * rows : (k + 1) * rows].astype(bf16), -k).astype(f32)
    return total


def turn_rows(values, t):
    rows = values.shape[0] // TP
    return jnp.concatenate(
        [lax.dynamic_slice_in_dim(values, ((t - k) & 3) * rows, rows, 0) for k in range(TP)], axis=0
    )


def tp_gather_natural(own, t):
    rows = own.shape[0]
    whole = jnp.zeros((rows * TP,) + own.shape[1:], own.dtype)
    whole = lax.dynamic_update_slice_in_dim(whole, own, t * rows, 0)
    for k in (1, 2, 3):
        whole = lax.dynamic_update_slice_in_dim(whole, move_tp(own, k), ((t - k) & 3) * rows, 0)
    return whole


def stage_gather(value, index_of, senders):
    count = len(senders) + 1
    whole = jnp.zeros((count,) + value.shape, value.dtype)
    whole = lax.dynamic_update_slice_in_dim(whole, value[None], index_of, 0)
    for received, index in senders:
        whole = lax.dynamic_update_slice_in_dim(whole, received[None], index, 0)
    return whole


def x_slot(x):
    return (x & 1) * 2 + (x >> 1)


def gather_vectors(own, y, x, core, t):
    layers, rows, width = own.shape
    value = own.reshape(1, layers * rows * width)
    value = stage_gather(value, t, [(move_tp(value, k), (t - k) & 3) for k in (1, 2, 3)])
    value = stage_gather(value, core, [(move(value, dc=1), 1 - core)])
    value = stage_gather(
        value, x_slot(x), [(move(value, dx=k), x_slot((x - k) & 3)) for k in (1, 2, 3)]
    )
    value = stage_gather(value, y, [(move(value, dy=k), (y - k) & 3) for k in (1, 2, 3)])
    value = value.reshape(-1, layers, rows, width)
    return value.transpose(1, 2, 0, 3).reshape(layers, rows, -1)


def scatter_vectors(whole, y, x, core, t):
    layers, rows, _ = whole.shape
    value = whole.reshape(layers, rows, 128, 8).transpose(2, 0, 1, 3)
    value = value.reshape(NY, NX, 2, TP, layers * rows * 8)

    def pick(array, index):
        return lax.dynamic_index_in_dim(array, index, 0, keepdims=False)

    value = pick(value, y) + sum(move(pick(value, (y + k) & 3), dy=k) for k in (1, 2, 3))
    value = pick(value, x_slot(x)) + sum(
        move(pick(value, x_slot((x + k) & 3)), dx=k) for k in (1, 2, 3)
    )
    value = pick(value, core) + move(pick(value, 1 - core), dc=1)
    value = pick(value, t) + sum(move_tp(pick(value, (t + k) & 3), k) for k in (1, 2, 3))
    return value.reshape(layers, rows, 8)


def gather_rows(own):
    count = 32
    spread = jnp.broadcast_to(own[None], (count,) + own.shape).reshape(-1, own.shape[1])
    return lax.all_to_all(spread, FC, split_axis=0, concat_axis=0, tiled=True)


def sum_rows(partial):
    pieces = lax.all_to_all(partial, FC, split_axis=0, concat_axis=0, tiled=True)
    return jnp.sum(pieces.reshape(32, -1, partial.shape[1]), axis=0, dtype=f32)


def kv_gather(own):
    across = move(own, dx=2)
    beside = move(own, dc=1)
    return [own, beside, across, move(across, dc=1)]


def kv_scatter(parts):
    own = parts[0].astype(f32) + move(parts[1], dc=1).astype(f32)
    far = (parts[2].astype(f32) + move(parts[3], dc=1).astype(f32)).astype(bf16)
    return own + move(far, dx=2).astype(f32)


def place_of(row, block, t):
    return block * 256 + (((t - (row >> 6)) & 3) << 6) + (row & 63)


def last_last(a, b):
    return lax.dot_general(a, b, (((1,), (1,)), ((), ())), preferred_element_type=f32)


def attend_kernel(meta, slopes, q_ref, kv0, kv1, kv2, kv3, out_ref):
    c, t, s1, s2 = meta[0], meta[1], meta[2], meta[3]
    blocks = (kv0, kv1, kv2, kv3)
    row_place = place_of(lax.broadcasted_iota(jnp.int32, (256, 1), 0), c, t)
    row_segment = (row_place >= s1).astype(jnp.int32) + (row_place >= s2).astype(jnp.int32)
    distances = []
    for k in range(4):
        key_place = place_of(lax.broadcasted_iota(jnp.int32, (1, 256), 1), c ^ k, t)
        key_segment = (key_place >= s1).astype(jnp.int32) + (key_place >= s2).astype(jnp.int32)
        gap = row_place - key_place
        allowed = (gap >= 0) & (row_segment == key_segment)
        distances.append(jnp.where(allowed, gap, -1).astype(f32))
    mixed = []
    for h in range(4):
        cols = slice(h * HD, (h + 1) * HD)
        value_cols = slice(256 + h * HD, 256 + (h + 1) * HD)
        query = q_ref[:, cols]
        slope = slopes[h]
        scores = [
            jnp.where(d >= 0, last_last(query, kv[:, cols]) * 0.125 - slope * d, -1e30)
            for d, kv in zip(distances, blocks)
        ]
        top = jnp.maximum(
            jnp.maximum(scores[0], scores[1]), jnp.maximum(scores[2], scores[3])
        ).max(axis=-1, keepdims=True)
        exponent = [jnp.exp(s - top) for s in scores]
        total = (exponent[0] + exponent[1] + exponent[2] + exponent[3]).sum(axis=-1, keepdims=True)
        scale = 1.0 / total
        mixed.append(
            sum(
                jnp.dot((e * scale).astype(bf16), kv[:, value_cols], preferred_element_type=f32)
                for e, kv in zip(exponent, blocks)
            )
        )
    out_ref[...] = jnp.concatenate(mixed, axis=1).astype(bf16)


def attend_back_kernel(
    meta, slopes, q_ref, do_ref, kv0, kv1, kv2, kv3, dq_ref, dkv0, dkv1, dkv2, dkv3
):
    c, t, s1, s2 = meta[0], meta[1], meta[2], meta[3]
    blocks = (kv0, kv1, kv2, kv3)
    back_blocks = (dkv0, dkv1, dkv2, dkv3)
    row_place = place_of(lax.broadcasted_iota(jnp.int32, (1, 256), 1), c, t)
    row_segment = (row_place >= s1).astype(jnp.int32) + (row_place >= s2).astype(jnp.int32)
    distances = []
    for k in range(4):
        key_place = place_of(lax.broadcasted_iota(jnp.int32, (256, 1), 0), c ^ k, t)
        key_segment = (key_place >= s1).astype(jnp.int32) + (key_place >= s2).astype(jnp.int32)
        gap = row_place - key_place
        allowed = (gap >= 0) & (row_segment == key_segment)
        distances.append(jnp.where(allowed, gap, -1).astype(f32))
    turned = [kv[:, :256].astype(f32).T.astype(bf16) for kv in blocks]
    back_query = []
    back_keys = [[] for _ in range(4)]
    back_values = [[] for _ in range(4)]
    for h in range(4):
        cols = slice(h * HD, (h + 1) * HD)
        value_cols = slice(256 + h * HD, 256 + (h + 1) * HD)
        query = q_ref[:, cols]
        back_rows = do_ref[:, cols]
        slope = slopes[h]
        scores = [
            jnp.where(d >= 0, last_last(kv[:, cols], query) * 0.125 - slope * d, -1e30)
            for d, kv in zip(distances, blocks)
        ]
        top = jnp.maximum(
            jnp.maximum(scores[0], scores[1]), jnp.maximum(scores[2], scores[3])
        ).max(axis=0, keepdims=True)
        exponent = [jnp.exp(s - top) for s in scores]
        total = (exponent[0] + exponent[1] + exponent[2] + exponent[3]).sum(axis=0, keepdims=True)
        scale = 1.0 / total
        probs = [e * scale for e in exponent]
        back_probs = [last_last(kv[:, value_cols], back_rows) for kv in blocks]
        products = [p * b for p, b in zip(probs, back_probs)]
        delta = (products[0] + products[1] + products[2] + products[3]).sum(axis=0, keepdims=True)
        turned_query = None
        for k in range(4):
            back_scores = (probs[k] * (back_probs[k] - delta)).astype(bf16)
            part = jnp.dot(turned[k][cols], back_scores, preferred_element_type=f32)
            turned_query = part if turned_query is None else turned_query + part
            back_keys[k].append(jnp.dot(back_scores, query, preferred_element_type=f32) * 0.125)
            back_values[k].append(
                jnp.dot(probs[k].astype(bf16), back_rows, preferred_element_type=f32)
            )
        back_query.append(turned_query)
    dq_ref[...] = (jnp.concatenate(back_query, axis=0) * 0.125).T.astype(bf16)
    for k in range(4):
        back_blocks[k][...] = jnp.concatenate(back_keys[k] + back_values[k], axis=1).astype(bf16)


SMEM = pl.BlockSpec(memory_space=pltpu.SMEM)
VMEM = pl.BlockSpec(memory_space=pltpu.VMEM)


def attend(meta, slopes, queries, kv_blocks):
    return pl.pallas_call(
        attend_kernel,
        out_shape=jax.ShapeDtypeStruct((256, 256), bf16),
        in_specs=[SMEM, SMEM] + [VMEM] * 5,
        out_specs=VMEM,
        compiler_params=pltpu.CompilerParams(vmem_limit_bytes=VMEM_LIMIT),
        name="attend",
    )(meta, slopes, queries, *kv_blocks)


def attend_back(meta, slopes, queries, back_mixed, kv_blocks):
    return pl.pallas_call(
        attend_back_kernel,
        out_shape=[jax.ShapeDtypeStruct((256, 256), bf16)]
        + [jax.ShapeDtypeStruct((256, 512), bf16)] * 4,
        in_specs=[SMEM, SMEM] + [VMEM] * 6,
        out_specs=[VMEM] * 5,
        compiler_params=pltpu.CompilerParams(vmem_limit_bytes=VMEM_LIMIT),
        name="attend_back",
    )(meta, slopes, queries, back_mixed, *kv_blocks)


def weight_grads(pairs):
    tokens = pairs[0][0].shape[0]
    height = pairs[0][0].shape[1]
    widths = [rhs.shape[1] for _, rhs in pairs]
    block = 256
    count = len(pairs)

    def kernel(*refs):
        out_ref = refs[-1]
        start = 0
        for i, width in enumerate(widths):
            out_ref[:, start : start + width] = lax.dot_general(
                refs[i][...],
                refs[count + i][...],
                (((0,), (0,)), ((), ())),
                preferred_element_type=f32,
            ).astype(bf16)
            start += width

    return pl.pallas_call(
        kernel,
        grid=(height // block,),
        out_shape=jax.ShapeDtypeStruct((height, sum(widths)), bf16),
        in_specs=[pl.BlockSpec((tokens, block), lambda i: (0, i))] * count
        + [pl.BlockSpec((tokens, w), lambda i: (0, 0)) for w in widths],
        out_specs=pl.BlockSpec((block, sum(widths)), lambda i: (i, 0)),
        compiler_params=pltpu.CompilerParams(vmem_limit_bytes=VMEM_LIMIT),
        name="weight_grads",
    )(*[lhs for lhs, _ in pairs], *[rhs for _, rhs in pairs])


def norm_parts(values):
    centre = values - jnp.mean(values, axis=-1, keepdims=True)
    spread = jnp.mean(centre * centre, axis=-1, keepdims=True)
    scale = lax.rsqrt(spread + norm_eps)
    return centre * scale, scale


def norm_back(back, unit, scale, gain_row):
    scaled = back * gain_row
    inner = scaled - jnp.mean(scaled, axis=-1, keepdims=True)
    inner = inner - unit * jnp.mean(scaled * unit, axis=-1, keepdims=True)
    return inner * scale, jnp.sum(back * unit, axis=0), jnp.sum(back, axis=0)


def gelu_tanh(values):
    return (
        0.5
        * values
        * (1.0 + jnp.tanh(gelu_factor * (values + 0.044715 * values * values * values)))
    )


def adamw_step(weight, moment, second, gradient, step_rate, decay_rate):
    moment = 0.9 * moment + 0.1 * gradient
    second = 0.95 * second + 0.05 * gradient * gradient
    first_fix = 1.0 - 0.9**STEP
    second_fix = 1.0 - 0.95**STEP
    update = moment / first_fix / (jnp.sqrt(second / second_fix) + 1e-08) + decay_rate * weight
    return (moment, second, weight - step_rate * update)


def matmul(a, b):
    return jnp.dot(a, b, preferred_element_type=f32)


def body(
    block_input,
    cotangent,
    sequence_starts,
    attention_weight,
    attention_first,
    attention_second,
    feedforward_weight,
    feedforward_first,
    feedforward_second,
    vector_weight,
    vector_first,
    vector_second,
):
    fsdp = lax.axis_index("fsdp")
    c = lax.axis_index("ctx")
    t = lax.axis_index("tp")
    y, x, core = fsdp >> 1, (fsdp & 1) + (c >> 1) * 2, c & 1
    rows = block_input.shape[0] // TP
    width = 256
    meta = jnp.stack([c, t, sequence_starts[0, 0], sequence_starts[0, 1]]).astype(jnp.int32)
    slopes = jnp.exp2(
        -8.0 * ((t * 4 + jnp.arange(4, dtype=jnp.int32)).astype(f32) + 1.0) / H
    )

    attention_low = attention_weight.astype(bf16)
    feedforward_low = feedforward_weight.astype(bf16)
    with jax.named_scope("gather_qkv0"):
        qkv0 = gather_rows(attention_low[0, :, :3].reshape(32, 3 * width))
    with jax.named_scope("gather_vectors"):
        vectors = gather_vectors(vector_weight, y, x, core, t)
    with jax.named_scope("gather_out0"):
        out0 = gather_rows(attention_low[0, :, 3])
    with jax.named_scope("gather_rest"):
        rest = lax.all_gather(
            jnp.stack(
                [
                    feedforward_low[0, :, 0],
                    feedforward_low[0, :, 1],
                    attention_low[1].reshape(32, 4 * width),
                    feedforward_low[1, :, 0],
                    feedforward_low[1, :, 1],
                ]
            ),
            FC,
            axis=1,
            tiled=True,
        )
    qkv_weight = (qkv0, rest[2][:, : 3 * width])
    out_weight = (out0, rest[2][:, 3 * width :])
    up_weight = (rest[0], rest[3])
    down_weight = (rest[1], rest[4])

    stream_full = turn_rows(block_input, t).astype(f32)
    stream = stream_full[:rows]
    kept = []
    for layer in range(2):
        vector = vectors[layer]
        bias_query = lax.dynamic_slice_in_dim(vector[2], t * width, width)
        bias_value = lax.dynamic_slice_in_dim(vector[3], t * width, width)
        bias_hidden = lax.dynamic_index_in_dim(vector[8:], t, 0, keepdims=False)
        with jax.named_scope(f"norm_one_{layer}"):
            if layer == 0:
                unit_full, scale_full = norm_parts(stream_full)
                unit_one, scale_one = unit_full[:rows], scale_full[:rows]
                normed = (unit_full * vector[0] + vector[1]).astype(bf16)
            else:
                unit_one, scale_one = norm_parts(stream)
                normed = tp_gather((unit_one * vector[0] + vector[1]).astype(bf16))
        with jax.named_scope(f"project_{layer}"):
            bias_kv = jnp.concatenate([jnp.zeros_like(bias_value), bias_value])
            kv_own = (matmul(normed, qkv_weight[layer][:, width:]) + bias_kv).astype(bf16)
            kv_blocks = kv_gather(kv_own)
            queries = (matmul(normed, qkv_weight[layer][:, :width]) + bias_query).astype(bf16)
        with jax.named_scope(f"attend_{layer}"):
            mixed = attend(meta, slopes, queries, kv_blocks)
        with jax.named_scope(f"out_{layer}"):
            middle = stream + tp_scatter(last_last(mixed, out_weight[layer])) + vector[4]
        with jax.named_scope(f"norm_two_{layer}"):
            unit_two, scale_two = norm_parts(middle)
            normed_two = tp_gather((unit_two * vector[5] + vector[6]).astype(bf16))
        with jax.named_scope(f"feedforward_{layer}"):
            hidden = matmul(normed_two, up_weight[layer]) + bias_hidden
            active = gelu_tanh(hidden).astype(bf16)
            stream = middle + tp_scatter(last_last(active, down_weight[layer])) + vector[7]
        kept.append(
            (
                normed,
                unit_one,
                scale_one,
                queries,
                kv_blocks,
                mixed,
                unit_two,
                scale_two,
                normed_two,
                hidden,
                active,
            )
        )
    with jax.named_scope("block_output"):
        block_output = tp_gather_natural(stream, t)

    back_branch = turn_rows(cotangent, t)
    back = back_branch[:rows].astype(f32)
    attention_grads = [None, None]
    feedforward_grads = [None, None]
    vector_grads = [None, None]
    for layer in (1, 0):
        (
            normed,
            unit_one,
            scale_one,
            queries,
            kv_blocks,
            mixed,
            unit_two,
            scale_two,
            normed_two,
            hidden,
            active,
        ) = kept[layer]
        vector = vectors[layer]
        with jax.named_scope(f"back_feedforward_{layer}"):
            if layer == 0:
                back_branch = tp_gather(back.astype(bf16))
            back_down_row = jnp.sum(back_branch[:rows].astype(f32), axis=0)
            back_active = matmul(back_branch, down_weight[layer])
            back_hidden = jax.vjp(gelu_tanh, hidden)[1](back_active)[0].astype(bf16)
            back_up_row = jnp.sum(back_hidden.astype(f32), axis=0)
            back_two = tp_scatter(last_last(back_hidden, up_weight[layer]))
        if layer == 1:
            with jax.named_scope(f"grads_feedforward_{layer}"):
                partial = weight_grads([(normed_two, back_hidden), (back_branch, active)])
                owned = lax.psum_scatter(partial, FC, scatter_dimension=0, tiled=True)
                feedforward_grads[layer] = owned.astype(f32).reshape(32, 2, 1024)
        with jax.named_scope(f"back_norm_two_{layer}"):
            step, back_gain_two, back_shift_two = norm_back(
                back_two, unit_two, scale_two, vector[5]
            )
            back_middle = back + step
            back_attn_own = back_middle.astype(bf16)
            back_attn = tp_gather(back_attn_own)
            back_out_row = jnp.sum(back_attn_own.astype(f32), axis=0)
        with jax.named_scope(f"back_attend_{layer}"):
            back_mixed = matmul(back_attn, out_weight[layer]).astype(bf16)
            back_query, *back_parts = attend_back(meta, slopes, queries, back_mixed, kv_blocks)
        if layer == 0:
            with jax.named_scope(f"grads_feedforward_{layer}"):
                owned_most = sum_rows(
                    weight_grads(
                        [(normed_two, back_hidden), (back_branch, active), (back_attn, mixed)]
                    )
                )
                feedforward_grads[layer] = owned_most[:, :2048].reshape(32, 2, 1024)
        with jax.named_scope(f"back_project_{layer}"):
            back_kv = kv_scatter(back_parts).astype(bf16)
            back_qkv = jnp.concatenate([back_query, back_kv], axis=1)
            back_one = tp_scatter(last_last(back_qkv, qkv_weight[layer]))
        with jax.named_scope(f"grads_attention_{layer}"):
            if layer == 1:
                owned = sum_rows(weight_grads([(normed, back_qkv), (back_attn, mixed)]))
            else:
                owned = jnp.concatenate(
                    [sum_rows(weight_grads([(normed, back_qkv)])), owned_most[:, 2048:]], axis=1
                )
            attention_grads[layer] = owned.reshape(32, 4, width)
        with jax.named_scope(f"back_norm_one_{layer}"):
            step, back_gain_one, back_shift_one = norm_back(
                back_one, unit_one, scale_one, vector[0]
            )
            back = back_middle + step
        with jax.named_scope(f"vector_grads_{layer}"):
            zero_row = jnp.zeros((1024,), f32)
            column_sums = jnp.sum(back_qkv.astype(f32), axis=0)
            query_row = lax.dynamic_update_slice_in_dim(
                zero_row, column_sums[:width], t * width, 0
            )
            value_row = lax.dynamic_update_slice_in_dim(
                zero_row, column_sums[2 * width :], t * width, 0
            )
            hidden_rows = lax.dynamic_update_slice_in_dim(
                jnp.zeros((4, 1024), f32), back_up_row[None], t, 0
            )
            vector_grads[layer] = jnp.concatenate(
                [
                    jnp.stack(
                        [
                            back_gain_one,
                            back_shift_one,
                            query_row,
                            value_row,
                            back_out_row,
                            back_gain_two,
                            back_shift_two,
                            back_down_row,
                        ]
                    ),
                    hidden_rows,
                ],
                axis=0,
            )
    with jax.named_scope("input_gradient"):
        input_gradient = tp_gather_natural(back, t)
    with jax.named_scope("scatter_vectors"):
        vector_total = scatter_vectors(jnp.stack(vector_grads), y, x, core, t)
    with jax.named_scope("adamw"):
        attention_out = adamw_step(
            attention_weight,
            attention_first,
            attention_second,
            jnp.stack(attention_grads),
            matrix_rate,
            weight_decay,
        )
        feedforward_out = adamw_step(
            feedforward_weight,
            feedforward_first,
            feedforward_second,
            jnp.stack(feedforward_grads),
            matrix_rate,
            weight_decay,
        )
        vector_out = adamw_step(
            vector_weight, vector_first, vector_second, vector_total, vector_rate, 0.0
        )
    return (block_output, input_gradient, *attention_out, *feedforward_out, *vector_out)


def solution(mesh):
    tokens = P(FC, None)
    weights = P(None, FC, None, "tp")
    vectors = P(None, None, ("fsdp", "ctx", "tp"))
    in_specs = (tokens, tokens, P("fsdp", None)) + (weights,) * 6 + (vectors,) * 3
    out_specs = (tokens,) * 2 + (weights,) * 6 + (vectors,) * 3
    return jax.shard_map(body, mesh=mesh, in_specs=in_specs, out_specs=out_specs, check_vma=False)
```

```python
import jax
import jax.numpy as jnp
from jax import lax
from jax.experimental import pallas as pl
from jax.experimental.pallas import tpu as pltpu
from jax.sharding import PartitionSpec as P

H = 16
HD = 64
STEP = 10
FC = ("fsdp", "ctx")
NY = 4
NX = 4
TP = 4

norm_eps = 1e-05
gelu_factor = 0.7978845608028654
matrix_rate = 0.05
vector_rate = 0.3
weight_decay = 0.1

f32 = jnp.float32
bf16 = jnp.bfloat16
VMEM_LIMIT = 48 * 1024 * 1024


def place(y, x, core):
    return (y * 2 + (x & 1)) * 4 + (x >> 1) * 2 + core


def shift_perm(dy=0, dx=0, dc=0):
    return [
        (place(y, x, c), place((y + dy) % NY, (x + dx) % NX, (c + dc) % 2))
        for y in range(NY)
        for x in range(NX)
        for c in range(2)
    ]


CHIPS = [
    [place(y, x, core) for y in range(NY) for x in (0, 2, 1, 3)] for core in range(2)
]


def move(value, dy=0, dx=0, dc=0):
    return lax.ppermute(value, FC, shift_perm(dy, dx, dc))


def move_tp(value, k):
    return lax.ppermute(value, "tp", [(i, (i + k) % TP) for i in range(TP)])


def chips_all_to_all(value):
    return lax.all_to_all(
        value, FC, split_axis=0, concat_axis=0, tiled=True, axis_index_groups=CHIPS
    )


def tp_spread(own):
    return [own] + [move_tp(own, k) for k in (1, 2, 3)]


def tp_exchange(chunks):
    return [chunks[0]] + [move_tp(chunks[k], -k) for k in (1, 2, 3)]


def turn_rows(values, t):
    rows = values.shape[0] // TP
    return [lax.dynamic_slice_in_dim(values, ((t - k) & 3) * rows, rows, 0) for k in range(TP)]


def tp_gather_natural(own, t):
    rows = own.shape[0]
    whole = jnp.zeros((rows * TP,) + own.shape[1:], own.dtype)
    whole = lax.dynamic_update_slice_in_dim(whole, own, t * rows, 0)
    for k in (1, 2, 3):
        whole = lax.dynamic_update_slice_in_dim(whole, move_tp(own, k), ((t - k) & 3) * rows, 0)
    return whole


def vector_columns(own, t):
    group = jnp.arange(32, dtype=jnp.int32)[None] >> 3
    return sum(
        jnp.where(group == ((t - k) & 3), jnp.tile(part, (1, TP)), 0.0)
        for k, part in enumerate(tp_spread(own))
    )


def scatter_vectors(whole):
    layers, rows, _ = whole.shape
    value = whole.reshape(layers * rows, 128, 8).transpose(1, 0, 2).reshape(128, -1)
    value = lax.all_to_all(
        value, ("fsdp", "ctx", "tp"), split_axis=0, concat_axis=0, tiled=True
    )
    return jnp.sum(value, axis=0).reshape(layers, rows, 8)


def kv_gather(own):
    across = move(own, dx=2)
    beside = move(own, dc=1)
    return [own, beside, across, move(across, dc=1)]


SMEM = pl.BlockSpec(memory_space=pltpu.SMEM)
VMEM = pl.BlockSpec(memory_space=pltpu.VMEM)
ANY = pl.BlockSpec(memory_space=pl.ANY)
ROWS = 64
TOK = 256
D = 1024
HW = 256


def last_last(a, b):
    return lax.dot_general(a, b, (((1,), (1,)), ((), ())), preferred_element_type=f32)


def first_first(a, b):
    return lax.dot_general(a, b, (((0,), (0,)), ((), ())), preferred_element_type=f32)


def matmul(a, b):
    return jnp.dot(a, b, preferred_element_type=f32)


def whole_of(refs):
    return jnp.concatenate([ref[...] for ref in refs], axis=0)


def run(name, kernel, outs, args, specs, out_specs=None, grid=None, scratch=(), after=()):
    count = len(args)
    extra = len(after)

    def wrapped(*refs):
        kernel(*refs[:count], *refs[count + extra :])

    if grid is None and any(spec.block_shape is not None for spec in specs):
        grid = (1,)
    grid_args = {} if grid is None else {"grid": grid}
    return pl.pallas_call(
        wrapped,
        out_shape=[jax.ShapeDtypeStruct(shape, dtype) for shape, dtype in outs],
        in_specs=list(specs) + [ANY] * extra,
        out_specs=[VMEM] * len(outs) if out_specs is None else out_specs,
        scratch_shapes=list(scratch),
        compiler_params=pltpu.CompilerParams(vmem_limit_bytes=VMEM_LIMIT),
        name=name,
        **grid_args,
    )(*args, *after)


def weight_spec(weight, width, column, stepped=False):
    array, slot, offset = weight
    if stepped:
        if slot is None:
            return pl.BlockSpec((D, width), lambda i: (0, offset // width + i))
        return pl.BlockSpec((None, D, width), lambda i: (slot, 0, offset // width + i))
    if slot is None:
        return pl.BlockSpec((D, width), lambda i: (0, column))
    return pl.BlockSpec((None, D, width), lambda i: (slot, 0, column))


CHUNKS = [((ROWS, D), f32)] + [((ROWS, D), bf16)] * 3


def store_chunks(total, refs):
    for k, ref in enumerate(refs):
        ref[...] = total[k * ROWS : (k + 1) * ROWS].astype(ref.dtype)


def norm_parts(values):
    centre = values - jnp.mean(values, axis=-1, keepdims=True)
    spread = jnp.mean(centre * centre, axis=-1, keepdims=True)
    scale = lax.rsqrt(spread + norm_eps)
    return centre * scale, scale


def unpack_kernel(core_ref, own_ref, other_ref, weight_ref, vector_ref):
    core = core_ref[0]
    for k in range(16):
        weight_ref[k, core] = own_ref[k, :, :D]
        weight_ref[k, 1 - core] = other_ref[k, :, :D]
        sums = [
            ref[k, :, D : D + 32].astype(f32) + ref[k, :, D + 32 : D + 64].astype(f32)
            for ref in (own_ref, other_ref)
        ]
        even = jnp.where(core == 0, sums[0], sums[1])
        odd = jnp.where(core == 0, sums[1], sums[0])
        vector_ref[:, k * 64 : k * 64 + 32] = even
        vector_ref[:, k * 64 + 32 : k * 64 + 64] = odd


def gather_first(own, vectors, core):
    high = vectors.astype(bf16)
    low = (vectors - high.astype(f32)).astype(bf16)
    extra = jnp.pad(jnp.concatenate([high, low], axis=1), ((0, 8), (0, 64)))
    packed = jnp.concatenate([own, extra], axis=1)
    spread = jnp.broadcast_to(packed[None], (16,) + packed.shape).reshape(-1, D + 128)
    mine = chips_all_to_all(spread)
    other = move(mine, dc=1)
    weight, vector = run(
        "unpack",
        unpack_kernel,
        [((16, 2, 32, D), bf16), ((32, D), f32)],
        [core[None], mine.reshape(16, 32, D + 128), other.reshape(16, 32, D + 128)],
        [SMEM, VMEM, VMEM],
    )
    return weight.reshape(D, D), vector


def first_kernel(x0, x1, x2, x3, vec, w_ref, bq, bv, n0, n1, n2, n3, kv_ref, q_ref):
    normed = []
    for x, n in zip((x0, x1, x2, x3), (n0, n1, n2, n3)):
        unit, _ = norm_parts(x[...].astype(f32))
        value = (unit * vec[0:1, :] + vec[1:2, :]).astype(bf16)
        n[...] = value
        normed.append(value)
    project(jnp.concatenate(normed, axis=0), w_ref, bq, bv, kv_ref, q_ref)


def project(normed, w_ref, bq, bv, kv_ref, q_ref):
    kv_ref[:, :HW] = matmul(normed, w_ref[:, HW : 2 * HW]).astype(bf16)
    kv_ref[:, HW:] = (matmul(normed, w_ref[:, 2 * HW : 3 * HW]) + bv[...]).astype(bf16)
    q_ref[...] = (matmul(normed, w_ref[:, :HW]) + bq[...]).astype(bf16)


def project_kernel(n0, n1, n2, n3, w_ref, bq, bv, kv_ref, q_ref):
    project(whole_of((n0, n1, n2, n3)), w_ref, bq, bv, kv_ref, q_ref)


def place_of(row, block, t):
    return block * 256 + (((t - (row >> 6)) & 3) << 6) + (row & 63)


def attend_kernel(meta, slopes, q_ref, kv0, kv1, kv2, kv3, w_ref, mixed_ref, *chunk_refs):
    c, t, s1, s2 = meta[0], meta[1], meta[2], meta[3]
    blocks = (kv0, kv1, kv2, kv3)
    row_place = place_of(lax.broadcasted_iota(jnp.int32, (256, 1), 0), c, t)
    row_segment = (row_place >= s1).astype(jnp.int32) + (row_place >= s2).astype(jnp.int32)
    distances = []
    for k in range(4):
        key_place = place_of(lax.broadcasted_iota(jnp.int32, (1, 256), 1), c ^ k, t)
        key_segment = (key_place >= s1).astype(jnp.int32) + (key_place >= s2).astype(jnp.int32)
        gap = row_place - key_place
        allowed = (gap >= 0) & (row_segment == key_segment)
        distances.append(jnp.where(allowed, gap, -1).astype(f32))
    mixed = []
    for h in range(4):
        cols = slice(h * HD, (h + 1) * HD)
        value_cols = slice(256 + h * HD, 256 + (h + 1) * HD)
        query = q_ref[:, cols]
        slope = slopes[h]
        scores = [
            jnp.where(d >= 0, last_last(query, kv[:, cols]) * 0.125 - slope * d, -1e30)
            for d, kv in zip(distances, blocks)
        ]
        top = jnp.maximum(
            jnp.maximum(scores[0], scores[1]), jnp.maximum(scores[2], scores[3])
        ).max(axis=-1, keepdims=True)
        exponent = [jnp.exp(s - top) for s in scores]
        total = (exponent[0] + exponent[1] + exponent[2] + exponent[3]).sum(axis=-1, keepdims=True)
        scale = 1.0 / total
        mixed.append(
            sum(
                matmul((e * scale).astype(bf16), kv[:, value_cols])
                for e, kv in zip(exponent, blocks)
            )
        )
    mixed = jnp.concatenate(mixed, axis=1).astype(bf16)
    mixed_ref[...] = mixed
    store_chunks(last_last(mixed, w_ref[...]), chunk_refs)


def attend_back_kernel(
    meta, slopes, q_ref, b0, b1, b2, b3, w_ref, kv0, kv1, kv2, kv3, dq_ref, dkv0, dkv1, dkv2, dkv3
):
    c, t, s1, s2 = meta[0], meta[1], meta[2], meta[3]
    blocks = (kv0, kv1, kv2, kv3)
    back_blocks = (dkv0, dkv1, dkv2, dkv3)
    back_mixed = matmul(whole_of((b0, b1, b2, b3)), w_ref[...]).astype(bf16)
    row_place = place_of(lax.broadcasted_iota(jnp.int32, (1, 256), 1), c, t)
    row_segment = (row_place >= s1).astype(jnp.int32) + (row_place >= s2).astype(jnp.int32)
    distances = []
    for k in range(4):
        key_place = place_of(lax.broadcasted_iota(jnp.int32, (256, 1), 0), c ^ k, t)
        key_segment = (key_place >= s1).astype(jnp.int32) + (key_place >= s2).astype(jnp.int32)
        gap = row_place - key_place
        allowed = (gap >= 0) & (row_segment == key_segment)
        distances.append(jnp.where(allowed, gap, -1).astype(f32))
    turned = [kv[:, :256].astype(f32).T.astype(bf16) for kv in blocks]
    back_query = []
    back_keys = [[] for _ in range(4)]
    back_values = [[] for _ in range(4)]
    for h in range(4):
        cols = slice(h * HD, (h + 1) * HD)
        value_cols = slice(256 + h * HD, 256 + (h + 1) * HD)
        query = q_ref[:, cols]
        back_rows = back_mixed[:, cols]
        slope = slopes[h]
        scores = [
            jnp.where(d >= 0, last_last(kv[:, cols], query) * 0.125 - slope * d, -1e30)
            for d, kv in zip(distances, blocks)
        ]
        top = jnp.maximum(
            jnp.maximum(scores[0], scores[1]), jnp.maximum(scores[2], scores[3])
        ).max(axis=0, keepdims=True)
        exponent = [jnp.exp(s - top) for s in scores]
        total = (exponent[0] + exponent[1] + exponent[2] + exponent[3]).sum(axis=0, keepdims=True)
        scale = 1.0 / total
        probs = [e * scale for e in exponent]
        back_probs = [last_last(kv[:, value_cols], back_rows) for kv in blocks]
        products = [p * b for p, b in zip(probs, back_probs)]
        delta = (products[0] + products[1] + products[2] + products[3]).sum(axis=0, keepdims=True)
        turned_query = None
        for k in range(4):
            back_scores = (probs[k] * (back_probs[k] - delta)).astype(bf16)
            part = matmul(turned[k][cols], back_scores)
            turned_query = part if turned_query is None else turned_query + part
            back_keys[k].append(matmul(back_scores, query) * 0.125)
            back_values[k].append(matmul(probs[k].astype(bf16), back_rows))
        back_query.append(turned_query)
    dq_ref[...] = (jnp.concatenate(back_query, axis=0) * 0.125).T.astype(bf16)
    for k in range(4):
        back_blocks[k][...] = jnp.concatenate(back_keys[k] + back_values[k], axis=1).astype(bf16)


def join_kernel(p0, p1, p2, p3, base, vec, out_ref, normed_ref, *, bias, gain, shift):
    value = base[...].astype(f32) + (
        (p0[...] + p1[...].astype(f32)) + (p2[...].astype(f32) + p3[...].astype(f32))
    )
    value = value + vec[bias : bias + 1, :]
    out_ref[...] = value
    if normed_ref is not None:
        unit, _ = norm_parts(value)
        normed_ref[...] = (unit * vec[gain : gain + 1, :] + vec[shift : shift + 1, :]).astype(bf16)


def join(terms, base, vec, bias, gain=None, shift=None, after=()):
    def kernel(*refs):
        join_kernel(
            *refs[:7],
            refs[7] if gain is not None else None,
            bias=bias,
            gain=gain,
            shift=shift,
        )

    outs = [((ROWS, D), f32)] + ([((ROWS, D), bf16)] if gain is not None else [])
    return run("join", kernel, outs, [*terms, base, vec], [VMEM] * 6, after=after)


def norm_back_kernel(p0, p1, p2, p3, base, before, gain, out_ref, low_ref, rows_ref):
    back = (p0[...] + p1[...].astype(f32)) + (p2[...].astype(f32) + p3[...].astype(f32))
    unit, scale = norm_parts(before[...].astype(f32))
    scaled = back * gain[...]
    inner = scaled - jnp.mean(scaled, axis=-1, keepdims=True)
    inner = inner - unit * jnp.mean(scaled * unit, axis=-1, keepdims=True)
    out = base[...].astype(f32) + inner * scale
    out_ref[...] = out
    low = out.astype(bf16)
    low_ref[...] = low
    rows_ref[0:1, :] = jnp.sum(back * unit, axis=0, keepdims=True)
    rows_ref[1:2, :] = jnp.sum(back, axis=0, keepdims=True)
    rows_ref[2:3, :] = jnp.sum(low.astype(f32), axis=0, keepdims=True)
    rows_ref[3:8, :] = jnp.zeros((5, D), f32)


def norm_back(terms, base, before, gain, after=()):
    return run(
        "norm_back",
        norm_back_kernel,
        [((ROWS, D), f32), ((ROWS, D), bf16), ((8, D), f32)],
        [*terms, base, before, gain],
        [VMEM] * 7,
        after=after,
    )


def forward_kernel(n0, n1, n2, n3, up, down, bias, hidden_ref, active_ref, c0, c1, c2, c3, total):
    step = pl.program_id(0)
    hidden = matmul(whole_of((n0, n1, n2, n3)), up[...]) + bias[...]
    hidden_ref[...] = hidden
    inner = gelu_factor * (hidden + 0.044715 * hidden * hidden * hidden)
    active = (0.5 * hidden * (1.0 + jnp.tanh(inner))).astype(bf16)
    active_ref[...] = active
    part = last_last(active, down[...])

    @pl.when(step == 0)
    def _():
        total[...] = part

    @pl.when(step > 0)
    def _():
        total[...] += part

    @pl.when(step == pl.num_programs(0) - 1)
    def _():
        store_chunks(total[...], (c0, c1, c2, c3))


def chunk_specs():
    return [pl.BlockSpec((ROWS, D), lambda i: (0, 0))] * 4


BLOCK = 256


def feedforward(chunks, up, down, bias, after=()):
    hidden_spec = pl.BlockSpec((TOK, BLOCK), lambda i: (0, i))
    hidden, active, *partial = run(
        "feedforward",
        forward_kernel,
        [((TOK, D), f32), ((TOK, D), bf16)] + CHUNKS,
        [*chunks, up[0], down[0], bias],
        chunk_specs()
        + [
            weight_spec(up, BLOCK, 0, True),
            weight_spec(down, BLOCK, 0, True),
            pl.BlockSpec((1, BLOCK), lambda i: (0, i)),
        ],
        [hidden_spec, hidden_spec] + chunk_specs(),
        grid=(D // BLOCK,),
        scratch=[pltpu.VMEM((TOK, D), f32)],
        after=after,
    )
    return hidden, active, partial


def backward_kernel(b0, b1, b2, b3, up, down, hidden_ref, back_ref, row_ref, c0, c1, c2, c3, total):
    step = pl.program_id(0)
    back_active = matmul(whole_of((b0, b1, b2, b3)), down[...])
    u = hidden_ref[...]
    square = u * u
    bent = jnp.tanh(gelu_factor * (u + 0.044715 * square * u))
    slope = 0.5 * (1.0 + bent) + 0.5 * u * (1.0 - bent * bent) * gelu_factor * (
        1.0 + 3 * 0.044715 * square
    )
    back = (back_active * slope).astype(bf16)
    back_ref[...] = back
    row_ref[...] = jnp.sum(back.astype(f32), axis=0, keepdims=True)
    part = last_last(back, up[...])

    @pl.when(step == 0)
    def _():
        total[...] = part

    @pl.when(step > 0)
    def _():
        total[...] += part

    @pl.when(step == pl.num_programs(0) - 1)
    def _():
        store_chunks(total[...], (c0, c1, c2, c3))


def feedforward_back(chunks, up, down, hidden, after=()):
    hidden_spec = pl.BlockSpec((TOK, BLOCK), lambda i: (0, i))
    row_spec = pl.BlockSpec((1, BLOCK), lambda i: (0, i))
    back, row, *partial = run(
        "feedforward_back",
        backward_kernel,
        [((TOK, D), bf16), ((1, D), f32)] + CHUNKS,
        [*chunks, up[0], down[0], hidden],
        chunk_specs()
        + [weight_spec(up, BLOCK, 0, True), weight_spec(down, BLOCK, 0, True), hidden_spec],
        [hidden_spec, row_spec] + chunk_specs(),
        grid=(D // BLOCK,),
        scratch=[pltpu.VMEM((TOK, D), f32)],
        after=after,
    )
    return back, row, partial


def project_back_kernel(dq_ref, own, beside, far, w_ref, kv_ref, row_ref, *chunk_refs):
    back_kv = (
        (own[...].astype(f32) + beside[...].astype(f32)) + far[...].astype(f32)
    ).astype(bf16)
    kv_ref[...] = back_kv
    row_ref[:, :HW] = jnp.sum(dq_ref[...].astype(f32), axis=0, keepdims=True)
    row_ref[:, HW:] = jnp.sum(back_kv.astype(f32), axis=0, keepdims=True)
    total = last_last(dq_ref[...], w_ref[:, :HW]) + last_last(back_kv, w_ref[:, HW : 3 * HW])
    store_chunks(total, chunk_refs)


def weight_grads(core, pairs, after=()):
    widths = [rhs.shape[1] for _, rhs in pairs]
    width = sum(widths)
    count = len(pairs)
    block = 256

    def kernel(*refs):
        core_ref, rest = refs[0], refs[1:]
        mine_ref, other_ref = rest[5 * count], rest[5 * count + 1]
        first = core_ref[0] == 0
        start = 0
        for i, columns in enumerate(widths):
            grads = first_first(whole_of(rest[4 * i : 4 * i + 4]), rest[4 * count + i][...])
            grads = grads.astype(bf16)
            for j in range(block // 64):
                even = grads[64 * j : 64 * j + 32]
                odd = grads[64 * j + 32 : 64 * j + 64]
                at = (slice(32 * j, 32 * j + 32), slice(start, start + columns))
                mine_ref[at] = jnp.where(first, even, odd)
                other_ref[at] = jnp.where(first, odd, even)
            start += columns

    lhs_spec = pl.BlockSpec((ROWS, block), lambda i: (0, i))
    out_spec = pl.BlockSpec((block // 2, width), lambda i: (i, 0))
    return run(
        "weight_grads",
        kernel,
        [((D // 2, width), bf16)] * 2,
        [core[None]] + [chunk for lhs, _ in pairs for chunk in lhs] + [rhs for _, rhs in pairs],
        [SMEM]
        + [lhs_spec] * (4 * count)
        + [pl.BlockSpec((TOK, w), lambda i: (0, 0)) for w in widths],
        [out_spec, out_spec],
        grid=(D // block,),
        after=after,
    )


def sum_rows(grads):
    mine, other = grads
    chip = (mine.astype(f32) + move(other, dc=1).astype(f32)).astype(bf16)
    return chips_all_to_all(chip)


def summed(pieces):
    return jnp.sum(pieces.reshape(16, 32, -1), axis=0, dtype=f32)


def adamw_step(weight, moment, second, gradient, step_rate, decay_rate):
    moment = 0.9 * moment + 0.1 * gradient
    second = 0.95 * second + 0.05 * gradient * gradient
    first_fix = 1.0 - 0.9**STEP
    second_fix = 1.0 - 0.95**STEP
    update = moment / first_fix / (jnp.sqrt(second / second_fix) + 1e-08) + decay_rate * weight
    return (moment, second, weight - step_rate * update)


def body(
    block_input,
    cotangent,
    sequence_starts,
    attention_weight,
    attention_first,
    attention_second,
    feedforward_weight,
    feedforward_first,
    feedforward_second,
    vector_weight,
    vector_first,
    vector_second,
):
    c = lax.axis_index("ctx")
    t = lax.axis_index("tp")
    core = (c & 1).astype(jnp.int32)
    meta = jnp.stack([c, t, sequence_starts[0, 0], sequence_starts[0, 1]]).astype(jnp.int32)
    slopes = jnp.exp2(-8.0 * ((t * 4 + jnp.arange(4, dtype=jnp.int32)).astype(f32) + 1.0) / H)

    with jax.named_scope("gather_first"):
        attention_low = attention_weight.astype(bf16)
        feedforward_low = feedforward_weight.astype(bf16)
        columns = vector_columns(vector_weight.reshape(24, 8), t)
        attention_zero, vectors = gather_first(
            attention_low[0].reshape(32, D), columns, core
        )
    with jax.named_scope("gather_rest"):
        rest = lax.all_gather(
            jnp.stack(
                [
                    feedforward_low[0, :, 0],
                    feedforward_low[0, :, 1],
                    attention_low[1].reshape(32, D),
                    feedforward_low[1, :, 0],
                    feedforward_low[1, :, 1],
                ]
            ),
            FC,
            axis=1,
            tiled=True,
        )
    attention_of = ((attention_zero, None, 0), (rest, 2, 0))
    up_of = ((rest, 0, 0), (rest, 3, 0))
    down_of = ((rest, 1, 0), (rest, 4, 0))

    input_chunks = turn_rows(block_input, t)
    stream = input_chunks[0]
    kept = []
    normed_own = None
    for layer in range(2):
        vector = lax.slice_in_dim(vectors, 12 * layer, 12 * layer + 12, axis=0)
        bias_query = lax.dynamic_slice(vector, (2, t * HW), (1, HW))
        bias_value = lax.dynamic_slice(vector, (3, t * HW), (1, HW))
        bias_hidden = lax.dynamic_slice(vector, (8 + t, 0), (1, D))
        weight = attention_of[layer]
        qkv_spec = weight_spec(weight, 3 * HW, 0)
        out_spec = weight_spec(weight, HW, 3)
        with jax.named_scope(f"project_{layer}"):
            if layer == 0:
                *normed, kv_own, queries = run(
                    "first",
                    first_kernel,
                    [((ROWS, D), bf16)] * 4 + [((TOK, 2 * HW), bf16), ((TOK, HW), bf16)],
                    [*input_chunks, vector, weight[0], bias_query, bias_value],
                    [VMEM] * 5 + [qkv_spec, VMEM, VMEM],
                )
            else:
                normed = tp_spread(normed_own)
                kv_own, queries = run(
                    "project",
                    project_kernel,
                    [((TOK, 2 * HW), bf16), ((TOK, HW), bf16)],
                    [*normed, weight[0], bias_query, bias_value],
                    [VMEM] * 4 + [qkv_spec, VMEM, VMEM],
                )
            kv_blocks = kv_gather(kv_own)
        with jax.named_scope(f"attend_{layer}"):
            mixed, *partial = run(
                "attend",
                attend_kernel,
                [((TOK, HW), bf16)] + CHUNKS,
                [meta, slopes, queries, *kv_blocks, weight[0]],
                [SMEM, SMEM] + [VMEM] * 5 + [out_spec],
            )
        with jax.named_scope(f"join_attend_{layer}"):
            before = stream
            middle, normed_two_own = join(tp_exchange(partial), stream, vector, 4, 5, 6)
        with jax.named_scope(f"feedforward_{layer}"):
            normed_two = tp_spread(normed_two_own)
            hidden, active, partial = feedforward(
                normed_two, up_of[layer], down_of[layer], bias_hidden
            )
        with jax.named_scope(f"join_feedforward_{layer}"):
            terms = tp_exchange(partial)
            if layer == 0:
                stream, normed_own = join(terms, middle, vectors, 7, 12, 13)
            else:
                (stream,) = join(terms, middle, vector, 7)
        kept.append(
            (before, normed, queries, kv_blocks, mixed, middle, normed_two, hidden, active)
        )
    with jax.named_scope("block_output"):
        block_output = tp_gather_natural(stream, t)

    back_chunks = turn_rows(cotangent, t)
    back = back_chunks[0]
    back_down_row = jnp.sum(back.astype(f32), axis=0, keepdims=True)
    vector_grads = [None, None]
    pieces = {}
    after = ()
    for layer in (1, 0):
        before, normed, queries, kv_blocks, mixed, middle, normed_two, hidden, active = kept[layer]
        vector = lax.slice_in_dim(vectors, 12 * layer, 12 * layer + 12, axis=0)
        weight = attention_of[layer]
        qkv_spec = weight_spec(weight, 3 * HW, 0)
        out_spec = weight_spec(weight, HW, 3)
        with jax.named_scope(f"back_feedforward_{layer}"):
            if layer == 0:
                back_chunks = tp_spread(back_own)
            back_hidden, hidden_row, partial = feedforward_back(
                back_chunks, up_of[layer], down_of[layer], hidden, after=after
            )
            terms = tp_exchange(partial)
        ff_pairs = [(normed_two, back_hidden), (back_chunks, active)]
        if layer == 1:
            with jax.named_scope("grads_feedforward_1"):
                grads = weight_grads(core, ff_pairs)
                pieces["ff1"] = sum_rows(grads)
            after = (grads[0],)
        else:
            after = ()
        with jax.named_scope(f"back_norm_two_{layer}"):
            back_middle, back_attn_own, rows_two = norm_back(
                terms, back, middle, vector[5:6], after=after
            )
            back_attn = tp_spread(back_attn_own)
        with jax.named_scope(f"back_attend_{layer}"):
            back_query, part_own, part_beside, part_across, part_corner = run(
                "attend_back",
                attend_back_kernel,
                [((TOK, HW), bf16)] + [((TOK, 2 * HW), bf16)] * 4,
                [meta, slopes, queries, *back_attn, weight[0], *kv_blocks],
                [SMEM, SMEM] + [VMEM] * 5 + [out_spec] + [VMEM] * 4,
            )
        with jax.named_scope(f"back_project_{layer}"):
            beside = move(part_beside, dc=1)
            far = part_across.astype(f32) + move(part_corner, dc=1).astype(f32)
            far = move(far.astype(bf16), dx=2)
        after = ()
        if layer == 0:
            with jax.named_scope("grads_feedforward_0"):
                grads = weight_grads(core, ff_pairs + [(back_attn, mixed)])
                pieces["ff0"] = sum_rows(grads)
            after = (grads[0],)
        with jax.named_scope(f"back_project_{layer}"):
            back_kv, qkv_row, *partial = run(
                "project_back",
                project_back_kernel,
                [((TOK, 2 * HW), bf16), ((1, 3 * HW), f32)] + CHUNKS,
                [back_query, part_own, beside, far, weight[0]],
                [VMEM] * 4 + [qkv_spec],
                after=after,
            )
            terms = tp_exchange(partial)
        with jax.named_scope(f"grads_attention_{layer}"):
            pairs = [(normed, back_query), (normed, back_kv)]
            if layer == 1:
                pairs.append((back_attn, mixed))
            grads = weight_grads(core, pairs)
            pieces[f"att{layer}"] = sum_rows(grads)
        with jax.named_scope(f"back_norm_one_{layer}"):
            back, back_own, rows_one = norm_back(
                terms, back_middle, before, vector[0:1], after=(grads[0],)
            )
        after = ()
        with jax.named_scope(f"vector_grads_{layer}"):
            zero_row = jnp.zeros((1, D), f32)
            vector_grads[layer] = jnp.concatenate(
                [
                    rows_one[0:2],
                    lax.dynamic_update_slice(zero_row, qkv_row[:, :HW], (0, t * HW)),
                    lax.dynamic_update_slice(zero_row, qkv_row[:, 2 * HW :], (0, t * HW)),
                    rows_two[2:3],
                    rows_two[0:2],
                    back_down_row,
                    lax.dynamic_update_slice(jnp.zeros((4, D), f32), hidden_row, (t, 0)),
                ],
                axis=0,
            )
            back_down_row = rows_one[2:3]
    with jax.named_scope("input_gradient"):
        input_gradient = tp_gather_natural(back, t)
    with jax.named_scope("scatter_vectors"):
        vector_total = scatter_vectors(jnp.stack(vector_grads))
    with jax.named_scope("adamw"):
        sums = {name: summed(piece) for name, piece in pieces.items()}
        attention_total = jnp.stack(
            [
                jnp.concatenate([sums["att0"], sums["ff0"][:, 2 * D :]], axis=1),
                sums["att1"],
            ]
        ).reshape(2, 32, 4, HW)
        feedforward_total = jnp.stack([sums["ff0"][:, : 2 * D], sums["ff1"]]).reshape(
            2, 32, 2, D
        )
        attention_out = adamw_step(
            attention_weight,
            attention_first,
            attention_second,
            attention_total,
            matrix_rate,
            weight_decay,
        )
        feedforward_out = adamw_step(
            feedforward_weight,
            feedforward_first,
            feedforward_second,
            feedforward_total,
            matrix_rate,
            weight_decay,
        )
        vector_out = adamw_step(
            vector_weight, vector_first, vector_second, vector_total, vector_rate, 0.0
        )
    return (block_output, input_gradient, *attention_out, *feedforward_out, *vector_out)


def solution(mesh):
    tokens = P(FC, None)
    weights = P(None, FC, None, "tp")
    vectors = P(None, None, ("fsdp", "ctx", "tp"))
    in_specs = (tokens, tokens, P("fsdp", None)) + (weights,) * 6 + (vectors,) * 3
    out_specs = (tokens,) * 2 + (weights,) * 6 + (vectors,) * 3
    return jax.shard_map(body, mesh=mesh, in_specs=in_specs, out_specs=out_specs, check_vma=False)
```

```python
import jax
import jax.numpy as jnp
from jax import lax
from jax.experimental import pallas as pl
from jax.experimental.pallas import tpu as pltpu
from jax.sharding import PartitionSpec as P

H = 16
HD = 64
STEP = 10
FC = ("fsdp", "ctx")
NY = 4
NX = 4
TP = 4

norm_eps = 1e-05
gelu_factor = 0.7978845608028654
matrix_rate = 0.05
vector_rate = 0.3
weight_decay = 0.1

f32 = jnp.float32
bf16 = jnp.bfloat16
VMEM_LIMIT = 48 * 1024 * 1024


def place(y, x, core):
    return (y * 2 + (x & 1)) * 4 + (x >> 1) * 2 + core


def shift_perm(dy=0, dx=0, dc=0):
    return [
        (place(y, x, c), place((y + dy) % NY, (x + dx) % NX, (c + dc) % 2))
        for y in range(NY)
        for x in range(NX)
        for c in range(2)
    ]


CHIPS = [
    [place(y, x, core) for y in range(NY) for x in (0, 2, 1, 3)] for core in range(2)
]


def move(value, dy=0, dx=0, dc=0):
    return lax.ppermute(value, FC, shift_perm(dy, dx, dc))


def move_tp(value, k):
    return lax.ppermute(value, "tp", [(i, (i + k) % TP) for i in range(TP)])


def chips_all_to_all(value):
    return lax.all_to_all(
        value, FC, split_axis=0, concat_axis=0, tiled=True, axis_index_groups=CHIPS
    )


def tp_spread(own):
    return [own] + [move_tp(own, k) for k in (1, 2, 3)]


def tp_exchange(chunks):
    return [chunks[0]] + [move_tp(chunks[k], -k) for k in (1, 2, 3)]


def turn_rows(values, t):
    rows = values.shape[0] // TP
    return [lax.dynamic_slice_in_dim(values, ((t - k) & 3) * rows, rows, 0) for k in range(TP)]


def tp_gather_natural(own, t):
    rows = own.shape[0]
    whole = jnp.zeros((rows * TP,) + own.shape[1:], own.dtype)
    whole = lax.dynamic_update_slice_in_dim(whole, own, t * rows, 0)
    for k in (1, 2, 3):
        whole = lax.dynamic_update_slice_in_dim(whole, move_tp(own, k), ((t - k) & 3) * rows, 0)
    return whole


def kv_gather(own):
    across = move(own, dx=2)
    beside = move(own, dc=1)
    return [own, beside, across, move(across, dc=1)]


SMEM = pl.BlockSpec(memory_space=pltpu.SMEM)
VMEM = pl.BlockSpec(memory_space=pltpu.VMEM)
ANY = pl.BlockSpec(memory_space=pl.ANY)
ROWS = 64
TOK = 256
D = 1024
HW = 256


def last_last(a, b):
    return lax.dot_general(a, b, (((1,), (1,)), ((), ())), preferred_element_type=f32)


def first_first(a, b):
    return lax.dot_general(a, b, (((0,), (0,)), ((), ())), preferred_element_type=f32)


def matmul(a, b):
    return jnp.dot(a, b, preferred_element_type=f32)


def whole_of(refs):
    return jnp.concatenate([ref[...] for ref in refs], axis=0)


def run(name, kernel, outs, args, specs, out_specs=None, grid=None, scratch=(), after=()):
    count = len(args)
    extra = len(after)

    def wrapped(*refs):
        kernel(*refs[:count], *refs[count + extra :])

    if grid is None and any(spec.block_shape is not None for spec in specs):
        grid = (1,)
    grid_args = {} if grid is None else {"grid": grid}
    return pl.pallas_call(
        wrapped,
        out_shape=[jax.ShapeDtypeStruct(shape, dtype) for shape, dtype in outs],
        in_specs=list(specs) + [ANY] * extra,
        out_specs=[VMEM] * len(outs) if out_specs is None else out_specs,
        scratch_shapes=list(scratch),
        compiler_params=pltpu.CompilerParams(vmem_limit_bytes=VMEM_LIMIT),
        name=name,
        **grid_args,
    )(*args, *after)


def weight_spec(weight, width, column, stepped=False):
    array, slot, offset = weight
    if stepped:
        if slot is None:
            return pl.BlockSpec((D, width), lambda i: (0, offset // width + i))
        return pl.BlockSpec((None, D, width), lambda i: (slot, 0, offset // width + i))
    if slot is None:
        return pl.BlockSpec((D, width), lambda i: (0, column))
    return pl.BlockSpec((None, D, width), lambda i: (slot, 0, column))


CHUNKS = [((ROWS, D), f32)] + [((ROWS, D), bf16)] * 3


def store_chunks(total, refs):
    for k, ref in enumerate(refs):
        ref[...] = total[k * ROWS : (k + 1) * ROWS].astype(ref.dtype)


def norm_parts(values):
    centre = values - jnp.mean(values, axis=-1, keepdims=True)
    spread = jnp.mean(centre * centre, axis=-1, keepdims=True)
    scale = lax.rsqrt(spread + norm_eps)
    return centre * scale, scale


def spread_first_kernel(t_ref, v0, v1, v2, v3, weight_ref, out_ref):
    group = lax.broadcasted_iota(jnp.int32, (24, 32), 1) >> 3
    columns = jnp.zeros((24, 32), f32)
    for k, part in enumerate((v0, v1, v2, v3)):
        tiled = jnp.concatenate([part[...]] * TP, axis=1)
        columns = jnp.where(group == ((t_ref[0] - k) & 3), tiled, columns)
    high = columns.astype(bf16)
    low = (columns - high.astype(f32)).astype(bf16)
    extra = jnp.concatenate(
        [
            jnp.concatenate([high.astype(f32), low.astype(f32), jnp.zeros((24, 64), f32)], axis=1),
            jnp.zeros((8, 128), f32),
        ],
        axis=0,
    ).astype(bf16)
    slots = [weight_ref[:, s, :].astype(bf16) for s in range(4)]
    for k in range(16):
        for s in range(4):
            out_ref[k, :, s * HW : (s + 1) * HW] = slots[s]
        out_ref[k, :, D:] = extra


def unpack_kernel(core_ref, own_ref, other_ref, weight_ref, vector_ref):
    core = core_ref[0]
    for k in range(16):
        weight_ref[k, core] = own_ref[k, :, :D]
        weight_ref[k, 1 - core] = other_ref[k, :, :D]
        sums = [
            ref[k, :, D : D + 32].astype(f32) + ref[k, :, D + 32 : D + 64].astype(f32)
            for ref in (own_ref, other_ref)
        ]
        even = jnp.where(core == 0, sums[0], sums[1])
        odd = jnp.where(core == 0, sums[1], sums[0])
        vector_ref[:, k * 64 : k * 64 + 32] = even
        vector_ref[:, k * 64 + 32 : k * 64 + 64] = odd


def gather_first(attention_weight, vector_parts, t, core, after):
    (spread,) = run(
        "spread_first",
        spread_first_kernel,
        [((16, 32, D + 128), bf16)],
        [t[None], *vector_parts, attention_weight],
        [SMEM] + [VMEM] * 4 + [pl.BlockSpec((None, 32, 4, HW), lambda i: (0, 0, 0, 0))],
        after=after,
    )
    mine = chips_all_to_all(spread.reshape(512, D + 128))
    other = move(mine, dc=1)
    weight, vector = run(
        "unpack",
        unpack_kernel,
        [((16, 2, 32, D), bf16), ((32, D), f32)],
        [core[None], mine.reshape(16, 32, D + 128), other.reshape(16, 32, D + 128)],
        [SMEM, VMEM, VMEM],
    )
    return weight.reshape(D, D), vector, mine


def x_slot(x):
    return (x & 1) * 2 + (x >> 1)


def cast_kernel(weight_ref, out_ref):
    for s in range(2):
        out_ref[:, s * D : (s + 1) * D] = weight_ref[:, s, :].astype(bf16)


def columns_kernel(spot, a0, a1, a2, a3, out_ref):
    for k, ref in enumerate((a0, a1, a2, a3)):
        out_ref[x_slot((spot[1] - k) & 3)] = ref[...]


def interleave_kernel(spot, *refs):
    y, core = spot[0], spot[2]
    own, other, outs = refs[:4], refs[4:8], refs[8:]
    for k in range(4):
        row = (y - k) & 3
        for ref, at in zip(outs, (0, D)):
            ref[row, 0, core] = own[k][0, :, at : at + D]
            ref[row, 0, 1 - core] = other[k][0, :, at : at + D]


def gather_second(feedforward_weight, spot):
    (own,) = run(
        "cast",
        cast_kernel,
        [((32, 2 * D), bf16)],
        [feedforward_weight],
        [pl.BlockSpec((None, 32, 2, D), lambda i: (0, 0, 0, 0))],
    )
    (columns,) = run(
        "columns",
        columns_kernel,
        [((4, 32, 2 * D), bf16)],
        [spot, own] + [move(own, dx=k) for k in (1, 2, 3)],
        [SMEM] + [VMEM] * 4,
    )
    rows = [columns] + [move(columns, dy=k) for k in (1, 2, 3)]
    others = [move(part, dc=1) for part in rows]
    part_spec = pl.BlockSpec((1, 32, 2 * D), lambda i: (i, 0, 0))
    whole_spec = pl.BlockSpec((4, 1, 2, 32, D), lambda i: (0, i, 0, 0, 0))
    up, down = run(
        "interleave",
        interleave_kernel,
        [((4, 4, 2, 32, D), bf16)] * 2,
        [spot, *rows, *others],
        [SMEM] + [part_spec] * 8,
        [whole_spec, whole_spec],
        grid=(4,),
    )
    return up.reshape(D, D), down.reshape(D, D), columns


def pack_kernel(attention_ref, feedforward_ref, out_ref):
    for s in range(4):
        out_ref[0, :, s * HW : (s + 1) * HW] = attention_ref[:, s, :].astype(bf16)
    for s in range(2):
        out_ref[1 + s] = feedforward_ref[:, s, :].astype(bf16)


def gather_layer_one(attention_weight, feedforward_weight, after):
    (packed,) = run(
        "pack",
        pack_kernel,
        [((3, 32, D), bf16)],
        [attention_weight, feedforward_weight],
        [
            pl.BlockSpec((None, 32, 4, HW), lambda i: (1, 0, 0, 0)),
            pl.BlockSpec((None, 32, 2, D), lambda i: (1, 0, 0, 0)),
        ],
        after=after,
    )
    return lax.all_gather(packed, FC, axis=1, tiled=True)


def first_kernel(x0, x1, x2, x3, vec, w_ref, bq, bv, n0, n1, n2, n3, kv_ref, q_ref):
    normed = []
    for x, n in zip((x0, x1, x2, x3), (n0, n1, n2, n3)):
        unit, _ = norm_parts(x[...].astype(f32))
        value = (unit * vec[0:1, :] + vec[1:2, :]).astype(bf16)
        n[...] = value
        normed.append(value)
    project(jnp.concatenate(normed, axis=0), w_ref, bq, bv, kv_ref, q_ref)


def project(normed, w_ref, bq, bv, kv_ref, q_ref):
    kv_ref[:, :HW] = matmul(normed, w_ref[:, HW : 2 * HW]).astype(bf16)
    kv_ref[:, HW:] = (matmul(normed, w_ref[:, 2 * HW : 3 * HW]) + bv[...]).astype(bf16)
    q_ref[...] = (matmul(normed, w_ref[:, :HW]) + bq[...]).astype(bf16)


def project_kernel(n0, n1, n2, n3, w_ref, bq, bv, kv_ref, q_ref):
    project(whole_of((n0, n1, n2, n3)), w_ref, bq, bv, kv_ref, q_ref)


def place_of(row, block, t):
    return block * 256 + (((t - (row >> 6)) & 3) << 6) + (row & 63)


def attend_kernel(meta, slopes, q_ref, kv0, kv1, kv2, kv3, w_ref, mixed_ref, *chunk_refs):
    c, t, s1, s2 = meta[0], meta[1], meta[2], meta[3]
    blocks = (kv0, kv1, kv2, kv3)
    row_place = place_of(lax.broadcasted_iota(jnp.int32, (256, 1), 0), c, t)
    row_segment = (row_place >= s1).astype(jnp.int32) + (row_place >= s2).astype(jnp.int32)
    distances = []
    for k in range(4):
        key_place = place_of(lax.broadcasted_iota(jnp.int32, (1, 256), 1), c ^ k, t)
        key_segment = (key_place >= s1).astype(jnp.int32) + (key_place >= s2).astype(jnp.int32)
        gap = row_place - key_place
        allowed = (gap >= 0) & (row_segment == key_segment)
        distances.append(jnp.where(allowed, gap, -1).astype(f32))
    mixed = []
    for h in range(4):
        cols = slice(h * HD, (h + 1) * HD)
        value_cols = slice(256 + h * HD, 256 + (h + 1) * HD)
        query = q_ref[:, cols]
        slope = slopes[h]
        scores = [
            jnp.where(d >= 0, last_last(query, kv[:, cols]) * 0.125 - slope * d, -1e30)
            for d, kv in zip(distances, blocks)
        ]
        top = jnp.maximum(
            jnp.maximum(scores[0], scores[1]), jnp.maximum(scores[2], scores[3])
        ).max(axis=-1, keepdims=True)
        exponent = [jnp.exp(s - top) for s in scores]
        total = (exponent[0] + exponent[1] + exponent[2] + exponent[3]).sum(axis=-1, keepdims=True)
        scale = 1.0 / total
        mixed.append(
            sum(
                matmul((e * scale).astype(bf16), kv[:, value_cols])
                for e, kv in zip(exponent, blocks)
            )
        )
    mixed = jnp.concatenate(mixed, axis=1).astype(bf16)
    mixed_ref[...] = mixed
    store_chunks(last_last(mixed, w_ref[...]), chunk_refs)


def attend_back_kernel(
    meta, slopes, q_ref, b0, b1, b2, b3, w_ref, kv0, kv1, kv2, kv3, dq_ref, dkv0, dkv1, dkv2, dkv3
):
    c, t, s1, s2 = meta[0], meta[1], meta[2], meta[3]
    blocks = (kv0, kv1, kv2, kv3)
    back_blocks = (dkv0, dkv1, dkv2, dkv3)
    back_mixed = matmul(whole_of((b0, b1, b2, b3)), w_ref[...]).astype(bf16)
    row_place = place_of(lax.broadcasted_iota(jnp.int32, (1, 256), 1), c, t)
    row_segment = (row_place >= s1).astype(jnp.int32) + (row_place >= s2).astype(jnp.int32)
    distances = []
    for k in range(4):
        key_place = place_of(lax.broadcasted_iota(jnp.int32, (256, 1), 0), c ^ k, t)
        key_segment = (key_place >= s1).astype(jnp.int32) + (key_place >= s2).astype(jnp.int32)
        gap = row_place - key_place
        allowed = (gap >= 0) & (row_segment == key_segment)
        distances.append(jnp.where(allowed, gap, -1).astype(f32))
    turned = [kv[:, :256].astype(f32).T.astype(bf16) for kv in blocks]
    back_query = []
    back_keys = [[] for _ in range(4)]
    back_values = [[] for _ in range(4)]
    for h in range(4):
        cols = slice(h * HD, (h + 1) * HD)
        value_cols = slice(256 + h * HD, 256 + (h + 1) * HD)
        query = q_ref[:, cols]
        back_rows = back_mixed[:, cols]
        slope = slopes[h]
        scores = [
            jnp.where(d >= 0, last_last(kv[:, cols], query) * 0.125 - slope * d, -1e30)
            for d, kv in zip(distances, blocks)
        ]
        top = jnp.maximum(
            jnp.maximum(scores[0], scores[1]), jnp.maximum(scores[2], scores[3])
        ).max(axis=0, keepdims=True)
        exponent = [jnp.exp(s - top) for s in scores]
        total = (exponent[0] + exponent[1] + exponent[2] + exponent[3]).sum(axis=0, keepdims=True)
        scale = 1.0 / total
        probs = [e * scale for e in exponent]
        back_probs = [last_last(kv[:, value_cols], back_rows) for kv in blocks]
        products = [p * b for p, b in zip(probs, back_probs)]
        delta = (products[0] + products[1] + products[2] + products[3]).sum(axis=0, keepdims=True)
        turned_query = None
        for k in range(4):
            back_scores = (probs[k] * (back_probs[k] - delta)).astype(bf16)
            part = matmul(turned[k][cols], back_scores)
            turned_query = part if turned_query is None else turned_query + part
            back_keys[k].append(matmul(back_scores, query) * 0.125)
            back_values[k].append(matmul(probs[k].astype(bf16), back_rows))
        back_query.append(turned_query)
    dq_ref[...] = (jnp.concatenate(back_query, axis=0) * 0.125).T.astype(bf16)
    for k in range(4):
        back_blocks[k][...] = jnp.concatenate(back_keys[k] + back_values[k], axis=1).astype(bf16)


def join_kernel(p0, p1, p2, p3, base, vec, out_ref, normed_ref, *, bias, gain, shift):
    value = base[...].astype(f32) + (
        (p0[...] + p1[...].astype(f32)) + (p2[...].astype(f32) + p3[...].astype(f32))
    )
    value = value + vec[bias : bias + 1, :]
    out_ref[...] = value
    if normed_ref is not None:
        unit, _ = norm_parts(value)
        normed_ref[...] = (unit * vec[gain : gain + 1, :] + vec[shift : shift + 1, :]).astype(bf16)


def join(terms, base, vec, bias, gain=None, shift=None, after=()):
    def kernel(*refs):
        join_kernel(
            *refs[:7],
            refs[7] if gain is not None else None,
            bias=bias,
            gain=gain,
            shift=shift,
        )

    outs = [((ROWS, D), f32)] + ([((ROWS, D), bf16)] if gain is not None else [])
    return run("join", kernel, outs, [*terms, base, vec], [VMEM] * 6, after=after)


def norm_back_kernel(p0, p1, p2, p3, base, before, gain, out_ref, low_ref, rows_ref):
    back = (p0[...] + p1[...].astype(f32)) + (p2[...].astype(f32) + p3[...].astype(f32))
    unit, scale = norm_parts(before[...].astype(f32))
    scaled = back * gain[...]
    inner = scaled - jnp.mean(scaled, axis=-1, keepdims=True)
    inner = inner - unit * jnp.mean(scaled * unit, axis=-1, keepdims=True)
    out = base[...].astype(f32) + inner * scale
    out_ref[...] = out
    low = out.astype(bf16)
    low_ref[...] = low
    rows_ref[0:1, :] = jnp.sum(back * unit, axis=0, keepdims=True)
    rows_ref[1:2, :] = jnp.sum(back, axis=0, keepdims=True)
    rows_ref[2:3, :] = jnp.sum(low.astype(f32), axis=0, keepdims=True)
    rows_ref[3:8, :] = jnp.zeros((5, D), f32)


def norm_back(terms, base, before, gain, after=()):
    return run(
        "norm_back",
        norm_back_kernel,
        [((ROWS, D), f32), ((ROWS, D), bf16), ((8, D), f32)],
        [*terms, base, before, gain],
        [VMEM] * 7,
        after=after,
    )


def forward_kernel(n0, n1, n2, n3, up, down, bias, hidden_ref, active_ref, c0, c1, c2, c3, total):
    step = pl.program_id(0)
    hidden = matmul(whole_of((n0, n1, n2, n3)), up[...]) + bias[...]
    hidden_ref[...] = hidden
    inner = gelu_factor * (hidden + 0.044715 * hidden * hidden * hidden)
    active = (0.5 * hidden * (1.0 + jnp.tanh(inner))).astype(bf16)
    active_ref[...] = active
    part = last_last(active, down[...])

    @pl.when(step == 0)
    def _():
        total[...] = part

    @pl.when(step > 0)
    def _():
        total[...] += part

    @pl.when(step == pl.num_programs(0) - 1)
    def _():
        store_chunks(total[...], (c0, c1, c2, c3))


def chunk_specs():
    return [pl.BlockSpec((ROWS, D), lambda i: (0, 0))] * 4


BLOCK = 256


def feedforward(chunks, up, down, bias, after=()):
    hidden_spec = pl.BlockSpec((TOK, BLOCK), lambda i: (0, i))
    hidden, active, *partial = run(
        "feedforward",
        forward_kernel,
        [((TOK, D), f32), ((TOK, D), bf16)] + CHUNKS,
        [*chunks, up[0], down[0], bias],
        chunk_specs()
        + [
            weight_spec(up, BLOCK, 0, True),
            weight_spec(down, BLOCK, 0, True),
            pl.BlockSpec((1, BLOCK), lambda i: (0, i)),
        ],
        [hidden_spec, hidden_spec] + chunk_specs(),
        grid=(D // BLOCK,),
        scratch=[pltpu.VMEM((TOK, D), f32)],
        after=after,
    )
    return hidden, active, partial


def backward_kernel(b0, b1, b2, b3, up, down, hidden_ref, back_ref, row_ref, c0, c1, c2, c3, total):
    step = pl.program_id(0)
    back_active = matmul(whole_of((b0, b1, b2, b3)), down[...])
    u = hidden_ref[...]
    square = u * u
    bent = jnp.tanh(gelu_factor * (u + 0.044715 * square * u))
    slope = 0.5 * (1.0 + bent) + 0.5 * u * (1.0 - bent * bent) * gelu_factor * (
        1.0 + 3 * 0.044715 * square
    )
    back = (back_active * slope).astype(bf16)
    back_ref[...] = back
    row_ref[...] = jnp.sum(back.astype(f32), axis=0, keepdims=True)
    part = last_last(back, up[...])

    @pl.when(step == 0)
    def _():
        total[...] = part

    @pl.when(step > 0)
    def _():
        total[...] += part

    @pl.when(step == pl.num_programs(0) - 1)
    def _():
        store_chunks(total[...], (c0, c1, c2, c3))


def feedforward_back(chunks, up, down, hidden, after=()):
    hidden_spec = pl.BlockSpec((TOK, BLOCK), lambda i: (0, i))
    row_spec = pl.BlockSpec((1, BLOCK), lambda i: (0, i))
    back, row, *partial = run(
        "feedforward_back",
        backward_kernel,
        [((TOK, D), bf16), ((1, D), f32)] + CHUNKS,
        [*chunks, up[0], down[0], hidden],
        chunk_specs()
        + [weight_spec(up, BLOCK, 0, True), weight_spec(down, BLOCK, 0, True), hidden_spec],
        [hidden_spec, row_spec] + chunk_specs(),
        grid=(D // BLOCK,),
        scratch=[pltpu.VMEM((TOK, D), f32)],
        after=after,
    )
    return back, row, partial


def project_back_kernel(dq_ref, own, beside, far, w_ref, kv_ref, row_ref, *chunk_refs):
    back_kv = (
        (own[...].astype(f32) + beside[...].astype(f32)) + far[...].astype(f32)
    ).astype(bf16)
    kv_ref[...] = back_kv
    row_ref[:, :HW] = jnp.sum(dq_ref[...].astype(f32), axis=0, keepdims=True)
    row_ref[:, HW:] = jnp.sum(back_kv.astype(f32), axis=0, keepdims=True)
    total = last_last(dq_ref[...], w_ref[:, :HW]) + last_last(back_kv, w_ref[:, HW : 3 * HW])
    store_chunks(total, chunk_refs)


def weight_grads(core, pairs, after=()):
    widths = [rhs.shape[1] for _, rhs in pairs]
    width = sum(widths)
    count = len(pairs)
    block = 256

    def kernel(*refs):
        core_ref, rest = refs[0], refs[1:]
        mine_ref, other_ref = rest[5 * count], rest[5 * count + 1]
        first = core_ref[0] == 0
        start = 0
        for i, columns in enumerate(widths):
            grads = first_first(whole_of(rest[4 * i : 4 * i + 4]), rest[4 * count + i][...])
            grads = grads.astype(bf16)
            for j in range(block // 64):
                even = grads[64 * j : 64 * j + 32]
                odd = grads[64 * j + 32 : 64 * j + 64]
                at = (slice(32 * j, 32 * j + 32), slice(start, start + columns))
                mine_ref[at] = jnp.where(first, even, odd)
                other_ref[at] = jnp.where(first, odd, even)
            start += columns

    lhs_spec = pl.BlockSpec((ROWS, block), lambda i: (0, i))
    out_spec = pl.BlockSpec((block // 2, width), lambda i: (i, 0))
    return run(
        "weight_grads",
        kernel,
        [((D // 2, width), bf16)] * 2,
        [core[None]] + [chunk for lhs, _ in pairs for chunk in lhs] + [rhs for _, rhs in pairs],
        [SMEM]
        + [lhs_spec] * (4 * count)
        + [pl.BlockSpec((TOK, w), lambda i: (0, 0)) for w in widths],
        [out_spec, out_spec],
        grid=(D // block,),
        after=after,
    )


def pair_kernel(a, b, out_ref):
    out_ref[...] = (a[...].astype(f32) + b[...].astype(f32)).astype(bf16)


def pair_sum(a, b):
    return run("pair_sum", pair_kernel, [(a.shape, bf16)], [a, b], [VMEM] * 2)[0]


def core_sum_kernel(spot, mine, other, o0, o1, o2, o3):
    for k, ref in enumerate((o0, o1, o2, o3)):
        row = (spot[0] + k) & 3
        ref[0] = (mine[row, 0].astype(f32) + other[row, 0].astype(f32)).astype(bf16)


def core_sum(grads, spot):
    mine, other = (part.reshape(4, 4, 32, -1) for part in grads)
    other = move(other, dc=1)
    width = mine.shape[-1]
    whole_spec = pl.BlockSpec((4, 1, 32, width), lambda i: (0, i, 0, 0))
    part_spec = pl.BlockSpec((1, 32, width), lambda i: (i, 0, 0))
    return run(
        "core_sum",
        core_sum_kernel,
        [((4, 32, width), bf16)] * 4,
        [spot, mine, other],
        [SMEM, whole_spec, whole_spec],
        [part_spec] * 4,
        grid=(4,),
    )


def y_sum_kernel(spot, p0, p1, p2, p3, o0, o1, o2, o3):
    for k, ref in enumerate((o0, o1, o2, o3)):
        slot = x_slot((spot[1] + k) & 3)
        ref[...] = (
            (p0[slot].astype(f32) + p1[slot].astype(f32))
            + (p2[slot].astype(f32) + p3[slot].astype(f32))
        ).astype(bf16)


def y_sum(parts, spot):
    terms = [parts[0]] + [move(parts[k], dy=k) for k in (1, 2, 3)]
    width = parts[0].shape[-1]
    return run(
        "y_sum", y_sum_kernel, [((32, width), bf16)] * 4, [spot, *terms], [SMEM] + [VMEM] * 4
    )


def x_sum(parts):
    return parts[0].astype(f32) + sum(move(parts[k], dx=k).astype(f32) for k in (1, 2, 3))


def vector_grads_kernel(spot, *refs):
    out_ref, whole = refs[-2], refs[-1]
    t = spot[3]
    whole[...] = jnp.zeros((32, D), f32)
    for layer in range(2):
        one, two, qkv, hidden, down = refs[5 * layer : 5 * layer + 5]
        at = 12 * layer
        whole[at : at + 2, :] = one[0:2, :]
        for s in range(4):
            cols = slice(s * HW, (s + 1) * HW)
            whole[at + 2 : at + 3, cols] = jnp.where(t == s, qkv[:, :HW], 0.0)
            whole[at + 3 : at + 4, cols] = jnp.where(t == s, qkv[:, 2 * HW :], 0.0)
            whole[at + 8 + s : at + 9 + s, :] = jnp.where(t == s, hidden[...], 0.0)
        whole[at + 4 : at + 5, :] = two[2:3, :]
        whole[at + 5 : at + 7, :] = two[0:2, :]
        whole[at + 7 : at + 8, :] = down[...]
    out_ref[...] = jnp.concatenate([whole[...], jnp.zeros((96, D), f32)], axis=0).T


def scatter_vectors(spot, rows):
    (value,) = run(
        "vector_grads",
        vector_grads_kernel,
        [((D, 128), f32)],
        [spot, *rows],
        [SMEM] + [VMEM] * len(rows),
        scratch=[pltpu.VMEM((32, D), f32)],
    )
    value = lax.all_to_all(
        value, ("fsdp", "ctx", "tp"), split_axis=0, concat_axis=0, tiled=True
    )
    return jnp.sum(value.reshape(128, 8, 128), axis=0)[:, :24].T.reshape(2, 12, 8)


def adamw_step(weight, moment, second, gradient, step_rate, decay_rate):
    moment = 0.9 * moment + 0.1 * gradient
    second = 0.95 * second + 0.05 * gradient * gradient
    first_fix = 1.0 - 0.9**STEP
    second_fix = 1.0 - 0.95**STEP
    update = moment / first_fix / (jnp.sqrt(second / second_fix) + 1e-08) + decay_rate * weight
    return (moment, second, weight - step_rate * update)


def body(
    block_input,
    cotangent,
    sequence_starts,
    attention_weight,
    attention_first,
    attention_second,
    feedforward_weight,
    feedforward_first,
    feedforward_second,
    vector_weight,
    vector_first,
    vector_second,
):
    c = lax.axis_index("ctx")
    t = lax.axis_index("tp")
    core = (c & 1).astype(jnp.int32)
    meta = jnp.stack([c, t, sequence_starts[0, 0], sequence_starts[0, 1]]).astype(jnp.int32)
    slopes = jnp.exp2(-8.0 * ((t * 4 + jnp.arange(4, dtype=jnp.int32)).astype(f32) + 1.0) / H)

    fsdp = lax.axis_index("fsdp")
    spot = jnp.stack([fsdp >> 1, (fsdp & 1) + (c >> 1) * 2, c & 1, t]).astype(jnp.int32)
    with jax.named_scope("gather_second"):
        up_zero, down_zero, columns_zero = gather_second(feedforward_weight, spot)
    with jax.named_scope("gather_first"):
        vector_parts = tp_spread(vector_weight.reshape(24, 8))
        attention_zero, vectors, first_rows = gather_first(
            attention_weight, vector_parts, t.astype(jnp.int32), core, (columns_zero,)
        )
    with jax.named_scope("gather_layer_one"):
        rest = gather_layer_one(attention_weight, feedforward_weight, (first_rows,))
    attention_of = ((attention_zero, None, 0), (rest, 0, 0))
    up_of = ((up_zero, None, 0), (rest, 1, 0))
    down_of = ((down_zero, None, 0), (rest, 2, 0))

    input_chunks = turn_rows(block_input, t)
    stream = input_chunks[0]
    kept = []
    normed_own = None
    for layer in range(2):
        vector = lax.slice_in_dim(vectors, 12 * layer, 12 * layer + 12, axis=0)
        bias_query = lax.dynamic_slice(vector, (2, t * HW), (1, HW))
        bias_value = lax.dynamic_slice(vector, (3, t * HW), (1, HW))
        bias_hidden = lax.dynamic_slice(vector, (8 + t, 0), (1, D))
        weight = attention_of[layer]
        qkv_spec = weight_spec(weight, 3 * HW, 0)
        out_spec = weight_spec(weight, HW, 3)
        with jax.named_scope(f"project_{layer}"):
            if layer == 0:
                *normed, kv_own, queries = run(
                    "first",
                    first_kernel,
                    [((ROWS, D), bf16)] * 4 + [((TOK, 2 * HW), bf16), ((TOK, HW), bf16)],
                    [*input_chunks, vector, weight[0], bias_query, bias_value],
                    [VMEM] * 5 + [qkv_spec, VMEM, VMEM],
                )
            else:
                normed = tp_spread(normed_own)
                kv_own, queries = run(
                    "project",
                    project_kernel,
                    [((TOK, 2 * HW), bf16), ((TOK, HW), bf16)],
                    [*normed, weight[0], bias_query, bias_value],
                    [VMEM] * 4 + [qkv_spec, VMEM, VMEM],
                )
            kv_blocks = kv_gather(kv_own)
        with jax.named_scope(f"attend_{layer}"):
            mixed, *partial = run(
                "attend",
                attend_kernel,
                [((TOK, HW), bf16)] + CHUNKS,
                [meta, slopes, queries, *kv_blocks, weight[0]],
                [SMEM, SMEM] + [VMEM] * 5 + [out_spec],
            )
        with jax.named_scope(f"join_attend_{layer}"):
            before = stream
            middle, normed_two_own = join(
                tp_exchange(partial),
                stream,
                vector,
                4,
                5,
                6,
                after=(up_zero,) if layer == 0 else (),
            )
        with jax.named_scope(f"feedforward_{layer}"):
            normed_two = tp_spread(normed_two_own)
            hidden, active, partial = feedforward(
                normed_two, up_of[layer], down_of[layer], bias_hidden
            )
        with jax.named_scope(f"join_feedforward_{layer}"):
            terms = tp_exchange(partial)
            if layer == 0:
                stream, normed_own = join(terms, middle, vectors, 7, 12, 13)
            else:
                (stream,) = join(terms, middle, vector, 7)
        kept.append(
            (before, normed, queries, kv_blocks, mixed, middle, normed_two, hidden, active)
        )
    with jax.named_scope("block_output"):
        block_output = tp_gather_natural(stream, t)

    back_chunks = turn_rows(cotangent, t)
    back = back_chunks[0]
    back_down_row = jnp.sum(back.astype(f32), axis=0, keepdims=True)
    vector_rows = [None, None]
    pieces = {}
    for layer in (1, 0):
        before, normed, queries, kv_blocks, mixed, middle, normed_two, hidden, active = kept[layer]
        vector = lax.slice_in_dim(vectors, 12 * layer, 12 * layer + 12, axis=0)
        weight = attention_of[layer]
        qkv_spec = weight_spec(weight, 3 * HW, 0)
        out_spec = weight_spec(weight, HW, 3)
        with jax.named_scope(f"back_feedforward_{layer}"):
            if layer == 0:
                back_chunks = tp_spread(back_own)
            back_hidden, hidden_row, partial = feedforward_back(
                back_chunks,
                up_of[layer],
                down_of[layer],
                hidden,
                after=(block_output, pieces["att1"][0], pieces["ff1"][0]) if layer == 0 else (),
            )
            terms = tp_exchange(partial)
        with jax.named_scope(f"grads_feedforward_{layer}"):
            grads_ff = weight_grads(core, [(normed_two, back_hidden), (back_chunks, active)])
            pieces[f"ff{layer}"] = core_sum(grads_ff, spot)
        with jax.named_scope(f"back_norm_two_{layer}"):
            back_middle, back_attn_own, rows_two = norm_back(
                terms,
                back,
                middle,
                vector[5:6],
                after=(grads_ff[0], stream) if layer == 1 else (grads_ff[0],),
            )
            back_attn = tp_spread(back_attn_own)
        with jax.named_scope(f"back_attend_{layer}"):
            back_query, part_own, part_beside, part_across, part_corner = run(
                "attend_back",
                attend_back_kernel,
                [((TOK, HW), bf16)] + [((TOK, 2 * HW), bf16)] * 4,
                [meta, slopes, queries, *back_attn, weight[0], *kv_blocks],
                [SMEM, SMEM] + [VMEM] * 5 + [out_spec] + [VMEM] * 4,
                after=(pieces["ff0"][0], pieces["att1"][0]) if layer == 0 else (pieces["ff1"][0],),
            )
        with jax.named_scope(f"sum_{layer}"):
            if layer == 0:
                pieces["att1"] = y_sum(pieces["att1"], spot)
        with jax.named_scope(f"back_project_{layer}"):
            beside = move(part_beside, dc=1)
            far = move(pair_sum(part_across, move(part_corner, dc=1)), dx=2)
            back_kv, qkv_row, *partial = run(
                "project_back",
                project_back_kernel,
                [((TOK, 2 * HW), bf16), ((1, 3 * HW), f32)] + CHUNKS,
                [back_query, part_own, beside, far, weight[0]],
                [VMEM] * 4 + [qkv_spec],
                after=(pieces["att1"][0],) if layer == 0 else (),
            )
            terms = tp_exchange(partial)
        with jax.named_scope(f"grads_attention_{layer}"):
            grads = weight_grads(
                core, [(normed, back_query), (normed, back_kv), (back_attn, mixed)]
            )
            pieces[f"att{layer}"] = core_sum(grads, spot)
            name = "ff1" if layer == 1 else "ff0"
            pieces[name] = y_sum(pieces[name], spot)
        with jax.named_scope(f"back_norm_one_{layer}"):
            back, back_own, rows_one = norm_back(
                terms,
                back_middle,
                before,
                vector[0:1],
                after=(grads[0],) if layer == 1 else (pieces["att0"][0], pieces["ff0"][0]),
            )
        vector_rows[layer] = (rows_one, rows_two, qkv_row, hidden_row, back_down_row)
        back_down_row = rows_one[2:3]
    with jax.named_scope("input_gradient"):
        input_gradient = tp_gather_natural(back, t)
    with jax.named_scope("scatter_vectors"):
        vector_total = scatter_vectors(spot, vector_rows[0] + vector_rows[1])
    with jax.named_scope("adamw"):
        pieces["att0"] = y_sum(pieces["att0"], spot)
        sums = {name: x_sum(piece) for name, piece in pieces.items()}
        attention_total = jnp.stack(
            [
                sums["att0"],
                sums["att1"],
            ]
        ).reshape(2, 32, 4, HW)
        feedforward_total = jnp.stack([sums["ff0"], sums["ff1"]]).reshape(2, 32, 2, D)
        attention_out = adamw_step(
            attention_weight,
            attention_first,
            attention_second,
            attention_total,
            matrix_rate,
            weight_decay,
        )
        feedforward_out = adamw_step(
            feedforward_weight,
            feedforward_first,
            feedforward_second,
            feedforward_total,
            matrix_rate,
            weight_decay,
        )
        vector_out = adamw_step(
            vector_weight, vector_first, vector_second, vector_total, vector_rate, 0.0
        )
    return (block_output, input_gradient, *attention_out, *feedforward_out, *vector_out)


def solution(mesh):
    tokens = P(FC, None)
    weights = P(None, FC, None, "tp")
    vectors = P(None, None, ("fsdp", "ctx", "tp"))
    in_specs = (tokens, tokens, P("fsdp", None)) + (weights,) * 6 + (vectors,) * 3
    out_specs = (tokens,) * 2 + (weights,) * 6 + (vectors,) * 3
    return jax.shard_map(body, mesh=mesh, in_specs=in_specs, out_specs=out_specs, check_vma=False)
```

```python
import jax
import jax.numpy as jnp
from jax import lax
from jax.experimental import pallas as pl
from jax.experimental.pallas import tpu as pltpu
from jax.sharding import PartitionSpec as P

H = 16
HD = 64
STEP = 10
FC = ("fsdp", "ctx")
NY = 4
NX = 4
TP = 4

norm_eps = 1e-05
gelu_factor = 0.7978845608028654
matrix_rate = 0.05
vector_rate = 0.3
weight_decay = 0.1

f32 = jnp.float32
bf16 = jnp.bfloat16
VMEM_LIMIT = 48 * 1024 * 1024


def place(y, x, core):
    return (y * 2 + (x & 1)) * 4 + (x >> 1) * 2 + core


def shift_perm(dy=0, dx=0, dc=0):
    return [
        (place(y, x, c), place((y + dy) % NY, (x + dx) % NX, (c + dc) % 2))
        for y in range(NY)
        for x in range(NX)
        for c in range(2)
    ]


CHIPS = [
    [place(y, x, core) for y in range(NY) for x in (0, 2, 1, 3)] for core in range(2)
]


ALONG_Y = [[place(y, x, core) for y in range(NY)] for x in range(NX) for core in range(2)]


def move(value, dy=0, dx=0, dc=0):
    return lax.ppermute(value, FC, shift_perm(dy, dx, dc))


def move_tp(value, k):
    return lax.ppermute(value, "tp", [(i, (i + k) % TP) for i in range(TP)])


def chips_all_to_all(value, groups=CHIPS):
    return lax.all_to_all(
        value, FC, split_axis=0, concat_axis=0, tiled=True, axis_index_groups=groups
    )


def tp_spread(own):
    return [own] + [move_tp(own, k) for k in (1, 2, 3)]


def tp_exchange(chunks):
    return [chunks[0]] + [move_tp(chunks[k], -k) for k in (1, 2, 3)]


def turn_rows(values, t):
    rows = values.shape[0] // TP
    return [lax.dynamic_slice_in_dim(values, ((t - k) & 3) * rows, rows, 0) for k in range(TP)]


def assemble_kernel(spot, p0, p1, p2, p3, out_ref):
    for k, ref in enumerate((p0, p1, p2, p3)):
        at = pl.multiple_of(((spot[3] - k) & 3) * ROWS, ROWS)
        out_ref[pl.ds(at, ROWS), :] = ref[...]


def tp_gather_natural(own, spot):
    return run(
        "assemble",
        assemble_kernel,
        [((TOK, D), f32)],
        [spot, *tp_spread(own)],
        [SMEM] + [VMEM] * 4,
    )[0]


def kv_gather(own):
    across = move(own, dx=2)
    beside = move(own, dc=1)
    return [own, beside, across, move(across, dc=1)]


SMEM = pl.BlockSpec(memory_space=pltpu.SMEM)
VMEM = pl.BlockSpec(memory_space=pltpu.VMEM)
ANY = pl.BlockSpec(memory_space=pl.ANY)
ROWS = 64
TOK = 256
D = 1024
HW = 256


def last_last(a, b):
    return lax.dot_general(a, b, (((1,), (1,)), ((), ())), preferred_element_type=f32)


def first_first(a, b):
    return lax.dot_general(a, b, (((0,), (0,)), ((), ())), preferred_element_type=f32)


def matmul(a, b):
    return jnp.dot(a, b, preferred_element_type=f32)


def whole_of(refs):
    return jnp.concatenate([ref[...] for ref in refs], axis=0)


FIRST_HBM = ("join", "norm_back")
OUT_HBM = ("weight_grads", "chip_sum")


def in_hbm(arrays):
    return [pltpu.with_memory_space_constraint(array, pltpu.HBM) for array in arrays]


def run(name, kernel, outs, args, specs, out_specs=None, grid=None, scratch=(), after=()):
    count = len(args)
    extra = len(after)

    def wrapped(*refs):
        kernel(*refs[:count], *refs[count + extra :])

    if grid is None and any(spec.block_shape is not None for spec in specs):
        grid = (1,)
    grid_args = {} if grid is None else {"grid": grid}
    return pl.pallas_call(
        wrapped,
        out_shape=[
            pltpu.HBM(shape, dtype)
            if name in OUT_HBM or (k == 0 and name in FIRST_HBM)
            else jax.ShapeDtypeStruct(shape, dtype)
            for k, (shape, dtype) in enumerate(outs)
        ],
        in_specs=list(specs) + [ANY] * extra,
        out_specs=[VMEM] * len(outs) if out_specs is None else out_specs,
        scratch_shapes=list(scratch),
        compiler_params=pltpu.CompilerParams(vmem_limit_bytes=VMEM_LIMIT),
        name=name,
        **grid_args,
    )(*args, *[in_hbm([a])[0] if a.size > 300000 else a for a in after])


def weight_spec(weight, width, column, stepped=False):
    array, slot, offset = weight
    if stepped:
        if slot is None:
            return pl.BlockSpec((D, width), lambda i: (0, offset // width + i))
        return pl.BlockSpec((None, D, width), lambda i: (slot, 0, offset // width + i))
    if slot is None:
        return pl.BlockSpec((D, width), lambda i: (0, column))
    return pl.BlockSpec((None, D, width), lambda i: (slot, 0, column))


def full_spec(array):
    return pl.BlockSpec(array.shape, lambda i: (0,) * array.ndim)


CHUNKS = [((ROWS, D), f32)] + [((ROWS, D), bf16)] * 3


def store_chunks(total, refs):
    for k, ref in enumerate(refs):
        ref[...] = total[k * ROWS : (k + 1) * ROWS].astype(ref.dtype)


def norm_parts(values):
    centre = values - jnp.mean(values, axis=-1, keepdims=True)
    spread = jnp.mean(centre * centre, axis=-1, keepdims=True)
    scale = lax.rsqrt(spread + norm_eps)
    return centre * scale, scale


def spread_first_kernel(t_ref, v0, v1, v2, v3, weight_ref, out_ref):
    group = lax.broadcasted_iota(jnp.int32, (24, 32), 1) >> 3
    columns = jnp.zeros((24, 32), f32)
    for k, part in enumerate((v0, v1, v2, v3)):
        tiled = jnp.concatenate([part[...]] * TP, axis=1)
        columns = jnp.where(group == ((t_ref[0] - k) & 3), tiled, columns)
    high = columns.astype(bf16)
    low = (columns - high.astype(f32)).astype(bf16)
    extra = jnp.concatenate(
        [
            jnp.concatenate([high.astype(f32), low.astype(f32), jnp.zeros((24, 64), f32)], axis=1),
            jnp.zeros((8, 128), f32),
        ],
        axis=0,
    ).astype(bf16)
    slots = [weight_ref[:, s, :].astype(bf16) for s in range(4)]
    for k in range(16):
        for s in range(4):
            out_ref[k, :, s * HW : (s + 1) * HW] = slots[s]
        out_ref[k, :, D:] = extra


def unpack_kernel(core_ref, own_ref, other_ref, weight_ref, vector_ref):
    core = core_ref[0]
    for k in range(16):
        weight_ref[k, core] = own_ref[k, :, :D]
        weight_ref[k, 1 - core] = other_ref[k, :, :D]
        sums = [
            ref[k, :, D : D + 32].astype(f32) + ref[k, :, D + 32 : D + 64].astype(f32)
            for ref in (own_ref, other_ref)
        ]
        even = jnp.where(core == 0, sums[0], sums[1])
        odd = jnp.where(core == 0, sums[1], sums[0])
        vector_ref[:, k * 64 : k * 64 + 32] = even
        vector_ref[:, k * 64 + 32 : k * 64 + 64] = odd


def gather_first(attention_weight, vector_parts, t, core):
    (spread,) = run(
        "spread_first",
        spread_first_kernel,
        [((16, 32, D + 128), bf16)],
        [t[None], *vector_parts, attention_weight],
        [SMEM] + [VMEM] * 4 + [pl.BlockSpec((None, 32, 4, HW), lambda i: (0, 0, 0, 0))],
    )
    mine = chips_all_to_all(spread.reshape(512, D + 128))
    other = move(mine, dc=1)
    weight, vector = run(
        "unpack",
        unpack_kernel,
        [((16, 2, 32, D), bf16), ((32, D), f32)],
        [core[None], mine.reshape(16, 32, D + 128), other.reshape(16, 32, D + 128)],
        [SMEM, VMEM, VMEM],
    )
    return weight.reshape(D, D), vector


def x_slot(x):
    return (x & 1) * 2 + (x >> 1)


def pack_kernel(attention_ref, feedforward_ref, out_ref):
    for s in range(2):
        out_ref[s] = feedforward_ref[0, :, s, :].astype(bf16)
        out_ref[3 + s] = feedforward_ref[1, :, s, :].astype(bf16)
    for s in range(4):
        out_ref[2, :, s * HW : (s + 1) * HW] = attention_ref[:, s, :].astype(bf16)


def gather_rest(attention_weight, feedforward_weight):
    (packed,) = run(
        "pack",
        pack_kernel,
        [((5, 32, D), bf16)],
        [attention_weight, feedforward_weight],
        [pl.BlockSpec((None, 32, 4, HW), lambda i: (1, 0, 0, 0)), VMEM],
    )
    return lax.all_gather(packed, FC, axis=1, tiled=True)


def first_kernel(x0, x1, x2, x3, vec, w_ref, bq, bv, n0, n1, n2, n3, kv_ref, q_ref):
    normed = []
    for x, n in zip((x0, x1, x2, x3), (n0, n1, n2, n3)):
        unit, _ = norm_parts(x[...].astype(f32))
        value = (unit * vec[0:1, :] + vec[1:2, :]).astype(bf16)
        n[...] = value
        normed.append(value)
    project(jnp.concatenate(normed, axis=0), w_ref, bq, bv, kv_ref, q_ref)


def project(normed, w_ref, bq, bv, kv_ref, q_ref):
    kv_ref[:, :HW] = matmul(normed, w_ref[:, HW : 2 * HW]).astype(bf16)
    kv_ref[:, HW:] = (matmul(normed, w_ref[:, 2 * HW : 3 * HW]) + bv[...]).astype(bf16)
    q_ref[...] = (matmul(normed, w_ref[:, :HW]) + bq[...]).astype(bf16)


def project_kernel(n0, n1, n2, n3, w_ref, bq, bv, kv_ref, q_ref):
    project(whole_of((n0, n1, n2, n3)), w_ref, bq, bv, kv_ref, q_ref)


def place_of(row, block, t):
    return block * 256 + (((t - (row >> 6)) & 3) << 6) + (row & 63)


def attend_kernel(meta, slopes, q_ref, kv0, kv1, kv2, kv3, w_ref, mixed_ref, *chunk_refs):
    c, t, s1, s2 = meta[0], meta[1], meta[2], meta[3]
    blocks = (kv0, kv1, kv2, kv3)
    row_place = place_of(lax.broadcasted_iota(jnp.int32, (256, 1), 0), c, t)
    row_segment = (row_place >= s1).astype(jnp.int32) + (row_place >= s2).astype(jnp.int32)
    distances = []
    for k in range(4):
        key_place = place_of(lax.broadcasted_iota(jnp.int32, (1, 256), 1), c ^ k, t)
        key_segment = (key_place >= s1).astype(jnp.int32) + (key_place >= s2).astype(jnp.int32)
        gap = row_place - key_place
        allowed = (gap >= 0) & (row_segment == key_segment)
        distances.append(jnp.where(allowed, gap, -1).astype(f32))
    mixed = []
    for h in range(4):
        cols = slice(h * HD, (h + 1) * HD)
        value_cols = slice(256 + h * HD, 256 + (h + 1) * HD)
        query = q_ref[:, cols]
        slope = slopes[h]
        scores = [
            jnp.where(d >= 0, last_last(query, kv[:, cols]) * 0.125 - slope * d, -1e30)
            for d, kv in zip(distances, blocks)
        ]
        top = jnp.maximum(
            jnp.maximum(scores[0], scores[1]), jnp.maximum(scores[2], scores[3])
        ).max(axis=-1, keepdims=True)
        exponent = [jnp.exp(s - top) for s in scores]
        total = (exponent[0] + exponent[1] + exponent[2] + exponent[3]).sum(axis=-1, keepdims=True)
        scale = 1.0 / total
        mixed.append(
            sum(
                matmul((e * scale).astype(bf16), kv[:, value_cols])
                for e, kv in zip(exponent, blocks)
            )
        )
    mixed = jnp.concatenate(mixed, axis=1).astype(bf16)
    mixed_ref[...] = mixed
    store_chunks(last_last(mixed, w_ref[...]), chunk_refs)


def attend_back_kernel(
    meta, slopes, q_ref, b0, b1, b2, b3, w_ref, kv0, kv1, kv2, kv3, dq_ref, dkv0, dkv1, dkv2, dkv3
):
    c, t, s1, s2 = meta[0], meta[1], meta[2], meta[3]
    blocks = (kv0, kv1, kv2, kv3)
    back_blocks = (dkv0, dkv1, dkv2, dkv3)
    back_mixed = matmul(whole_of((b0, b1, b2, b3)), w_ref[...]).astype(bf16)
    row_place = place_of(lax.broadcasted_iota(jnp.int32, (1, 256), 1), c, t)
    row_segment = (row_place >= s1).astype(jnp.int32) + (row_place >= s2).astype(jnp.int32)
    distances = []
    for k in range(4):
        key_place = place_of(lax.broadcasted_iota(jnp.int32, (256, 1), 0), c ^ k, t)
        key_segment = (key_place >= s1).astype(jnp.int32) + (key_place >= s2).astype(jnp.int32)
        gap = row_place - key_place
        allowed = (gap >= 0) & (row_segment == key_segment)
        distances.append(jnp.where(allowed, gap, -1).astype(f32))
    turned = [kv[:, :256].astype(f32).T.astype(bf16) for kv in blocks]
    back_query = []
    back_keys = [[] for _ in range(4)]
    back_values = [[] for _ in range(4)]
    for h in range(4):
        cols = slice(h * HD, (h + 1) * HD)
        value_cols = slice(256 + h * HD, 256 + (h + 1) * HD)
        query = q_ref[:, cols]
        back_rows = back_mixed[:, cols]
        slope = slopes[h]
        scores = [
            jnp.where(d >= 0, last_last(kv[:, cols], query) * 0.125 - slope * d, -1e30)
            for d, kv in zip(distances, blocks)
        ]
        top = jnp.maximum(
            jnp.maximum(scores[0], scores[1]), jnp.maximum(scores[2], scores[3])
        ).max(axis=0, keepdims=True)
        exponent = [jnp.exp(s - top) for s in scores]
        total = (exponent[0] + exponent[1] + exponent[2] + exponent[3]).sum(axis=0, keepdims=True)
        scale = 1.0 / total
        probs = [e * scale for e in exponent]
        back_probs = [last_last(kv[:, value_cols], back_rows) for kv in blocks]
        products = [p * b for p, b in zip(probs, back_probs)]
        delta = (products[0] + products[1] + products[2] + products[3]).sum(axis=0, keepdims=True)
        turned_query = None
        for k in range(4):
            back_scores = (probs[k] * (back_probs[k] - delta)).astype(bf16)
            part = matmul(turned[k][cols], back_scores)
            turned_query = part if turned_query is None else turned_query + part
            back_keys[k].append(matmul(back_scores, query) * 0.125)
            back_values[k].append(matmul(probs[k].astype(bf16), back_rows))
        back_query.append(turned_query)
    dq_ref[...] = (jnp.concatenate(back_query, axis=0) * 0.125).T.astype(bf16)
    for k in range(4):
        back_blocks[k][...] = jnp.concatenate(back_keys[k] + back_values[k], axis=1).astype(bf16)


def join_kernel(p0, p1, p2, p3, base, vec, out_ref, normed_ref, *, bias, gain, shift):
    value = base[...].astype(f32) + (
        (p0[...] + p1[...].astype(f32)) + (p2[...].astype(f32) + p3[...].astype(f32))
    )
    value = value + vec[bias : bias + 1, :]
    out_ref[...] = value
    if normed_ref is not None:
        unit, _ = norm_parts(value)
        normed_ref[...] = (unit * vec[gain : gain + 1, :] + vec[shift : shift + 1, :]).astype(bf16)


def join(terms, base, vec, bias, gain=None, shift=None, after=()):
    def kernel(*refs):
        join_kernel(
            *refs[:7],
            refs[7] if gain is not None else None,
            bias=bias,
            gain=gain,
            shift=shift,
        )

    outs = [((ROWS, D), f32)] + ([((ROWS, D), bf16)] if gain is not None else [])
    return run(
        "join",
        kernel,
        outs,
        [*terms, *in_hbm([base]), vec],
        [VMEM] * 4 + [full_spec(base), VMEM],
        after=after,
    )


def norm_back_kernel(p0, p1, p2, p3, base, before, gain, out_ref, low_ref, rows_ref):
    back = (p0[...] + p1[...].astype(f32)) + (p2[...].astype(f32) + p3[...].astype(f32))
    unit, scale = norm_parts(before[...].astype(f32))
    scaled = back * gain[...]
    inner = scaled - jnp.mean(scaled, axis=-1, keepdims=True)
    inner = inner - unit * jnp.mean(scaled * unit, axis=-1, keepdims=True)
    out = base[...].astype(f32) + inner * scale
    out_ref[...] = out
    low = out.astype(bf16)
    low_ref[...] = low
    rows_ref[0:1, :] = jnp.sum(back * unit, axis=0, keepdims=True)
    rows_ref[1:2, :] = jnp.sum(back, axis=0, keepdims=True)
    rows_ref[2:3, :] = jnp.sum(low.astype(f32), axis=0, keepdims=True)
    rows_ref[3:8, :] = jnp.zeros((5, D), f32)


def norm_back(terms, base, before, gain, after=()):
    return run(
        "norm_back",
        norm_back_kernel,
        [((ROWS, D), f32), ((ROWS, D), bf16), ((8, D), f32)],
        [*terms, *in_hbm([base, before]), gain],
        [VMEM] * 4 + [full_spec(base), full_spec(before), VMEM],
        after=after,
    )


def forward_kernel(n0, n1, n2, n3, up, down, bias, hidden_ref, active_ref, c0, c1, c2, c3, total):
    step = pl.program_id(0)
    hidden = matmul(whole_of((n0, n1, n2, n3)), up[...]) + bias[...]
    hidden_ref[...] = hidden
    inner = gelu_factor * (hidden + 0.044715 * hidden * hidden * hidden)
    active = (0.5 * hidden * (1.0 + jnp.tanh(inner))).astype(bf16)
    active_ref[...] = active
    part = last_last(active, down[...])

    @pl.when(step == 0)
    def _():
        total[...] = part

    @pl.when(step > 0)
    def _():
        total[...] += part

    @pl.when(step == pl.num_programs(0) - 1)
    def _():
        store_chunks(total[...], (c0, c1, c2, c3))


def chunk_specs():
    return [pl.BlockSpec((ROWS, D), lambda i: (0, 0))] * 4


BLOCK = 256


def feedforward(chunks, up, down, bias, after=()):
    hidden_spec = pl.BlockSpec((TOK, BLOCK), lambda i: (0, i))
    hidden, active, *partial = run(
        "feedforward",
        forward_kernel,
        [((TOK, D), f32), ((TOK, D), bf16)] + CHUNKS,
        [*chunks, up[0], down[0], bias],
        chunk_specs()
        + [
            weight_spec(up, BLOCK, 0, True),
            weight_spec(down, BLOCK, 0, True),
            pl.BlockSpec((1, BLOCK), lambda i: (0, i)),
        ],
        [hidden_spec, hidden_spec] + chunk_specs(),
        grid=(D // BLOCK,),
        scratch=[pltpu.VMEM((TOK, D), f32)],
        after=after,
    )
    return hidden, active, partial


def backward_kernel(b0, b1, b2, b3, up, down, hidden_ref, back_ref, row_ref, c0, c1, c2, c3, total):
    step = pl.program_id(0)
    back_active = matmul(whole_of((b0, b1, b2, b3)), down[...])
    u = hidden_ref[...]
    square = u * u
    bent = jnp.tanh(gelu_factor * (u + 0.044715 * square * u))
    slope = 0.5 * (1.0 + bent) + 0.5 * u * (1.0 - bent * bent) * gelu_factor * (
        1.0 + 3 * 0.044715 * square
    )
    back = (back_active * slope).astype(bf16)
    back_ref[...] = back
    row_ref[...] = jnp.sum(back.astype(f32), axis=0, keepdims=True)
    part = last_last(back, up[...])

    @pl.when(step == 0)
    def _():
        total[...] = part

    @pl.when(step > 0)
    def _():
        total[...] += part

    @pl.when(step == pl.num_programs(0) - 1)
    def _():
        store_chunks(total[...], (c0, c1, c2, c3))


def feedforward_back(chunks, up, down, hidden, after=()):
    hidden_spec = pl.BlockSpec((TOK, BLOCK), lambda i: (0, i))
    row_spec = pl.BlockSpec((1, BLOCK), lambda i: (0, i))
    back, row, *partial = run(
        "feedforward_back",
        backward_kernel,
        [((TOK, D), bf16), ((1, D), f32)] + CHUNKS,
        [*chunks, up[0], down[0], hidden],
        chunk_specs()
        + [weight_spec(up, BLOCK, 0, True), weight_spec(down, BLOCK, 0, True), hidden_spec],
        [hidden_spec, row_spec] + chunk_specs(),
        grid=(D // BLOCK,),
        scratch=[pltpu.VMEM((TOK, D), f32)],
        after=after,
    )
    return back, row, partial


def project_back_kernel(dq_ref, own, beside, far, w_ref, kv_ref, row_ref, *chunk_refs):
    back_kv = (
        (own[...].astype(f32) + beside[...].astype(f32)) + far[...].astype(f32)
    ).astype(bf16)
    kv_ref[...] = back_kv
    row_ref[:, :HW] = jnp.sum(dq_ref[...].astype(f32), axis=0, keepdims=True)
    row_ref[:, HW:] = jnp.sum(back_kv.astype(f32), axis=0, keepdims=True)
    total = last_last(dq_ref[...], w_ref[:, :HW]) + last_last(back_kv, w_ref[:, HW : 3 * HW])
    store_chunks(total, chunk_refs)


def whole_weight_grads(pairs, after=()):
    widths = [rhs.shape[1] for _, rhs in pairs]
    width = sum(widths)
    count = len(pairs)
    block = 256

    def kernel(*refs):
        out_ref = refs[5 * count]
        start = 0
        for i, columns in enumerate(widths):
            grads = first_first(whole_of(refs[4 * i : 4 * i + 4]), refs[4 * count + i][...])
            out_ref[:, start : start + columns] = grads.astype(bf16)
            start += columns

    (out,) = run(
        "weight_grads",
        kernel,
        [((D, width), bf16)],
        [chunk for lhs, _ in pairs for chunk in lhs] + [rhs for _, rhs in pairs],
        [pl.BlockSpec((ROWS, block), lambda i: (0, i))] * (4 * count)
        + [pl.BlockSpec((TOK, w), lambda i: (0, 0)) for w in widths],
        [pl.BlockSpec((block, width), lambda i: (i, 0))],
        grid=(D // block,),
        after=after,
    )
    return out


def weight_grads(core, pairs, after=()):
    widths = [rhs.shape[1] for _, rhs in pairs]
    width = sum(widths)
    count = len(pairs)
    block = 256

    def kernel(*refs):
        core_ref, rest = refs[0], refs[1:]
        mine_ref, other_ref = rest[5 * count], rest[5 * count + 1]
        first = core_ref[0] == 0
        start = 0
        for i, columns in enumerate(widths):
            grads = first_first(whole_of(rest[4 * i : 4 * i + 4]), rest[4 * count + i][...])
            grads = grads.astype(bf16)
            for j in range(block // 64):
                even = grads[64 * j : 64 * j + 32]
                odd = grads[64 * j + 32 : 64 * j + 64]
                at = (slice(32 * j, 32 * j + 32), slice(start, start + columns))
                mine_ref[at] = jnp.where(first, even, odd)
                other_ref[at] = jnp.where(first, odd, even)
            start += columns

    lhs_spec = pl.BlockSpec((ROWS, block), lambda i: (0, i))
    out_spec = pl.BlockSpec((block // 2, width), lambda i: (i, 0))
    return run(
        "weight_grads",
        kernel,
        [((D // 2, width), bf16)] * 2,
        [core[None]] + [chunk for lhs, _ in pairs for chunk in lhs] + [rhs for _, rhs in pairs],
        [SMEM]
        + [lhs_spec] * (4 * count)
        + [pl.BlockSpec((TOK, w), lambda i: (0, 0)) for w in widths],
        [out_spec, out_spec],
        grid=(D // block,),
        after=after,
    )


def summed(pieces):
    return jnp.sum(pieces.reshape(16, 32, -1), axis=0, dtype=f32)


def pair_kernel(a, b, out_ref):
    out_ref[...] = (a[...].astype(f32) + b[...].astype(f32)).astype(bf16)


def pair_sum(a, b, steps=None, after=()):
    spec, out_specs, grid = VMEM, None, None
    if steps is not None:
        spec = pl.BlockSpec((a.shape[0] // steps, a.shape[1]), lambda i: (i, 0))
        out_specs, grid = [spec], (steps,)
    (out,) = run(
        "pair_sum" if steps is None else "chip_sum", pair_kernel, [(a.shape, bf16)], [a, b], [spec] * 2, out_specs, grid, after=after
    )
    return out


def chip_sum(grads, after=()):
    mine, other = grads
    return pair_sum(mine, move(other, dc=1), steps=4, after=after)


def hold_kernel(*refs):
    count = len(refs) // 2
    for k in range(count):
        refs[count + k][...] = refs[k][...]


def hold(arrays, after):
    return run(
        "hold",
        hold_kernel,
        [(a.shape, a.dtype) for a in arrays],
        arrays,
        [VMEM] * len(arrays),
        after=after,
    )


def feedforward_adamw_kernel(one_ref, zero_ref, weight, moment, second, m_ref, s_ref, w_ref):
    for layer, total in enumerate((zero_ref[...], one_ref[...].astype(f32))):
        for s in range(2):
            at = (layer, slice(None), s, slice(None))
            m_ref[at], s_ref[at], w_ref[at] = adamw_step(
                weight[at],
                moment[at],
                second[at],
                total[:, s * D : (s + 1) * D],
                matrix_rate,
                weight_decay,
            )


def feedforward_adamw(pieces_one, pieces_zero, weight, moment, second):
    shape = weight.shape
    return run(
        "feedforward_adamw",
        feedforward_adamw_kernel,
        [(shape, f32)] * 3,
        [pieces_one, pieces_zero, weight, moment, second],
        [VMEM] * 5,
    )


def core_sum_kernel(spot, mine, other, o0, o1, o2, o3):
    for k, ref in enumerate((o0, o1, o2, o3)):
        row = (spot[0] + k) & 3
        ref[0] = (mine[row, 0].astype(f32) + other[row, 0].astype(f32)).astype(bf16)


def core_sum(grads, spot, after=()):
    mine, other = (part.reshape(4, 4, 32, -1) for part in grads)
    other = move(other, dc=1)
    width = mine.shape[-1]
    whole_spec = pl.BlockSpec((4, 1, 32, width), lambda i: (0, i, 0, 0))
    part_spec = pl.BlockSpec((1, 32, width), lambda i: (i, 0, 0))
    return run(
        "core_sum",
        core_sum_kernel,
        [((4, 32, width), bf16)] * 4,
        [spot, mine, other],
        [SMEM, whole_spec, whole_spec],
        [part_spec] * 4,
        grid=(4,),
        after=after,
    )


def y_sum_kernel(spot, p0, p1, p2, p3, o0, o1, o2, o3):
    for k, ref in enumerate((o0, o1, o2, o3)):
        slot = x_slot((spot[1] + k) & 3)
        ref[...] = (
            (p0[slot].astype(f32) + p1[slot].astype(f32))
            + (p2[slot].astype(f32) + p3[slot].astype(f32))
        ).astype(bf16)


def y_sum_received(pieces, spot):
    width = pieces.shape[1]
    pieces = pieces.reshape(16, 32, width)
    return run(
        "y_sum",
        y_sum_kernel,
        [((32, width), bf16)] * 4,
        [spot] + [pieces] * 4,
        [SMEM] + [pl.BlockSpec((4, 32, width), lambda i, k=k: (k, 0, 0)) for k in range(4)],
    )


def y_sum(parts, spot):
    terms = [parts[0]] + [move(parts[k], dy=k) for k in (1, 2, 3)]
    width = parts[0].shape[-1]
    return run(
        "y_sum", y_sum_kernel, [((32, width), bf16)] * 4, [spot, *terms], [SMEM] + [VMEM] * 4
    )


def x_sum(parts):
    return parts[0].astype(f32) + sum(move(parts[k], dx=k).astype(f32) for k in (1, 2, 3))


def vector_grads_kernel(spot, *refs):
    out_ref, whole = refs[-2], refs[-1]
    t = spot[3]
    whole[...] = jnp.zeros((32, D), f32)
    for layer in range(2):
        one, two, qkv, hidden, down = refs[5 * layer : 5 * layer + 5]
        at = 12 * layer
        whole[at : at + 2, :] = one[0:2, :]
        for s in range(4):
            cols = slice(s * HW, (s + 1) * HW)
            whole[at + 2 : at + 3, cols] = jnp.where(t == s, qkv[:, :HW], 0.0)
            whole[at + 3 : at + 4, cols] = jnp.where(t == s, qkv[:, 2 * HW :], 0.0)
            whole[at + 8 + s : at + 9 + s, :] = jnp.where(t == s, hidden[...], 0.0)
        whole[at + 4 : at + 5, :] = two[2:3, :]
        whole[at + 5 : at + 7, :] = two[0:2, :]
        whole[at + 7 : at + 8, :] = down[...]
    out_ref[...] = jnp.concatenate([whole[...], jnp.zeros((96, D), f32)], axis=0).T


def scatter_vectors(spot, rows):
    (value,) = run(
        "vector_grads",
        vector_grads_kernel,
        [((D, 128), f32)],
        [spot, *rows],
        [SMEM] + [VMEM] * len(rows),
        scratch=[pltpu.VMEM((32, D), f32)],
    )
    value = lax.all_to_all(
        value, ("fsdp", "ctx", "tp"), split_axis=0, concat_axis=0, tiled=True
    )
    return jnp.sum(value.reshape(128, 8, 128), axis=0)[:, :24].T.reshape(2, 12, 8)


def adamw_step(weight, moment, second, gradient, step_rate, decay_rate):
    moment = 0.9 * moment + 0.1 * gradient
    second = 0.95 * second + 0.05 * gradient * gradient
    first_fix = 1.0 - 0.9**STEP
    second_fix = 1.0 - 0.95**STEP
    update = moment / first_fix / (jnp.sqrt(second / second_fix) + 1e-08) + decay_rate * weight
    return (moment, second, weight - step_rate * update)


def body(
    block_input,
    cotangent,
    sequence_starts,
    attention_weight,
    attention_first,
    attention_second,
    feedforward_weight,
    feedforward_first,
    feedforward_second,
    vector_weight,
    vector_first,
    vector_second,
):
    c = lax.axis_index("ctx")
    t = lax.axis_index("tp")
    core = (c & 1).astype(jnp.int32)
    meta = jnp.stack([c, t, sequence_starts[0, 0], sequence_starts[0, 1]]).astype(jnp.int32)
    slopes = jnp.exp2(-8.0 * ((t * 4 + jnp.arange(4, dtype=jnp.int32)).astype(f32) + 1.0) / H)

    fsdp = lax.axis_index("fsdp")
    spot = jnp.stack([fsdp >> 1, (fsdp & 1) + (c >> 1) * 2, c & 1, t]).astype(jnp.int32)
    with jax.named_scope("gather_rest"):
        rest = gather_rest(attention_weight, feedforward_weight)
    with jax.named_scope("gather_first"):
        vector_parts = tp_spread(vector_weight.reshape(24, 8))
        attention_zero, vectors = gather_first(
            attention_weight, vector_parts, t.astype(jnp.int32), core
        )
    attention_of = ((attention_zero, None, 0), (rest, 2, 0))
    up_of = ((rest, 0, 0), (rest, 3, 0))
    down_of = ((rest, 1, 0), (rest, 4, 0))

    input_chunks = turn_rows(block_input, t)
    stream = input_chunks[0]
    kept = []
    normed_own = None
    for layer in range(2):
        vector = lax.slice_in_dim(vectors, 12 * layer, 12 * layer + 12, axis=0)
        bias_query = lax.dynamic_slice(vector, (2, t * HW), (1, HW))
        bias_value = lax.dynamic_slice(vector, (3, t * HW), (1, HW))
        bias_hidden = lax.dynamic_slice(vector, (8 + t, 0), (1, D))
        weight = attention_of[layer]
        qkv_spec = weight_spec(weight, 3 * HW, 0)
        out_spec = weight_spec(weight, HW, 3)
        with jax.named_scope(f"project_{layer}"):
            if layer == 0:
                *normed, kv_own, queries = run(
                    "first",
                    first_kernel,
                    [((ROWS, D), bf16)] * 4 + [((TOK, 2 * HW), bf16), ((TOK, HW), bf16)],
                    [*input_chunks, vector, weight[0], bias_query, bias_value],
                    [VMEM] * 5 + [qkv_spec, VMEM, VMEM],
                )
            else:
                normed = tp_spread(normed_own)
                kv_own, queries = run(
                    "project",
                    project_kernel,
                    [((TOK, 2 * HW), bf16), ((TOK, HW), bf16)],
                    [*normed, weight[0], bias_query, bias_value],
                    [VMEM] * 4 + [qkv_spec, VMEM, VMEM],
                )
            kv_blocks = kv_gather(kv_own)
        with jax.named_scope(f"attend_{layer}"):
            mixed, *partial = run(
                "attend",
                attend_kernel,
                [((TOK, HW), bf16)] + CHUNKS,
                [meta, slopes, queries, *kv_blocks, weight[0]],
                [SMEM, SMEM] + [VMEM] * 5 + [out_spec],
            )
        with jax.named_scope(f"join_attend_{layer}"):
            before = stream
            middle, normed_two_own = join(
                tp_exchange(partial),
                stream,
                vector,
                4,
                5,
                6,
            )
        with jax.named_scope(f"feedforward_{layer}"):
            normed_two = tp_spread(normed_two_own)
            hidden, active, partial = feedforward(
                normed_two, up_of[layer], down_of[layer], bias_hidden
            )
        with jax.named_scope(f"join_feedforward_{layer}"):
            if layer == 0:
                stream, normed_own = join(tp_exchange(partial), middle, vectors, 7, 12, 13)
            else:
                last_partial, last_vector, last_middle = partial, vector, middle
        kept.append(
            (before, normed, queries, kv_blocks, mixed, middle, normed_two, hidden, active)
        )
    back_chunks = turn_rows(cotangent, t)
    back = back_chunks[0]
    back_down_row = jnp.sum(back.astype(f32), axis=0, keepdims=True)
    vector_rows = [None, None]
    pieces = {}
    for layer in (1, 0):
        before, normed, queries, kv_blocks, mixed, middle, normed_two, hidden, active = kept[layer]
        vector = lax.slice_in_dim(vectors, 12 * layer, 12 * layer + 12, axis=0)
        weight = attention_of[layer]
        qkv_spec = weight_spec(weight, 3 * HW, 0)
        out_spec = weight_spec(weight, HW, 3)
        with jax.named_scope(f"back_feedforward_{layer}"):
            if layer == 0:
                back_chunks = tp_spread(back_own)
            back_hidden, hidden_row, partial = feedforward_back(
                back_chunks,
                up_of[layer],
                down_of[layer],
                hidden,
                after=(pieces["att1"],) if layer == 0 else (),
            )
            terms = tp_exchange(partial)
        with jax.named_scope(f"grads_feedforward_{layer}"):
            pairs = [(in_hbm(normed_two), back_hidden), (back_chunks, *in_hbm([active]))]
            if layer == 1:
                grads_ff = whole_weight_grads(pairs)
                pieces["ff1"] = lax.psum_scatter(grads_ff, FC, scatter_dimension=0, tiled=True)
                tied = (grads_ff,)
            else:
                grads_ff = weight_grads(core, pairs)
                pieces["att1"] = chips_all_to_all(pieces["att1"])
                chip_ff = chip_sum(grads_ff, after=(pieces["att1"],))
                column_ff = chips_all_to_all(chip_ff, ALONG_Y)
                tied = (grads_ff[0],)
        with jax.named_scope(f"back_norm_two_{layer}"):
            back_middle, back_attn_own, rows_two = norm_back(
                terms,
                back,
                middle,
                vector[5:6],
                after=tied,
            )
            back_attn = tp_spread(back_attn_own)
        with jax.named_scope(f"back_attend_{layer}"):
            back_query, part_own, part_beside, part_across, part_corner = run(
                "attend_back",
                attend_back_kernel,
                [((TOK, HW), bf16)] + [((TOK, 2 * HW), bf16)] * 4,
                [meta, slopes, queries, *back_attn, weight[0], *kv_blocks],
                [SMEM, SMEM, full_spec(queries)]
                + [VMEM] * 4
                + [out_spec]
                + [full_spec(kv) for kv in kv_blocks],
                after=(chip_ff,) if layer == 0 else (),
            )
        with jax.named_scope(f"back_project_{layer}"):
            beside = move(part_beside, dc=1)
            far = move(pair_sum(part_across, move(part_corner, dc=1)), dx=2)
            if layer == 1:
                held = hold(last_partial[1:], after=(part_own,))
                (stream,) = join(
                    tp_exchange([last_partial[0], *held]), last_middle, last_vector, 7
                )
            else:
                block_output = tp_gather_natural(hold([stream], after=(part_own,))[0], spot)
            back_kv, qkv_row, *partial = run(
                "project_back",
                project_back_kernel,
                [((TOK, 2 * HW), bf16), ((1, 3 * HW), f32)] + CHUNKS,
                [back_query, part_own, beside, far, weight[0]],
                [VMEM] * 4 + [qkv_spec],
                after=(stream,) if layer == 1 else (block_output,),
            )
            terms = tp_exchange(partial)
        with jax.named_scope(f"grads_attention_{layer}"):
            normed = in_hbm(normed)
            grads = weight_grads(
                core,
                [(normed, back_query), (normed, back_kv), (back_attn, *in_hbm([mixed]))],
            )
            if layer == 1:
                pieces["att1"] = chip_sum(grads)
            else:
                pieces["ff0"] = y_sum_received(column_ff, spot)
        with jax.named_scope(f"back_norm_one_{layer}"):
            back, back_own, rows_one = norm_back(
                terms,
                back_middle,
                before,
                vector[0:1],
                after=(grads[0],) if layer == 1 else (grads[0], pieces["ff0"][0]),
            )
        vector_rows[layer] = (rows_one, rows_two, qkv_row, hidden_row, back_down_row)
        back_down_row = rows_one[2:3]
    with jax.named_scope("grads_attention_0"):
        pieces["att0"] = core_sum(grads, spot, after=(back_own,))
    with jax.named_scope("input_gradient"):
        input_gradient = tp_gather_natural(back, spot)
    with jax.named_scope("scatter_vectors"):
        vector_total = scatter_vectors(
            spot, vector_rows[0] + vector_rows[1]
        )
    with jax.named_scope("adamw"):
        attention_total = jnp.stack(
            [x_sum(y_sum(pieces["att0"], spot)), summed(pieces["att1"])]
        ).reshape(2, 32, 4, HW)
        attention_out = adamw_step(
            attention_weight,
            attention_first,
            attention_second,
            attention_total,
            matrix_rate,
            weight_decay,
        )
        feedforward_out = feedforward_adamw(
            pieces["ff1"],
            x_sum(pieces["ff0"]),
            feedforward_weight,
            feedforward_first,
            feedforward_second,
        )
        vector_out = adamw_step(
            vector_weight, vector_first, vector_second, vector_total, vector_rate, 0.0
        )
    return (block_output, input_gradient, *attention_out, *feedforward_out, *vector_out)


def solution(mesh):
    tokens = P(FC, None)
    weights = P(None, FC, None, "tp")
    vectors = P(None, None, ("fsdp", "ctx", "tp"))
    in_specs = (tokens, tokens, P("fsdp", None)) + (weights,) * 6 + (vectors,) * 3
    out_specs = (tokens,) * 2 + (weights,) * 6 + (vectors,) * 3
    return jax.shard_map(body, mesh=mesh, in_specs=in_specs, out_specs=out_specs, check_vma=False)
```

```python
import jax
import jax.numpy as jnp
from jax import lax
from jax.experimental import pallas as pl
from jax.experimental.pallas import tpu as pltpu
from jax.sharding import PartitionSpec as P

H = 16
HD = 64
STEP = 10
FC = ("fsdp", "ctx")
NY = 4
NX = 4
TP = 4

norm_eps = 1e-05
gelu_factor = 0.7978845608028654
matrix_rate = 0.05
vector_rate = 0.3
weight_decay = 0.1

f32 = jnp.float32
bf16 = jnp.bfloat16
VMEM_LIMIT = 48 * 1024 * 1024


def place(y, x, core):
    return (y * 2 + (x & 1)) * 4 + (x >> 1) * 2 + core


def shift_perm(dy=0, dx=0, dc=0):
    return [
        (place(y, x, c), place((y + dy) % NY, (x + dx) % NX, (c + dc) % 2))
        for y in range(NY)
        for x in range(NX)
        for c in range(2)
    ]


CHIPS = [
    [place(y, x, core) for y in range(NY) for x in (0, 2, 1, 3)] for core in range(2)
]


ALONG_Y = [[place(y, x, core) for y in range(NY)] for x in range(NX) for core in range(2)]


def move(value, dy=0, dx=0, dc=0):
    return lax.ppermute(value, FC, shift_perm(dy, dx, dc))


def move_tp(value, k):
    return lax.ppermute(value, "tp", [(i, (i + k) % TP) for i in range(TP)])


def chips_all_to_all(value, groups=CHIPS):
    return lax.all_to_all(
        value, FC, split_axis=0, concat_axis=0, tiled=True, axis_index_groups=groups
    )


def tp_spread(own):
    return [own] + [move_tp(own, k) for k in (1, 2, 3)]


def tp_exchange(chunks):
    return [chunks[0]] + [move_tp(chunks[k], -k) for k in (1, 2, 3)]


def turn_rows(values, t):
    rows = values.shape[0] // TP
    return [lax.dynamic_slice_in_dim(values, ((t - k) & 3) * rows, rows, 0) for k in range(TP)]


def assemble_kernel(spot, p0, p1, p2, p3, out_ref):
    for k, ref in enumerate((p0, p1, p2, p3)):
        at = pl.multiple_of(((spot[3] - k) & 3) * ROWS, ROWS)
        out_ref[pl.ds(at, ROWS), :] = ref[...]


def assemble(chunks, spot, after=()):
    return run(
        "assemble",
        assemble_kernel,
        [((TOK, D), f32)],
        [spot, *chunks],
        [SMEM] + [VMEM] * 4,
        after=after,
    )[0]


def kv_gather(own):
    across = move(own, dx=2)
    beside = move(own, dc=1)
    return [own, beside, across, move(across, dc=1)]


SMEM = pl.BlockSpec(memory_space=pltpu.SMEM)
VMEM = pl.BlockSpec(memory_space=pltpu.VMEM)
ANY = pl.BlockSpec(memory_space=pl.ANY)
ROWS = 64
TOK = 256
D = 1024
HW = 256


def last_last(a, b):
    return lax.dot_general(a, b, (((1,), (1,)), ((), ())), preferred_element_type=f32)


def first_first(a, b):
    return lax.dot_general(a, b, (((0,), (0,)), ((), ())), preferred_element_type=f32)


def matmul(a, b):
    return jnp.dot(a, b, preferred_element_type=f32)


def whole_of(refs):
    return jnp.concatenate([ref[...] for ref in refs], axis=0)


FIRST_HBM = ("join", "norm_back")
OUT_HBM = ("weight_grads", "chip_sum")


def in_hbm(arrays):
    return [pltpu.with_memory_space_constraint(array, pltpu.HBM) for array in arrays]


def run(name, kernel, outs, args, specs, out_specs=None, grid=None, scratch=(), after=()):
    count = len(args)
    extra = len(after)

    def wrapped(*refs):
        kernel(*refs[:count], *refs[count + extra :])

    if grid is None and any(spec.block_shape is not None for spec in specs):
        grid = (1,)
    grid_args = {} if grid is None else {"grid": grid}
    return pl.pallas_call(
        wrapped,
        out_shape=[
            pltpu.HBM(shape, dtype)
            if name in OUT_HBM or (k == 0 and name in FIRST_HBM)
            else jax.ShapeDtypeStruct(shape, dtype)
            for k, (shape, dtype) in enumerate(outs)
        ],
        in_specs=list(specs) + [ANY] * extra,
        out_specs=[VMEM] * len(outs) if out_specs is None else out_specs,
        scratch_shapes=list(scratch),
        compiler_params=pltpu.CompilerParams(vmem_limit_bytes=VMEM_LIMIT),
        name=name,
        **grid_args,
    )(*args, *[in_hbm([a])[0] if a.size > 300000 else a for a in after])


def weight_spec(weight, width, column, stepped=False):
    array, slot, offset = weight
    if stepped:
        if slot is None:
            return pl.BlockSpec((D, width), lambda i: (0, offset // width + i))
        return pl.BlockSpec((None, D, width), lambda i: (slot, 0, offset // width + i))
    if slot is None:
        return pl.BlockSpec((D, width), lambda i: (0, column))
    return pl.BlockSpec((None, D, width), lambda i: (slot, 0, column))


def full_spec(array):
    return pl.BlockSpec(array.shape, lambda i: (0,) * array.ndim)


CHUNKS = [((ROWS, D), f32)] + [((ROWS, D), bf16)] * 3


def store_chunks(total, refs):
    for k, ref in enumerate(refs):
        ref[...] = total[k * ROWS : (k + 1) * ROWS].astype(ref.dtype)


def norm_parts(values):
    centre = values - jnp.mean(values, axis=-1, keepdims=True)
    spread = jnp.mean(centre * centre, axis=-1, keepdims=True)
    scale = lax.rsqrt(spread + norm_eps)
    return centre * scale, scale


def spread_first_kernel(t_ref, v0, v1, v2, v3, weight_ref, out_ref):
    group = lax.broadcasted_iota(jnp.int32, (24, 32), 1) >> 3
    columns = jnp.zeros((24, 32), f32)
    for k, part in enumerate((v0, v1, v2, v3)):
        tiled = jnp.concatenate([part[...]] * TP, axis=1)
        columns = jnp.where(group == ((t_ref[0] - k) & 3), tiled, columns)
    high = columns.astype(bf16)
    low = (columns - high.astype(f32)).astype(bf16)
    extra = jnp.concatenate(
        [
            jnp.concatenate([high.astype(f32), low.astype(f32), jnp.zeros((24, 64), f32)], axis=1),
            jnp.zeros((8, 128), f32),
        ],
        axis=0,
    ).astype(bf16)
    slots = [weight_ref[:, s, :].astype(bf16) for s in range(4)]
    for k in range(16):
        for s in range(4):
            out_ref[k, :, s * HW : (s + 1) * HW] = slots[s]
        out_ref[k, :, D:] = extra


def unpack_kernel(core_ref, own_ref, other_ref, weight_ref, vector_ref):
    core = core_ref[0]
    for k in range(16):
        weight_ref[k, core] = own_ref[k, :, :D]
        weight_ref[k, 1 - core] = other_ref[k, :, :D]
        sums = [
            ref[k, :, D : D + 32].astype(f32) + ref[k, :, D + 32 : D + 64].astype(f32)
            for ref in (own_ref, other_ref)
        ]
        even = jnp.where(core == 0, sums[0], sums[1])
        odd = jnp.where(core == 0, sums[1], sums[0])
        vector_ref[:, k * 64 : k * 64 + 32] = even
        vector_ref[:, k * 64 + 32 : k * 64 + 64] = odd


def gather_first(attention_weight, vector_parts, t, core, after):
    (spread,) = run(
        "spread_first",
        spread_first_kernel,
        [((16, 32, D + 128), bf16)],
        [t[None], *vector_parts, attention_weight],
        [SMEM] + [VMEM] * 4 + [pl.BlockSpec((None, 32, 4, HW), lambda i: (0, 0, 0, 0))],
        after=after,
    )
    mine = chips_all_to_all(spread.reshape(512, D + 128))
    other = move(mine, dc=1)
    weight, vector = run(
        "unpack",
        unpack_kernel,
        [((16, 2, 32, D), bf16), ((32, D), f32)],
        [core[None], mine.reshape(16, 32, D + 128), other.reshape(16, 32, D + 128)],
        [SMEM, VMEM, VMEM],
    )
    return weight.reshape(D, D), vector


def x_slot(x):
    return (x & 1) * 2 + (x >> 1)


def pack_kernel(attention_ref, feedforward_ref, out_ref):
    for s in range(2):
        out_ref[s] = feedforward_ref[0, :, s, :].astype(bf16)
        out_ref[3 + s] = feedforward_ref[1, :, s, :].astype(bf16)
    for s in range(4):
        out_ref[2, :, s * HW : (s + 1) * HW] = attention_ref[:, s, :].astype(bf16)


def gather_rest(attention_weight, feedforward_weight):
    (packed,) = run(
        "pack",
        pack_kernel,
        [((5, 32, D), bf16)],
        [attention_weight, feedforward_weight],
        [pl.BlockSpec((None, 32, 4, HW), lambda i: (1, 0, 0, 0)), VMEM],
    )
    return lax.all_gather(packed, FC, axis=1, tiled=True)


def first_kernel(x0, x1, x2, x3, vec, w_ref, bq, bv, n0, n1, n2, n3, kv_ref, q_ref):
    normed = []
    for x, n in zip((x0, x1, x2, x3), (n0, n1, n2, n3)):
        unit, _ = norm_parts(x[...].astype(f32))
        value = (unit * vec[0:1, :] + vec[1:2, :]).astype(bf16)
        n[...] = value
        normed.append(value)
    project(jnp.concatenate(normed, axis=0), w_ref, bq, bv, kv_ref, q_ref)


def project(normed, w_ref, bq, bv, kv_ref, q_ref):
    kv_ref[:, :HW] = matmul(normed, w_ref[:, HW : 2 * HW]).astype(bf16)
    kv_ref[:, HW:] = (matmul(normed, w_ref[:, 2 * HW : 3 * HW]) + bv[...]).astype(bf16)
    q_ref[...] = (matmul(normed, w_ref[:, :HW]) + bq[...]).astype(bf16)


def project_kernel(n0, n1, n2, n3, w_ref, bq, bv, kv_ref, q_ref):
    project(whole_of((n0, n1, n2, n3)), w_ref, bq, bv, kv_ref, q_ref)


def place_of(row, block, t):
    return block * 256 + (((t - (row >> 6)) & 3) << 6) + (row & 63)


def attend_kernel(meta, slopes, q_ref, kv0, kv1, kv2, kv3, w_ref, mixed_ref, *chunk_refs):
    c, t, s1, s2 = meta[0], meta[1], meta[2], meta[3]
    blocks = (kv0, kv1, kv2, kv3)
    row_place = place_of(lax.broadcasted_iota(jnp.int32, (256, 1), 0), c, t)
    row_segment = (row_place >= s1).astype(jnp.int32) + (row_place >= s2).astype(jnp.int32)
    distances = []
    for k in range(4):
        key_place = place_of(lax.broadcasted_iota(jnp.int32, (1, 256), 1), c ^ k, t)
        key_segment = (key_place >= s1).astype(jnp.int32) + (key_place >= s2).astype(jnp.int32)
        gap = row_place - key_place
        allowed = (gap >= 0) & (row_segment == key_segment)
        distances.append(jnp.where(allowed, gap, -1).astype(f32))
    mixed = []
    for h in range(4):
        cols = slice(h * HD, (h + 1) * HD)
        value_cols = slice(256 + h * HD, 256 + (h + 1) * HD)
        query = q_ref[:, cols]
        slope = slopes[h]
        scores = [
            jnp.where(d >= 0, last_last(query, kv[:, cols]) * 0.125 - slope * d, -1e30)
            for d, kv in zip(distances, blocks)
        ]
        top = jnp.maximum(
            jnp.maximum(scores[0], scores[1]), jnp.maximum(scores[2], scores[3])
        ).max(axis=-1, keepdims=True)
        exponent = [jnp.exp(s - top) for s in scores]
        total = (exponent[0] + exponent[1] + exponent[2] + exponent[3]).sum(axis=-1, keepdims=True)
        scale = 1.0 / total
        mixed.append(
            sum(
                matmul((e * scale).astype(bf16), kv[:, value_cols])
                for e, kv in zip(exponent, blocks)
            )
        )
    mixed = jnp.concatenate(mixed, axis=1).astype(bf16)
    mixed_ref[...] = mixed
    store_chunks(last_last(mixed, w_ref[...]), chunk_refs)


def attend_back_kernel(
    meta, slopes, q_ref, b0, b1, b2, b3, w_ref, kv0, kv1, kv2, kv3, dq_ref, dkv0, dkv1, dkv2, dkv3
):
    c, t, s1, s2 = meta[0], meta[1], meta[2], meta[3]
    blocks = (kv0, kv1, kv2, kv3)
    back_blocks = (dkv0, dkv1, dkv2, dkv3)
    back_mixed = matmul(whole_of((b0, b1, b2, b3)), w_ref[...]).astype(bf16)
    row_place = place_of(lax.broadcasted_iota(jnp.int32, (1, 256), 1), c, t)
    row_segment = (row_place >= s1).astype(jnp.int32) + (row_place >= s2).astype(jnp.int32)
    distances = []
    for k in range(4):
        key_place = place_of(lax.broadcasted_iota(jnp.int32, (256, 1), 0), c ^ k, t)
        key_segment = (key_place >= s1).astype(jnp.int32) + (key_place >= s2).astype(jnp.int32)
        gap = row_place - key_place
        allowed = (gap >= 0) & (row_segment == key_segment)
        distances.append(jnp.where(allowed, gap, -1).astype(f32))
    turned = [kv[:, :256].astype(f32).T.astype(bf16) for kv in blocks]
    back_query = []
    back_keys = [[] for _ in range(4)]
    back_values = [[] for _ in range(4)]
    for h in range(4):
        cols = slice(h * HD, (h + 1) * HD)
        value_cols = slice(256 + h * HD, 256 + (h + 1) * HD)
        query = q_ref[:, cols]
        back_rows = back_mixed[:, cols]
        slope = slopes[h]
        scores = [
            jnp.where(d >= 0, last_last(kv[:, cols], query) * 0.125 - slope * d, -1e30)
            for d, kv in zip(distances, blocks)
        ]
        top = jnp.maximum(
            jnp.maximum(scores[0], scores[1]), jnp.maximum(scores[2], scores[3])
        ).max(axis=0, keepdims=True)
        exponent = [jnp.exp(s - top) for s in scores]
        total = (exponent[0] + exponent[1] + exponent[2] + exponent[3]).sum(axis=0, keepdims=True)
        scale = 1.0 / total
        probs = [e * scale for e in exponent]
        back_probs = [last_last(kv[:, value_cols], back_rows) for kv in blocks]
        products = [p * b for p, b in zip(probs, back_probs)]
        delta = (products[0] + products[1] + products[2] + products[3]).sum(axis=0, keepdims=True)
        turned_query = None
        for k in range(4):
            back_scores = (probs[k] * (back_probs[k] - delta)).astype(bf16)
            part = matmul(turned[k][cols], back_scores)
            turned_query = part if turned_query is None else turned_query + part
            back_keys[k].append(matmul(back_scores, query) * 0.125)
            back_values[k].append(matmul(probs[k].astype(bf16), back_rows))
        back_query.append(turned_query)
    dq_ref[...] = (jnp.concatenate(back_query, axis=0) * 0.125).T.astype(bf16)
    for k in range(4):
        back_blocks[k][...] = jnp.concatenate(back_keys[k] + back_values[k], axis=1).astype(bf16)


def join_kernel(p0, p1, p2, p3, base, vec, out_ref, normed_ref, *, bias, gain, shift):
    value = base[...].astype(f32) + (
        (p0[...] + p1[...].astype(f32)) + (p2[...].astype(f32) + p3[...].astype(f32))
    )
    value = value + vec[bias : bias + 1, :]
    out_ref[...] = value
    if normed_ref is not None:
        unit, _ = norm_parts(value)
        normed_ref[...] = (unit * vec[gain : gain + 1, :] + vec[shift : shift + 1, :]).astype(bf16)


def join(terms, base, vec, bias, gain=None, shift=None, after=()):
    def kernel(*refs):
        join_kernel(
            *refs[:7],
            refs[7] if gain is not None else None,
            bias=bias,
            gain=gain,
            shift=shift,
        )

    outs = [((ROWS, D), f32)] + ([((ROWS, D), bf16)] if gain is not None else [])
    return run(
        "join",
        kernel,
        outs,
        [*terms, *in_hbm([base]), vec],
        [VMEM] * 4 + [full_spec(base), VMEM],
        after=after,
    )


def norm_back_kernel(p0, p1, p2, p3, base, before, gain, out_ref, low_ref, rows_ref):
    back = (p0[...] + p1[...].astype(f32)) + (p2[...].astype(f32) + p3[...].astype(f32))
    unit, scale = norm_parts(before[...].astype(f32))
    scaled = back * gain[...]
    inner = scaled - jnp.mean(scaled, axis=-1, keepdims=True)
    inner = inner - unit * jnp.mean(scaled * unit, axis=-1, keepdims=True)
    out = base[...].astype(f32) + inner * scale
    out_ref[...] = out
    low = out.astype(bf16)
    low_ref[...] = low
    rows_ref[0:1, :] = jnp.sum(back * unit, axis=0, keepdims=True)
    rows_ref[1:2, :] = jnp.sum(back, axis=0, keepdims=True)
    rows_ref[2:3, :] = jnp.sum(low.astype(f32), axis=0, keepdims=True)
    rows_ref[3:8, :] = jnp.zeros((5, D), f32)


def norm_back(terms, base, before, gain, after=()):
    return run(
        "norm_back",
        norm_back_kernel,
        [((ROWS, D), f32), ((ROWS, D), bf16), ((8, D), f32)],
        [*terms, *in_hbm([base, before]), gain],
        [VMEM] * 4 + [full_spec(base), full_spec(before), VMEM],
        after=after,
    )


def forward_kernel(n0, n1, n2, n3, up, down, bias, hidden_ref, active_ref, c0, c1, c2, c3, total):
    step = pl.program_id(0)
    hidden = matmul(whole_of((n0, n1, n2, n3)), up[...]) + bias[...]
    hidden_ref[...] = hidden
    inner = gelu_factor * (hidden + 0.044715 * hidden * hidden * hidden)
    active = (0.5 * hidden * (1.0 + jnp.tanh(inner))).astype(bf16)
    active_ref[...] = active
    part = last_last(active, down[...])

    @pl.when(step == 0)
    def _():
        total[...] = part

    @pl.when(step > 0)
    def _():
        total[...] += part

    @pl.when(step == pl.num_programs(0) - 1)
    def _():
        store_chunks(total[...], (c0, c1, c2, c3))


def chunk_specs():
    return [pl.BlockSpec((ROWS, D), lambda i: (0, 0))] * 4


BLOCK = 512


def feedforward(chunks, up, down, bias, after=()):
    hidden_spec = pl.BlockSpec((TOK, BLOCK), lambda i: (0, i))
    hidden, active, *partial = run(
        "feedforward",
        forward_kernel,
        [((TOK, D), f32), ((TOK, D), bf16)] + CHUNKS,
        [*chunks, up[0], down[0], bias],
        chunk_specs()
        + [
            weight_spec(up, BLOCK, 0, True),
            weight_spec(down, BLOCK, 0, True),
            pl.BlockSpec((1, BLOCK), lambda i: (0, i)),
        ],
        [hidden_spec, hidden_spec] + chunk_specs(),
        grid=(D // BLOCK,),
        scratch=[pltpu.VMEM((TOK, D), f32)],
        after=after,
    )
    return hidden, active, partial


def backward_kernel(b0, b1, b2, b3, up, down, hidden_ref, back_ref, row_ref, c0, c1, c2, c3, total):
    step = pl.program_id(0)
    back_active = matmul(whole_of((b0, b1, b2, b3)), down[...])
    u = hidden_ref[...]
    square = u * u
    bent = jnp.tanh(gelu_factor * (u + 0.044715 * square * u))
    slope = 0.5 * (1.0 + bent) + 0.5 * u * (1.0 - bent * bent) * gelu_factor * (
        1.0 + 3 * 0.044715 * square
    )
    back = (back_active * slope).astype(bf16)
    back_ref[...] = back
    row_ref[...] = jnp.sum(back.astype(f32), axis=0, keepdims=True)
    part = last_last(back, up[...])

    @pl.when(step == 0)
    def _():
        total[...] = part

    @pl.when(step > 0)
    def _():
        total[...] += part

    @pl.when(step == pl.num_programs(0) - 1)
    def _():
        store_chunks(total[...], (c0, c1, c2, c3))


def feedforward_back(chunks, up, down, hidden, after=()):
    hidden_spec = pl.BlockSpec((TOK, BLOCK), lambda i: (0, i))
    row_spec = pl.BlockSpec((1, BLOCK), lambda i: (0, i))
    back, row, *partial = run(
        "feedforward_back",
        backward_kernel,
        [((TOK, D), bf16), ((1, D), f32)] + CHUNKS,
        [*chunks, up[0], down[0], hidden],
        chunk_specs()
        + [weight_spec(up, BLOCK, 0, True), weight_spec(down, BLOCK, 0, True), hidden_spec],
        [hidden_spec, row_spec] + chunk_specs(),
        grid=(D // BLOCK,),
        scratch=[pltpu.VMEM((TOK, D), f32)],
        after=after,
    )
    return back, row, partial


def project_back_kernel(dq_ref, own, beside, far, w_ref, kv_ref, row_ref, *chunk_refs):
    back_kv = (
        (own[...].astype(f32) + beside[...].astype(f32)) + far[...].astype(f32)
    ).astype(bf16)
    kv_ref[...] = back_kv
    row_ref[:, :HW] = jnp.sum(dq_ref[...].astype(f32), axis=0, keepdims=True)
    row_ref[:, HW:] = jnp.sum(back_kv.astype(f32), axis=0, keepdims=True)
    total = last_last(dq_ref[...], w_ref[:, :HW]) + last_last(back_kv, w_ref[:, HW : 3 * HW])
    store_chunks(total, chunk_refs)


def whole_weight_grads(pairs, after=()):
    widths = [rhs.shape[1] for _, rhs in pairs]
    width = sum(widths)
    count = len(pairs)
    block = 256

    def kernel(*refs):
        out_ref = refs[5 * count]
        start = 0
        for i, columns in enumerate(widths):
            grads = first_first(whole_of(refs[4 * i : 4 * i + 4]), refs[4 * count + i][...])
            out_ref[:, start : start + columns] = grads.astype(bf16)
            start += columns

    (out,) = run(
        "weight_grads",
        kernel,
        [((D, width), bf16)],
        [chunk for lhs, _ in pairs for chunk in lhs] + [rhs for _, rhs in pairs],
        [pl.BlockSpec((ROWS, block), lambda i: (0, i))] * (4 * count)
        + [pl.BlockSpec((TOK, w), lambda i: (0, 0)) for w in widths],
        [pl.BlockSpec((block, width), lambda i: (i, 0))],
        grid=(D // block,),
        after=after,
    )
    return out


def weight_grads(core, pairs, after=()):
    widths = [rhs.shape[1] for _, rhs in pairs]
    width = sum(widths)
    count = len(pairs)
    block = 256

    def kernel(*refs):
        core_ref, rest = refs[0], refs[1:]
        mine_ref, other_ref = rest[5 * count], rest[5 * count + 1]
        first = core_ref[0] == 0
        start = 0
        for i, columns in enumerate(widths):
            grads = first_first(whole_of(rest[4 * i : 4 * i + 4]), rest[4 * count + i][...])
            grads = grads.astype(bf16)
            for j in range(block // 64):
                even = grads[64 * j : 64 * j + 32]
                odd = grads[64 * j + 32 : 64 * j + 64]
                at = (slice(32 * j, 32 * j + 32), slice(start, start + columns))
                mine_ref[at] = jnp.where(first, even, odd)
                other_ref[at] = jnp.where(first, odd, even)
            start += columns

    lhs_spec = pl.BlockSpec((ROWS, block), lambda i: (0, i))
    out_spec = pl.BlockSpec((block // 2, width), lambda i: (i, 0))
    return run(
        "weight_grads",
        kernel,
        [((D // 2, width), bf16)] * 2,
        [core[None]] + [chunk for lhs, _ in pairs for chunk in lhs] + [rhs for _, rhs in pairs],
        [SMEM]
        + [lhs_spec] * (4 * count)
        + [pl.BlockSpec((TOK, w), lambda i: (0, 0)) for w in widths],
        [out_spec, out_spec],
        grid=(D // block,),
        after=after,
    )


def summed(pieces):
    return jnp.sum(pieces.reshape(16, 32, -1), axis=0, dtype=f32)


def pair_kernel(a, b, out_ref):
    out_ref[...] = (a[...].astype(f32) + b[...].astype(f32)).astype(bf16)


def pair_sum(a, b):
    return run("pair_sum", pair_kernel, [(a.shape, bf16)], [a, b], [VMEM] * 2)[0]


def chip_sum(grads, after=()):
    args = [part for mine, other in grads for part in (mine, move(other, dc=1))]
    widths = [mine.shape[1] for mine, _ in grads]
    rows = D // 8

    def kernel(*refs):
        start = 0
        for i, width in enumerate(widths):
            total = refs[2 * i][...].astype(f32) + refs[2 * i + 1][...].astype(f32)
            refs[-1][:, start : start + width] = total.astype(bf16)
            start += width

    return run(
        "chip_sum",
        kernel,
        [((D // 2, sum(widths)), bf16)],
        args,
        [pl.BlockSpec((rows, a.shape[1]), lambda i: (i, 0)) for a in args],
        [pl.BlockSpec((rows, sum(widths)), lambda i: (i, 0))],
        grid=(4,),
        after=after,
    )[0]


def hold_kernel(*refs):
    count = len(refs) // 2
    for k in range(count):
        refs[count + k][...] = refs[k][...]


def hold(arrays, after):
    return run(
        "hold",
        hold_kernel,
        [(a.shape, a.dtype) for a in arrays],
        arrays,
        [VMEM] * len(arrays),
        after=after,
    )


def feedforward_adamw_kernel(one_ref, zero_ref, weight, moment, second, m_ref, s_ref, w_ref):
    for layer, total in enumerate((zero_ref[...], one_ref[...].astype(f32))):
        for s in range(2):
            at = (layer, slice(None), s, slice(None))
            m_ref[at], s_ref[at], w_ref[at] = adamw_step(
                weight[at],
                moment[at],
                second[at],
                total[:, s * D : (s + 1) * D],
                matrix_rate,
                weight_decay,
            )


def feedforward_adamw(pieces_one, pieces_zero, weight, moment, second):
    shape = weight.shape
    return run(
        "feedforward_adamw",
        feedforward_adamw_kernel,
        [(shape, f32)] * 3,
        [pieces_one, pieces_zero, weight, moment, second],
        [VMEM] * 5,
    )


def core_sum_kernel(spot, mine, other, o0, o1, o2, o3):
    for k, ref in enumerate((o0, o1, o2, o3)):
        row = (spot[0] + k) & 3
        ref[0] = (mine[row, 0].astype(f32) + other[row, 0].astype(f32)).astype(bf16)


def core_sum(grads, spot, after=()):
    mine, other = (part.reshape(4, 4, 32, -1) for part in grads)
    other = move(other, dc=1)
    width = mine.shape[-1]
    whole_spec = pl.BlockSpec((4, 1, 32, width), lambda i: (0, i, 0, 0))
    part_spec = pl.BlockSpec((1, 32, width), lambda i: (i, 0, 0))
    return run(
        "core_sum",
        core_sum_kernel,
        [((4, 32, width), bf16)] * 4,
        [spot, mine, other],
        [SMEM, whole_spec, whole_spec],
        [part_spec] * 4,
        grid=(4,),
        after=after,
    )


def y_sum_kernel(spot, p0, p1, p2, p3, o0, o1, o2, o3):
    for k, ref in enumerate((o0, o1, o2, o3)):
        slot = x_slot((spot[1] + k) & 3)
        ref[...] = (
            (p0[slot].astype(f32) + p1[slot].astype(f32))
            + (p2[slot].astype(f32) + p3[slot].astype(f32))
        ).astype(bf16)


def y_sum_received(pieces, spot):
    width = pieces.shape[1]
    pieces = pieces.reshape(16, 32, width)
    return run(
        "y_sum",
        y_sum_kernel,
        [((32, width), bf16)] * 4,
        [spot] + [pieces] * 4,
        [SMEM] + [pl.BlockSpec((4, 32, width), lambda i, k=k: (k, 0, 0)) for k in range(4)],
    )


def y_sum(parts, spot, after=()):
    terms = [parts[0]] + [move(parts[k], dy=k) for k in (1, 2, 3)]
    width = parts[0].shape[-1]
    return run(
        "y_sum",
        y_sum_kernel,
        [((32, width), bf16)] * 4,
        [spot, *terms],
        [SMEM] + [VMEM] * 4,
        after=after,
    )


def x_sum(parts):
    return parts[0].astype(f32) + sum(move(parts[k], dx=k).astype(f32) for k in (1, 2, 3))


def vector_grads_kernel(spot, *refs):
    out_ref, whole = refs[-2], refs[-1]
    t = spot[3]
    whole[...] = jnp.zeros((32, D), f32)
    for layer in range(2):
        one, two, qkv, hidden, down = refs[5 * layer : 5 * layer + 5]
        at = 12 * layer
        whole[at : at + 2, :] = one[0:2, :]
        for s in range(4):
            cols = slice(s * HW, (s + 1) * HW)
            whole[at + 2 : at + 3, cols] = jnp.where(t == s, qkv[:, :HW], 0.0)
            whole[at + 3 : at + 4, cols] = jnp.where(t == s, qkv[:, 2 * HW :], 0.0)
            whole[at + 8 + s : at + 9 + s, :] = jnp.where(t == s, hidden[...], 0.0)
        whole[at + 4 : at + 5, :] = two[2:3, :]
        whole[at + 5 : at + 7, :] = two[0:2, :]
        whole[at + 7 : at + 8, :] = down[...]
    out_ref[...] = jnp.concatenate([whole[...], jnp.zeros((96, D), f32)], axis=0).T


def scatter_vectors(spot, rows):
    (partial,) = run(
        "vector_grads",
        vector_grads_kernel,
        [((D, 128), f32)],
        [spot, *rows],
        [SMEM] + [VMEM] * len(rows),
        scratch=[pltpu.VMEM((32, D), f32)],
    )
    value = lax.all_to_all(
        partial, ("fsdp", "ctx", "tp"), split_axis=0, concat_axis=0, tiled=True
    )
    return partial, jnp.sum(value.reshape(128, 8, 128), axis=0)[:, :24].T.reshape(2, 12, 8)


def adamw_step(weight, moment, second, gradient, step_rate, decay_rate):
    moment = 0.9 * moment + 0.1 * gradient
    second = 0.95 * second + 0.05 * gradient * gradient
    first_fix = 1.0 - 0.9**STEP
    second_fix = 1.0 - 0.95**STEP
    update = moment / first_fix / (jnp.sqrt(second / second_fix) + 1e-08) + decay_rate * weight
    return (moment, second, weight - step_rate * update)


def body(
    block_input,
    cotangent,
    sequence_starts,
    attention_weight,
    attention_first,
    attention_second,
    feedforward_weight,
    feedforward_first,
    feedforward_second,
    vector_weight,
    vector_first,
    vector_second,
):
    c = lax.axis_index("ctx")
    t = lax.axis_index("tp")
    core = (c & 1).astype(jnp.int32)
    meta = jnp.stack([c, t, sequence_starts[0, 0], sequence_starts[0, 1]]).astype(jnp.int32)
    slopes = jnp.exp2(-8.0 * ((t * 4 + jnp.arange(4, dtype=jnp.int32)).astype(f32) + 1.0) / H)

    fsdp = lax.axis_index("fsdp")
    spot = jnp.stack([fsdp >> 1, (fsdp & 1) + (c >> 1) * 2, c & 1, t]).astype(jnp.int32)
    with jax.named_scope("gather_rest"):
        rest = gather_rest(attention_weight, feedforward_weight)
    with jax.named_scope("gather_first"):
        vector_parts = tp_spread(vector_weight.reshape(24, 8))
        attention_zero, vectors = gather_first(
            attention_weight, vector_parts, t.astype(jnp.int32), core, (meta, slopes)
        )
    attention_of = ((attention_zero, None, 0), (rest, 2, 0))
    up_of = ((rest, 0, 0), (rest, 3, 0))
    down_of = ((rest, 1, 0), (rest, 4, 0))

    input_chunks = turn_rows(block_input, t)
    stream = input_chunks[0]
    kept = []
    normed_own = None
    for layer in range(2):
        vector = lax.slice_in_dim(vectors, 12 * layer, 12 * layer + 12, axis=0)
        bias_query = lax.dynamic_slice(vector, (2, t * HW), (1, HW))
        bias_value = lax.dynamic_slice(vector, (3, t * HW), (1, HW))
        bias_hidden = lax.dynamic_slice(vector, (8 + t, 0), (1, D))
        weight = attention_of[layer]
        qkv_spec = weight_spec(weight, 3 * HW, 0)
        out_spec = weight_spec(weight, HW, 3)
        with jax.named_scope(f"project_{layer}"):
            if layer == 0:
                *normed, kv_own, queries = run(
                    "first",
                    first_kernel,
                    [((ROWS, D), bf16)] * 4 + [((TOK, 2 * HW), bf16), ((TOK, HW), bf16)],
                    [*input_chunks, vector, weight[0], bias_query, bias_value],
                    [VMEM] * 5 + [qkv_spec, VMEM, VMEM],
                )
            else:
                normed = tp_spread(normed_own)
                kv_own, queries = run(
                    "project",
                    project_kernel,
                    [((TOK, 2 * HW), bf16), ((TOK, HW), bf16)],
                    [*normed, weight[0], bias_query, bias_value],
                    [VMEM] * 4 + [qkv_spec, VMEM, VMEM],
                )
            kv_blocks = kv_gather(kv_own)
        with jax.named_scope(f"attend_{layer}"):
            mixed, *partial = run(
                "attend",
                attend_kernel,
                [((TOK, HW), bf16)] + CHUNKS,
                [meta, slopes, queries, *kv_blocks, weight[0]],
                [SMEM, SMEM] + [VMEM] * 5 + [out_spec],
            )
        with jax.named_scope(f"join_attend_{layer}"):
            before = stream
            middle, normed_two_own = join(
                tp_exchange(partial),
                stream,
                vector,
                4,
                5,
                6,
            )
        with jax.named_scope(f"feedforward_{layer}"):
            normed_two = tp_spread(normed_two_own)
            hidden, active, partial = feedforward(
                normed_two, up_of[layer], down_of[layer], bias_hidden
            )
        with jax.named_scope(f"join_feedforward_{layer}"):
            if layer == 0:
                stream, normed_own = join(tp_exchange(partial), middle, vectors, 7, 12, 13)
            else:
                last_partial, last_vector, last_middle = partial, vector, middle
        kept.append(
            (before, normed, queries, kv_blocks, mixed, middle, normed_two, hidden, active)
        )
    back_chunks = turn_rows(cotangent, t)
    back = back_chunks[0]
    back_down_row = jnp.sum(back.astype(f32), axis=0, keepdims=True)
    vector_rows = [None, None]
    pieces = {}
    for layer in (1, 0):
        before, normed, queries, kv_blocks, mixed, middle, normed_two, hidden, active = kept[layer]
        vector = lax.slice_in_dim(vectors, 12 * layer, 12 * layer + 12, axis=0)
        weight = attention_of[layer]
        qkv_spec = weight_spec(weight, 3 * HW, 0)
        out_spec = weight_spec(weight, HW, 3)
        with jax.named_scope(f"back_feedforward_{layer}"):
            if layer == 0:
                back_chunks = tp_spread(back_own)
            back_hidden, hidden_row, partial = feedforward_back(
                back_chunks,
                up_of[layer],
                down_of[layer],
                hidden,
            )
            terms = tp_exchange(partial)
        with jax.named_scope(f"grads_feedforward_{layer}"):
            pairs = [(in_hbm(normed_two), back_hidden), (back_chunks, *in_hbm([active]))]
            if layer == 1:
                grads_ff = whole_weight_grads(pairs)
                pieces["ff1"] = lax.psum_scatter(grads_ff, FC, scatter_dimension=0, tiled=True)
                tied = (grads_ff,)
            else:
                grads_ff = weight_grads(core, pairs)
                chip_ff = chip_sum([grads_ff, grads_att])
                column_ff = chips_all_to_all(chip_ff, ALONG_Y)
                tied = (grads_ff[0],)
        with jax.named_scope(f"back_norm_two_{layer}"):
            back_middle, back_attn_own, rows_two = norm_back(
                terms,
                back,
                middle,
                vector[5:6],
                after=tied,
            )
            back_attn = tp_spread(back_attn_own)
        with jax.named_scope(f"back_attend_{layer}"):
            back_query, part_own, part_beside, part_across, part_corner = run(
                "attend_back",
                attend_back_kernel,
                [((TOK, HW), bf16)] + [((TOK, 2 * HW), bf16)] * 4,
                [meta, slopes, queries, *back_attn, weight[0], *kv_blocks],
                [SMEM, SMEM, full_spec(queries)]
                + [VMEM] * 4
                + [out_spec]
                + [full_spec(kv) for kv in kv_blocks],
                after=(chip_ff,) if layer == 0 else (),
            )
        with jax.named_scope(f"back_project_{layer}"):
            beside = move(part_beside, dc=1)
            far = move(pair_sum(part_across, move(part_corner, dc=1)), dx=2)
            if layer == 1:
                held = hold(last_partial[1:], after=(part_own,))
                (stream,) = join(
                    tp_exchange([last_partial[0], *held]), last_middle, last_vector, 7
                )
            else:
                output_chunks = tp_spread(hold([stream], after=(part_own,))[0])
            back_kv, qkv_row, *partial = run(
                "project_back",
                project_back_kernel,
                [((TOK, 2 * HW), bf16), ((1, 3 * HW), f32)] + CHUNKS,
                [back_query, part_own, beside, far, weight[0]],
                [VMEM] * 4 + [qkv_spec],
                after=(stream,) if layer == 1 else tuple(output_chunks[1:]),
            )
            terms = tp_exchange(partial)
        with jax.named_scope(f"grads_attention_{layer}"):
            normed = in_hbm(normed)
            grads = weight_grads(
                core,
                [(normed, back_query), (normed, back_kv), (back_attn, *in_hbm([mixed]))],
            )
            if layer == 1:
                grads_att = grads
            else:
                pieces["ff0"] = y_sum_received(column_ff, spot)
                pieces["att0"] = core_sum(grads, spot)
        with jax.named_scope(f"back_norm_one_{layer}"):
            back, back_own, rows_one = norm_back(
                terms,
                back_middle,
                before,
                vector[0:1],
                after=(grads[0],) if layer == 1 else (pieces["att0"][0], pieces["ff0"][0]),
            )
        vector_rows[layer] = (rows_one, rows_two, qkv_row, hidden_row, back_down_row)
        back_down_row = rows_one[2:3]
    with jax.named_scope("input_gradient"):
        input_gradient = assemble(tp_spread(back), spot)
    with jax.named_scope("block_output"):
        block_output = assemble(output_chunks, spot, after=(back_own,))
    with jax.named_scope("scatter_vectors"):
        vector_partial, vector_total = scatter_vectors(spot, vector_rows[0] + vector_rows[1])
    with jax.named_scope("grads_attention_0"):
        pieces["att0"] = [pieces["att0"][0], *hold(pieces["att0"][1:], after=(back_own,))]
    with jax.named_scope("adamw"):
        owned_zero = x_sum(pieces["ff0"])
        attention_total = jnp.stack(
            [x_sum(y_sum(pieces["att0"], spot, (vector_total,))), owned_zero[:, 2 * D :]]
        ).reshape(2, 32, 4, HW)
        attention_out = adamw_step(
            attention_weight,
            attention_first,
            attention_second,
            attention_total,
            matrix_rate,
            weight_decay,
        )
        feedforward_out = feedforward_adamw(
            pieces["ff1"],
            owned_zero[:, : 2 * D],
            feedforward_weight,
            feedforward_first,
            feedforward_second,
        )
        vector_out = adamw_step(
            vector_weight, vector_first, vector_second, vector_total, vector_rate, 0.0
        )
    return (block_output, input_gradient, *attention_out, *feedforward_out, *vector_out)


def solution(mesh):
    tokens = P(FC, None)
    weights = P(None, FC, None, "tp")
    vectors = P(None, None, ("fsdp", "ctx", "tp"))
    in_specs = (tokens, tokens, P("fsdp", None)) + (weights,) * 6 + (vectors,) * 3
    out_specs = (tokens,) * 2 + (weights,) * 6 + (vectors,) * 3
    return jax.shard_map(body, mesh=mesh, in_specs=in_specs, out_specs=out_specs, check_vma=False)
```

```python
import jax
import jax.numpy as jnp
from jax import lax
from jax.experimental import pallas as pl
from jax.experimental.pallas import tpu as pltpu
from jax.sharding import PartitionSpec as P

H = 16
HD = 64
STEP = 10
FC = ("fsdp", "ctx")
NY = 4
NX = 4
TP = 4

norm_eps = 1e-05
gelu_factor = 0.7978845608028654
matrix_rate = 0.05
vector_rate = 0.3
weight_decay = 0.1

f32 = jnp.float32
bf16 = jnp.bfloat16
VMEM_LIMIT = 48 * 1024 * 1024


def place(y, x, core):
    return (y * 2 + (x & 1)) * 4 + (x >> 1) * 2 + core


def shift_perm(dy=0, dx=0, dc=0):
    return [
        (place(y, x, c), place((y + dy) % NY, (x + dx) % NX, (c + dc) % 2))
        for y in range(NY)
        for x in range(NX)
        for c in range(2)
    ]


CHIPS = [
    [place(y, x, core) for y in range(NY) for x in (0, 2, 1, 3)] for core in range(2)
]


ALONG_X = [[place(y, x, core) for x in (0, 2, 1, 3)] for y in range(NY) for core in range(2)]
ALONG_Y = [[place(y, x, core) for y in range(NY)] for x in range(NX) for core in range(2)]


def move(value, dy=0, dx=0, dc=0):
    return lax.ppermute(value, FC, shift_perm(dy, dx, dc))


def move_tp(value, k):
    return lax.ppermute(value, "tp", [(i, (i + k) % TP) for i in range(TP)])


def chips_all_to_all(value, groups=CHIPS):
    return lax.all_to_all(
        value, FC, split_axis=0, concat_axis=0, tiled=True, axis_index_groups=groups
    )


def tp_spread(own):
    return [own] + [move_tp(own, k) for k in (1, 2, 3)]


def tp_exchange(chunks):
    return [chunks[0]] + [move_tp(chunks[k], -k) for k in (1, 2, 3)]


def turn_rows(values, t):
    rows = values.shape[0] // TP
    return [lax.dynamic_slice_in_dim(values, ((t - k) & 3) * rows, rows, 0) for k in range(TP)]


def assemble_kernel(spot, p0, p1, p2, p3, out_ref):
    for k, ref in enumerate((p0, p1, p2, p3)):
        at = pl.multiple_of(((spot[3] - k) & 3) * ROWS, ROWS)
        out_ref[pl.ds(at, ROWS), :] = ref[...]


def assemble(chunks, spot, after=()):
    return run(
        "assemble",
        assemble_kernel,
        [((TOK, D), f32)],
        [spot, *chunks],
        [SMEM] + [VMEM] * 4,
        after=after,
    )[0]


def kv_gather(own):
    across = move(own, dx=2)
    beside = move(own, dc=1)
    return [own, beside, across, move(across, dc=1)]


SMEM = pl.BlockSpec(memory_space=pltpu.SMEM)
VMEM = pl.BlockSpec(memory_space=pltpu.VMEM)
ANY = pl.BlockSpec(memory_space=pl.ANY)
ROWS = 64
TOK = 256
D = 1024
HW = 256


def last_last(a, b):
    return lax.dot_general(a, b, (((1,), (1,)), ((), ())), preferred_element_type=f32)


def first_first(a, b):
    return lax.dot_general(a, b, (((0,), (0,)), ((), ())), preferred_element_type=f32)


def matmul(a, b):
    return jnp.dot(a, b, preferred_element_type=f32)


def whole_of(refs):
    return jnp.concatenate([ref[...] for ref in refs], axis=0)


FIRST_HBM = ("join", "norm_back")
OUT_HBM = ("weight_grads", "chip_sum")


def in_hbm(arrays):
    return [pltpu.with_memory_space_constraint(array, pltpu.HBM) for array in arrays]


def run(name, kernel, outs, args, specs, out_specs=None, grid=None, scratch=(), after=()):
    count = len(args)
    extra = len(after)

    def wrapped(*refs):
        kernel(*refs[:count], *refs[count + extra :])

    if grid is None and any(spec.block_shape is not None for spec in specs):
        grid = (1,)
    grid_args = {} if grid is None else {"grid": grid}
    return pl.pallas_call(
        wrapped,
        out_shape=[
            pltpu.HBM(shape, dtype)
            if name in OUT_HBM or (k == 0 and name in FIRST_HBM)
            else jax.ShapeDtypeStruct(shape, dtype)
            for k, (shape, dtype) in enumerate(outs)
        ],
        in_specs=list(specs) + [ANY] * extra,
        out_specs=[VMEM] * len(outs) if out_specs is None else out_specs,
        scratch_shapes=list(scratch),
        compiler_params=pltpu.CompilerParams(vmem_limit_bytes=VMEM_LIMIT),
        name=name,
        **grid_args,
    )(*args, *[in_hbm([a])[0] if a.size > 300000 else a for a in after])


def weight_spec(weight, width, column, stepped=False):
    array, slot, offset = weight
    if stepped:
        if slot is None:
            return pl.BlockSpec((D, width), lambda i: (0, offset // width + i))
        return pl.BlockSpec((None, D, width), lambda i: (slot, 0, offset // width + i))
    if slot is None:
        return pl.BlockSpec((D, width), lambda i: (0, column))
    return pl.BlockSpec((None, D, width), lambda i: (slot, 0, column))


def full_spec(array):
    return pl.BlockSpec(array.shape, lambda i: (0,) * array.ndim)


CHUNKS = [((ROWS, D), f32)] + [((ROWS, D), bf16)] * 3


def store_chunks(total, refs):
    for k, ref in enumerate(refs):
        ref[...] = total[k * ROWS : (k + 1) * ROWS].astype(ref.dtype)


def norm_parts(values):
    centre = values - jnp.mean(values, axis=-1, keepdims=True)
    spread = jnp.mean(centre * centre, axis=-1, keepdims=True)
    scale = lax.rsqrt(spread + norm_eps)
    return centre * scale, scale


def spread_first_kernel(t_ref, v0, v1, v2, v3, weight_ref, out_ref):
    group = lax.broadcasted_iota(jnp.int32, (24, 32), 1) >> 3
    columns = jnp.zeros((24, 32), f32)
    for k, part in enumerate((v0, v1, v2, v3)):
        tiled = jnp.concatenate([part[...]] * TP, axis=1)
        columns = jnp.where(group == ((t_ref[0] - k) & 3), tiled, columns)
    high = columns.astype(bf16)
    low = (columns - high.astype(f32)).astype(bf16)
    extra = jnp.concatenate(
        [
            jnp.concatenate([high.astype(f32), low.astype(f32), jnp.zeros((24, 64), f32)], axis=1),
            jnp.zeros((8, 128), f32),
        ],
        axis=0,
    ).astype(bf16)
    slots = [weight_ref[:, s, :].astype(bf16) for s in range(4)]
    for k in range(16):
        for s in range(4):
            out_ref[k, :, s * HW : (s + 1) * HW] = slots[s]
        out_ref[k, :, D:] = extra


def unpack_kernel(core_ref, own_ref, other_ref, weight_ref, vector_ref):
    core = core_ref[0]
    for k in range(16):
        weight_ref[k, core] = own_ref[k, :, :D]
        weight_ref[k, 1 - core] = other_ref[k, :, :D]
        sums = [
            ref[k, :, D : D + 32].astype(f32) + ref[k, :, D + 32 : D + 64].astype(f32)
            for ref in (own_ref, other_ref)
        ]
        even = jnp.where(core == 0, sums[0], sums[1])
        odd = jnp.where(core == 0, sums[1], sums[0])
        vector_ref[:, k * 64 : k * 64 + 32] = even
        vector_ref[:, k * 64 + 32 : k * 64 + 64] = odd


def gather_first(attention_weight, vector_parts, t, core, after):
    (spread,) = run(
        "spread_first",
        spread_first_kernel,
        [((16, 32, D + 128), bf16)],
        [t[None], *vector_parts, attention_weight],
        [SMEM] + [VMEM] * 4 + [pl.BlockSpec((None, 32, 4, HW), lambda i: (0, 0, 0, 0))],
        after=after,
    )
    mine = chips_all_to_all(spread.reshape(512, D + 128))
    other = move(mine, dc=1)
    weight, vector = run(
        "unpack",
        unpack_kernel,
        [((16, 2, 32, D), bf16), ((32, D), f32)],
        [core[None], mine.reshape(16, 32, D + 128), other.reshape(16, 32, D + 128)],
        [SMEM, VMEM, VMEM],
    )
    return weight.reshape(D, D), vector


def x_slot(x):
    return (x & 1) * 2 + (x >> 1)


def pack_kernel(attention_ref, feedforward_ref, out_ref):
    for s in range(2):
        out_ref[s] = feedforward_ref[0, :, s, :].astype(bf16)
        out_ref[3 + s] = feedforward_ref[1, :, s, :].astype(bf16)
    for s in range(4):
        out_ref[2, :, s * HW : (s + 1) * HW] = attention_ref[:, s, :].astype(bf16)


def gather_rest(attention_weight, feedforward_weight):
    (packed,) = run(
        "pack",
        pack_kernel,
        [((5, 32, D), bf16)],
        [attention_weight, feedforward_weight],
        [pl.BlockSpec((None, 32, 4, HW), lambda i: (1, 0, 0, 0)), VMEM],
    )
    return lax.all_gather(packed, FC, axis=1, tiled=True)


def first_kernel(x0, x1, x2, x3, vec, w_ref, bq, bv, n0, n1, n2, n3, kv_ref, q_ref):
    normed = []
    for x, n in zip((x0, x1, x2, x3), (n0, n1, n2, n3)):
        unit, _ = norm_parts(x[...].astype(f32))
        value = (unit * vec[0:1, :] + vec[1:2, :]).astype(bf16)
        n[...] = value
        normed.append(value)
    project(jnp.concatenate(normed, axis=0), w_ref, bq, bv, kv_ref, q_ref)


def project(normed, w_ref, bq, bv, kv_ref, q_ref):
    kv_ref[:, :HW] = matmul(normed, w_ref[:, HW : 2 * HW]).astype(bf16)
    kv_ref[:, HW:] = (matmul(normed, w_ref[:, 2 * HW : 3 * HW]) + bv[...]).astype(bf16)
    q_ref[...] = (matmul(normed, w_ref[:, :HW]) + bq[...]).astype(bf16)


def project_kernel(n0, n1, n2, n3, w_ref, bq, bv, kv_ref, q_ref):
    project(whole_of((n0, n1, n2, n3)), w_ref, bq, bv, kv_ref, q_ref)


def place_of(row, block, t):
    return block * 256 + (((t - (row >> 6)) & 3) << 6) + (row & 63)


def attend_kernel(meta, slopes, q_ref, kv0, kv1, kv2, kv3, w_ref, mixed_ref, *chunk_refs):
    c, t, s1, s2 = meta[0], meta[1], meta[2], meta[3]
    blocks = (kv0, kv1, kv2, kv3)
    row_place = place_of(lax.broadcasted_iota(jnp.int32, (256, 1), 0), c, t)
    row_segment = (row_place >= s1).astype(jnp.int32) + (row_place >= s2).astype(jnp.int32)
    distances = []
    for k in range(4):
        key_place = place_of(lax.broadcasted_iota(jnp.int32, (1, 256), 1), c ^ k, t)
        key_segment = (key_place >= s1).astype(jnp.int32) + (key_place >= s2).astype(jnp.int32)
        gap = row_place - key_place
        allowed = (gap >= 0) & (row_segment == key_segment)
        distances.append(jnp.where(allowed, gap, -1).astype(f32))
    mixed = []
    for h in range(4):
        cols = slice(h * HD, (h + 1) * HD)
        value_cols = slice(256 + h * HD, 256 + (h + 1) * HD)
        query = q_ref[:, cols]
        slope = slopes[h]
        scores = [
            jnp.where(d >= 0, last_last(query, kv[:, cols]) * 0.125 - slope * d, -1e30)
            for d, kv in zip(distances, blocks)
        ]
        top = jnp.maximum(
            jnp.maximum(scores[0], scores[1]), jnp.maximum(scores[2], scores[3])
        ).max(axis=-1, keepdims=True)
        exponent = [jnp.exp(s - top) for s in scores]
        total = (exponent[0] + exponent[1] + exponent[2] + exponent[3]).sum(axis=-1, keepdims=True)
        scale = 1.0 / total
        mixed.append(
            sum(
                matmul((e * scale).astype(bf16), kv[:, value_cols])
                for e, kv in zip(exponent, blocks)
            )
        )
    mixed = jnp.concatenate(mixed, axis=1).astype(bf16)
    mixed_ref[...] = mixed
    store_chunks(last_last(mixed, w_ref[...]), chunk_refs)


def attend_back_kernel(
    meta, slopes, q_ref, b0, b1, b2, b3, w_ref, kv0, kv1, kv2, kv3, dq_ref, dkv0, dkv1, dkv2, dkv3
):
    c, t, s1, s2 = meta[0], meta[1], meta[2], meta[3]
    blocks = (kv0, kv1, kv2, kv3)
    back_blocks = (dkv0, dkv1, dkv2, dkv3)
    back_mixed = matmul(whole_of((b0, b1, b2, b3)), w_ref[...]).astype(bf16)
    row_place = place_of(lax.broadcasted_iota(jnp.int32, (1, 256), 1), c, t)
    row_segment = (row_place >= s1).astype(jnp.int32) + (row_place >= s2).astype(jnp.int32)
    distances = []
    for k in range(4):
        key_place = place_of(lax.broadcasted_iota(jnp.int32, (256, 1), 0), c ^ k, t)
        key_segment = (key_place >= s1).astype(jnp.int32) + (key_place >= s2).astype(jnp.int32)
        gap = row_place - key_place
        allowed = (gap >= 0) & (row_segment == key_segment)
        distances.append(jnp.where(allowed, gap, -1).astype(f32))
    turned = [kv[:, :256].astype(f32).T.astype(bf16) for kv in blocks]
    back_query = []
    back_keys = [[] for _ in range(4)]
    back_values = [[] for _ in range(4)]
    for h in range(4):
        cols = slice(h * HD, (h + 1) * HD)
        value_cols = slice(256 + h * HD, 256 + (h + 1) * HD)
        query = q_ref[:, cols]
        back_rows = back_mixed[:, cols]
        slope = slopes[h]
        scores = [
            jnp.where(d >= 0, last_last(kv[:, cols], query) * 0.125 - slope * d, -1e30)
            for d, kv in zip(distances, blocks)
        ]
        top = jnp.maximum(
            jnp.maximum(scores[0], scores[1]), jnp.maximum(scores[2], scores[3])
        ).max(axis=0, keepdims=True)
        exponent = [jnp.exp(s - top) for s in scores]
        total = (exponent[0] + exponent[1] + exponent[2] + exponent[3]).sum(axis=0, keepdims=True)
        scale = 1.0 / total
        probs = [e * scale for e in exponent]
        back_probs = [last_last(kv[:, value_cols], back_rows) for kv in blocks]
        products = [p * b for p, b in zip(probs, back_probs)]
        delta = (products[0] + products[1] + products[2] + products[3]).sum(axis=0, keepdims=True)
        turned_query = None
        for k in range(4):
            back_scores = (probs[k] * (back_probs[k] - delta)).astype(bf16)
            part = matmul(turned[k][cols], back_scores)
            turned_query = part if turned_query is None else turned_query + part
            back_keys[k].append(matmul(back_scores, query) * 0.125)
            back_values[k].append(matmul(probs[k].astype(bf16), back_rows))
        back_query.append(turned_query)
    dq_ref[...] = (jnp.concatenate(back_query, axis=0) * 0.125).T.astype(bf16)
    for k in range(4):
        back_blocks[k][...] = jnp.concatenate(back_keys[k] + back_values[k], axis=1).astype(bf16)


def join_kernel(p0, p1, p2, p3, base, vec, out_ref, normed_ref, *, bias, gain, shift):
    value = base[...].astype(f32) + (
        (p0[...] + p1[...].astype(f32)) + (p2[...].astype(f32) + p3[...].astype(f32))
    )
    value = value + vec[bias : bias + 1, :]
    out_ref[...] = value
    if normed_ref is not None:
        unit, _ = norm_parts(value)
        normed_ref[...] = (unit * vec[gain : gain + 1, :] + vec[shift : shift + 1, :]).astype(bf16)


def join(terms, base, vec, bias, gain=None, shift=None, after=()):
    def kernel(*refs):
        join_kernel(
            *refs[:7],
            refs[7] if gain is not None else None,
            bias=bias,
            gain=gain,
            shift=shift,
        )

    outs = [((ROWS, D), f32)] + ([((ROWS, D), bf16)] if gain is not None else [])
    return run(
        "join",
        kernel,
        outs,
        [*terms, *in_hbm([base]), vec],
        [VMEM] * 4 + [full_spec(base), VMEM],
        after=after,
    )


def norm_back_kernel(p0, p1, p2, p3, base, before, gain, out_ref, low_ref, rows_ref):
    back = (p0[...] + p1[...].astype(f32)) + (p2[...].astype(f32) + p3[...].astype(f32))
    unit, scale = norm_parts(before[...].astype(f32))
    scaled = back * gain[...]
    inner = scaled - jnp.mean(scaled, axis=-1, keepdims=True)
    inner = inner - unit * jnp.mean(scaled * unit, axis=-1, keepdims=True)
    out = base[...].astype(f32) + inner * scale
    out_ref[...] = out
    low = out.astype(bf16)
    low_ref[...] = low
    rows_ref[0:1, :] = jnp.sum(back * unit, axis=0, keepdims=True)
    rows_ref[1:2, :] = jnp.sum(back, axis=0, keepdims=True)
    rows_ref[2:3, :] = jnp.sum(low.astype(f32), axis=0, keepdims=True)
    rows_ref[3:8, :] = jnp.zeros((5, D), f32)


def norm_back(terms, base, before, gain, after=()):
    return run(
        "norm_back",
        norm_back_kernel,
        [((ROWS, D), f32), ((ROWS, D), bf16), ((8, D), f32)],
        [*terms, *in_hbm([base, before]), gain],
        [VMEM] * 4 + [full_spec(base), full_spec(before), VMEM],
        after=after,
    )


def forward_kernel(n0, n1, n2, n3, up, down, bias, hidden_ref, active_ref, c0, c1, c2, c3, total):
    step = pl.program_id(0)
    hidden = matmul(whole_of((n0, n1, n2, n3)), up[...]) + bias[...]
    hidden_ref[...] = hidden
    inner = gelu_factor * (hidden + 0.044715 * hidden * hidden * hidden)
    active = (0.5 * hidden * (1.0 + jnp.tanh(inner))).astype(bf16)
    active_ref[...] = active
    part = last_last(active, down[...])

    @pl.when(step == 0)
    def _():
        total[...] = part

    @pl.when(step > 0)
    def _():
        total[...] += part

    @pl.when(step == pl.num_programs(0) - 1)
    def _():
        store_chunks(total[...], (c0, c1, c2, c3))


def chunk_specs():
    return [pl.BlockSpec((ROWS, D), lambda i: (0, 0))] * 4


BLOCK = 512


def feedforward(chunks, up, down, bias, after=()):
    hidden_spec = pl.BlockSpec((TOK, BLOCK), lambda i: (0, i))
    hidden, active, *partial = run(
        "feedforward",
        forward_kernel,
        [((TOK, D), f32), ((TOK, D), bf16)] + CHUNKS,
        [*chunks, up[0], down[0], bias],
        chunk_specs()
        + [
            weight_spec(up, BLOCK, 0, True),
            weight_spec(down, BLOCK, 0, True),
            pl.BlockSpec((1, BLOCK), lambda i: (0, i)),
        ],
        [hidden_spec, hidden_spec] + chunk_specs(),
        grid=(D // BLOCK,),
        scratch=[pltpu.VMEM((TOK, D), f32)],
        after=after,
    )
    return hidden, active, partial


def backward_kernel(b0, b1, b2, b3, up, down, hidden_ref, back_ref, row_ref, c0, c1, c2, c3, total):
    step = pl.program_id(0)
    back_active = matmul(whole_of((b0, b1, b2, b3)), down[...])
    u = hidden_ref[...]
    square = u * u
    bent = jnp.tanh(gelu_factor * (u + 0.044715 * square * u))
    slope = 0.5 * (1.0 + bent) + 0.5 * u * (1.0 - bent * bent) * gelu_factor * (
        1.0 + 3 * 0.044715 * square
    )
    back = (back_active * slope).astype(bf16)
    back_ref[...] = back
    row_ref[...] = jnp.sum(back.astype(f32), axis=0, keepdims=True)
    part = last_last(back, up[...])

    @pl.when(step == 0)
    def _():
        total[...] = part

    @pl.when(step > 0)
    def _():
        total[...] += part

    @pl.when(step == pl.num_programs(0) - 1)
    def _():
        store_chunks(total[...], (c0, c1, c2, c3))


def feedforward_back(chunks, up, down, hidden, after=()):
    hidden_spec = pl.BlockSpec((TOK, BLOCK), lambda i: (0, i))
    row_spec = pl.BlockSpec((1, BLOCK), lambda i: (0, i))
    back, row, *partial = run(
        "feedforward_back",
        backward_kernel,
        [((TOK, D), bf16), ((1, D), f32)] + CHUNKS,
        [*chunks, up[0], down[0], hidden],
        chunk_specs()
        + [weight_spec(up, BLOCK, 0, True), weight_spec(down, BLOCK, 0, True), hidden_spec],
        [hidden_spec, row_spec] + chunk_specs(),
        grid=(D // BLOCK,),
        scratch=[pltpu.VMEM((TOK, D), f32)],
        after=after,
    )
    return back, row, partial


def project_back_kernel(dq_ref, own, beside, far, w_ref, kv_ref, row_ref, *chunk_refs):
    back_kv = (
        (own[...].astype(f32) + beside[...].astype(f32)) + far[...].astype(f32)
    ).astype(bf16)
    kv_ref[...] = back_kv
    row_ref[:, :HW] = jnp.sum(dq_ref[...].astype(f32), axis=0, keepdims=True)
    row_ref[:, HW:] = jnp.sum(back_kv.astype(f32), axis=0, keepdims=True)
    total = last_last(dq_ref[...], w_ref[:, :HW]) + last_last(back_kv, w_ref[:, HW : 3 * HW])
    store_chunks(total, chunk_refs)


def whole_weight_grads(pairs, after=()):
    widths = [rhs.shape[1] for _, rhs in pairs]
    width = sum(widths)
    count = len(pairs)
    block = 256

    def kernel(*refs):
        out_ref = refs[5 * count]
        start = 0
        for i, columns in enumerate(widths):
            grads = first_first(whole_of(refs[4 * i : 4 * i + 4]), refs[4 * count + i][...])
            out_ref[:, start : start + columns] = grads.astype(bf16)
            start += columns

    (out,) = run(
        "weight_grads",
        kernel,
        [((D, width), bf16)],
        [chunk for lhs, _ in pairs for chunk in lhs] + [rhs for _, rhs in pairs],
        [pl.BlockSpec((ROWS, block), lambda i: (0, i))] * (4 * count)
        + [pl.BlockSpec((TOK, w), lambda i: (0, 0)) for w in widths],
        [pl.BlockSpec((block, width), lambda i: (i, 0))],
        grid=(D // block,),
        after=after,
    )
    return out


def weight_grads(core, pairs, after=()):
    widths = [rhs.shape[1] for _, rhs in pairs]
    width = sum(widths)
    count = len(pairs)
    block = 256

    def kernel(*refs):
        core_ref, rest = refs[0], refs[1:]
        mine_ref, other_ref = rest[5 * count], rest[5 * count + 1]
        first = core_ref[0] == 0
        start = 0
        for i, columns in enumerate(widths):
            grads = first_first(whole_of(rest[4 * i : 4 * i + 4]), rest[4 * count + i][...])
            grads = grads.astype(bf16)
            for j in range(block // 64):
                even = grads[64 * j : 64 * j + 32]
                odd = grads[64 * j + 32 : 64 * j + 64]
                at = (slice(32 * j, 32 * j + 32), slice(start, start + columns))
                mine_ref[at] = jnp.where(first, even, odd)
                other_ref[at] = jnp.where(first, odd, even)
            start += columns

    lhs_spec = pl.BlockSpec((ROWS, block), lambda i: (0, i))
    out_spec = pl.BlockSpec((block // 2, width), lambda i: (i, 0))
    return run(
        "weight_grads",
        kernel,
        [((D // 2, width), bf16)] * 2,
        [core[None]] + [chunk for lhs, _ in pairs for chunk in lhs] + [rhs for _, rhs in pairs],
        [SMEM]
        + [lhs_spec] * (4 * count)
        + [pl.BlockSpec((TOK, w), lambda i: (0, 0)) for w in widths],
        [out_spec, out_spec],
        grid=(D // block,),
        after=after,
    )


def summed(pieces):
    return jnp.sum(pieces.reshape(16, 32, -1), axis=0, dtype=f32)


def pair_kernel(a, b, out_ref):
    out_ref[...] = (a[...].astype(f32) + b[...].astype(f32)).astype(bf16)


def pair_sum(a, b):
    return run("pair_sum", pair_kernel, [(a.shape, bf16)], [a, b], [VMEM] * 2)[0]


def chip_sum(grads, after=()):
    args = [part for mine, other in grads for part in (mine, move(other, dc=1))]
    widths = [mine.shape[1] for mine, _ in grads]
    rows = D // 8

    def kernel(*refs):
        start = 0
        for i, width in enumerate(widths):
            total = refs[2 * i][...].astype(f32) + refs[2 * i + 1][...].astype(f32)
            refs[-1][:, start : start + width] = total.astype(bf16)
            start += width

    return run(
        "chip_sum",
        kernel,
        [((D // 2, sum(widths)), bf16)],
        args,
        [pl.BlockSpec((rows, a.shape[1]), lambda i: (i, 0)) for a in args],
        [pl.BlockSpec((rows, sum(widths)), lambda i: (i, 0))],
        grid=(4,),
        after=after,
    )[0]


def hold_kernel(*refs):
    count = len(refs) // 2
    for k in range(count):
        refs[count + k][...] = refs[k][...]


def hold(arrays, after):
    return run(
        "hold",
        hold_kernel,
        [(a.shape, a.dtype) for a in arrays],
        arrays,
        [VMEM] * len(arrays),
        after=after,
    )


def four(refs, cols):
    parts = [refs[k][..., cols].astype(f32) for k in range(4)]
    return (parts[0] + parts[1]) + (parts[2] + parts[3])


def feedforward_adamw_kernel(zero_ref, one_ref, weight, moment, second, m_ref, s_ref, w_ref):
    zero = four(zero_ref, slice(0, 2 * D))
    for layer, total in enumerate((zero, one_ref[...].astype(f32))):
        for s in range(2):
            at = (layer, slice(None), s, slice(None))
            m_ref[at], s_ref[at], w_ref[at] = adamw_step(
                weight[at],
                moment[at],
                second[at],
                total[:, s * D : (s + 1) * D],
                matrix_rate,
                weight_decay,
            )


def attention_adamw_kernel(
    a0, a1, a2, a3, zero_ref, weight, moment, second, m_ref, s_ref, w_ref
):
    zero = four((a0, a1, a2, a3), slice(0, D))
    one = four(zero_ref, slice(2 * D, 3 * D))
    for layer, total in enumerate((zero, one)):
        for s in range(4):
            at = (layer, slice(None), s, slice(None))
            m_ref[at], s_ref[at], w_ref[at] = adamw_step(
                weight[at],
                moment[at],
                second[at],
                total[:, s * HW : (s + 1) * HW],
                matrix_rate,
                weight_decay,
            )


def matrix_adamw(name, kernel, grads, weight, moment, second, after=()):
    return run(
        name,
        kernel,
        [(weight.shape, f32)] * 3,
        [*grads, weight, moment, second],
        [VMEM] * (len(grads) + 3),
        after=after,
    )


def core_sum_kernel(spot, mine, other, o0, o1, o2, o3):
    for k, ref in enumerate((o0, o1, o2, o3)):
        row = (spot[0] + k) & 3
        ref[0] = (mine[row, 0].astype(f32) + other[row, 0].astype(f32)).astype(bf16)


def core_sum(grads, spot, after=()):
    mine, other = (part.reshape(4, 4, 32, -1) for part in grads)
    other = move(other, dc=1)
    width = mine.shape[-1]
    whole_spec = pl.BlockSpec((4, 1, 32, width), lambda i: (0, i, 0, 0))
    part_spec = pl.BlockSpec((1, 32, width), lambda i: (i, 0, 0))
    return run(
        "core_sum",
        core_sum_kernel,
        [((4, 32, width), bf16)] * 4,
        [spot, mine, other],
        [SMEM, whole_spec, whole_spec],
        [part_spec] * 4,
        grid=(4,),
        after=after,
    )


def y_sum_kernel(spot, p0, p1, p2, p3, o0, o1, o2, o3):
    for k, ref in enumerate((o0, o1, o2, o3)):
        slot = x_slot((spot[1] + k) & 3)
        ref[...] = (
            (p0[slot].astype(f32) + p1[slot].astype(f32))
            + (p2[slot].astype(f32) + p3[slot].astype(f32))
        ).astype(bf16)


def quarter_kernel(p0, p1, p2, p3, out_ref):
    out_ref[...] = (
        (p0[...].astype(f32) + p1[...].astype(f32)) + (p2[...].astype(f32) + p3[...].astype(f32))
    ).astype(bf16)


def quarter_sum(pieces):
    rows, width = pieces.shape[0] // 4, pieces.shape[1]
    return run(
        "quarter_sum",
        quarter_kernel,
        [((rows, width), bf16)],
        [pieces] * 4,
        [pl.BlockSpec((rows // 4, width), lambda i, k=k: (4 * k + i, 0)) for k in range(4)],
        [pl.BlockSpec((rows // 4, width), lambda i: (i, 0))],
        grid=(4,),
    )[0]


def y_sum(parts, spot, after=()):
    terms = [parts[0]] + [move(parts[k], dy=k) for k in (1, 2, 3)]
    width = parts[0].shape[-1]
    return run(
        "y_sum",
        y_sum_kernel,
        [((32, width), bf16)] * 4,
        [spot, *terms],
        [SMEM] + [VMEM] * 4,
        after=after,
    )


def x_terms(parts):
    return [parts[0]] + [move(parts[k], dx=k) for k in (1, 2, 3)]


def vector_grads_kernel(spot, *refs):
    out_ref, whole = refs[-2], refs[-1]
    t = spot[3]
    whole[...] = jnp.zeros((32, D), f32)
    for layer in range(2):
        one, two, qkv, hidden, down = refs[5 * layer : 5 * layer + 5]
        at = 12 * layer
        whole[at : at + 2, :] = one[0:2, :]
        for s in range(4):
            cols = slice(s * HW, (s + 1) * HW)
            whole[at + 2 : at + 3, cols] = jnp.where(t == s, qkv[:, :HW], 0.0)
            whole[at + 3 : at + 4, cols] = jnp.where(t == s, qkv[:, 2 * HW :], 0.0)
            whole[at + 8 + s : at + 9 + s, :] = jnp.where(t == s, hidden[...], 0.0)
        whole[at + 4 : at + 5, :] = two[2:3, :]
        whole[at + 5 : at + 7, :] = two[0:2, :]
        whole[at + 7 : at + 8, :] = down[...]
    out_ref[...] = jnp.concatenate([whole[...], jnp.zeros((96, D), f32)], axis=0).T


def scatter_vectors(spot, rows, after):
    (partial,) = run(
        "vector_grads",
        vector_grads_kernel,
        [((D, 128), f32)],
        [spot, *rows],
        [SMEM] + [VMEM] * len(rows),
        scratch=[pltpu.VMEM((32, D), f32)],
        after=after,
    )
    value = lax.all_to_all(
        partial, ("fsdp", "ctx", "tp"), split_axis=0, concat_axis=0, tiled=True
    )
    return jnp.sum(value.reshape(128, 8, 128), axis=0)[:, :24].T.reshape(2, 12, 8)


def adamw_step(weight, moment, second, gradient, step_rate, decay_rate):
    moment = 0.9 * moment + 0.1 * gradient
    second = 0.95 * second + 0.05 * gradient * gradient
    first_fix = 1.0 - 0.9**STEP
    second_fix = 1.0 - 0.95**STEP
    update = moment / first_fix / (jnp.sqrt(second / second_fix) + 1e-08) + decay_rate * weight
    return (moment, second, weight - step_rate * update)


def body(
    block_input,
    cotangent,
    sequence_starts,
    attention_weight,
    attention_first,
    attention_second,
    feedforward_weight,
    feedforward_first,
    feedforward_second,
    vector_weight,
    vector_first,
    vector_second,
):
    c = lax.axis_index("ctx")
    t = lax.axis_index("tp")
    core = (c & 1).astype(jnp.int32)
    meta = jnp.stack([c, t, sequence_starts[0, 0], sequence_starts[0, 1]]).astype(jnp.int32)
    slopes = jnp.exp2(-8.0 * ((t * 4 + jnp.arange(4, dtype=jnp.int32)).astype(f32) + 1.0) / H)

    fsdp = lax.axis_index("fsdp")
    spot = jnp.stack([fsdp >> 1, (fsdp & 1) + (c >> 1) * 2, c & 1, t]).astype(jnp.int32)
    with jax.named_scope("gather_rest"):
        rest = gather_rest(attention_weight, feedforward_weight)
    with jax.named_scope("gather_first"):
        vector_parts = tp_spread(vector_weight.reshape(24, 8))
        attention_zero, vectors = gather_first(
            attention_weight, vector_parts, t.astype(jnp.int32), core, (meta, slopes)
        )
    attention_of = ((attention_zero, None, 0), (rest, 2, 0))
    up_of = ((rest, 0, 0), (rest, 3, 0))
    down_of = ((rest, 1, 0), (rest, 4, 0))

    input_chunks = turn_rows(block_input, t)
    stream = input_chunks[0]
    kept = []
    normed_own = None
    for layer in range(2):
        vector = lax.slice_in_dim(vectors, 12 * layer, 12 * layer + 12, axis=0)
        bias_query = lax.dynamic_slice(vector, (2, t * HW), (1, HW))
        bias_value = lax.dynamic_slice(vector, (3, t * HW), (1, HW))
        bias_hidden = lax.dynamic_slice(vector, (8 + t, 0), (1, D))
        weight = attention_of[layer]
        qkv_spec = weight_spec(weight, 3 * HW, 0)
        out_spec = weight_spec(weight, HW, 3)
        with jax.named_scope(f"project_{layer}"):
            if layer == 0:
                *normed, kv_own, queries = run(
                    "first",
                    first_kernel,
                    [((ROWS, D), bf16)] * 4 + [((TOK, 2 * HW), bf16), ((TOK, HW), bf16)],
                    [*input_chunks, vector, weight[0], bias_query, bias_value],
                    [VMEM] * 5 + [qkv_spec, VMEM, VMEM],
                )
            else:
                normed = tp_spread(normed_own)
                kv_own, queries = run(
                    "project",
                    project_kernel,
                    [((TOK, 2 * HW), bf16), ((TOK, HW), bf16)],
                    [*normed, weight[0], bias_query, bias_value],
                    [VMEM] * 4 + [qkv_spec, VMEM, VMEM],
                )
            kv_blocks = kv_gather(kv_own)
        with jax.named_scope(f"attend_{layer}"):
            mixed, *partial = run(
                "attend",
                attend_kernel,
                [((TOK, HW), bf16)] + CHUNKS,
                [meta, slopes, queries, *kv_blocks, weight[0]],
                [SMEM, SMEM] + [VMEM] * 5 + [out_spec],
            )
        with jax.named_scope(f"join_attend_{layer}"):
            before = stream
            middle, normed_two_own = join(
                tp_exchange(partial),
                stream,
                vector,
                4,
                5,
                6,
            )
        with jax.named_scope(f"feedforward_{layer}"):
            normed_two = tp_spread(normed_two_own)
            hidden, active, partial = feedforward(
                normed_two, up_of[layer], down_of[layer], bias_hidden
            )
        with jax.named_scope(f"join_feedforward_{layer}"):
            if layer == 0:
                stream, normed_own = join(tp_exchange(partial), middle, vectors, 7, 12, 13)
            else:
                last_partial, last_vector, last_middle = partial, vector, middle
        kept.append(
            (before, normed, queries, kv_blocks, mixed, middle, normed_two, hidden, active)
        )
    back_chunks = turn_rows(cotangent, t)
    back = back_chunks[0]
    back_down_row = jnp.sum(back.astype(f32), axis=0, keepdims=True)
    vector_rows = [None, None]
    pieces = {}
    for layer in (1, 0):
        before, normed, queries, kv_blocks, mixed, middle, normed_two, hidden, active = kept[layer]
        vector = lax.slice_in_dim(vectors, 12 * layer, 12 * layer + 12, axis=0)
        weight = attention_of[layer]
        qkv_spec = weight_spec(weight, 3 * HW, 0)
        out_spec = weight_spec(weight, HW, 3)
        with jax.named_scope(f"back_feedforward_{layer}"):
            if layer == 0:
                back_chunks = tp_spread(back_own)
            back_hidden, hidden_row, partial = feedforward_back(
                back_chunks,
                up_of[layer],
                down_of[layer],
                hidden,
            )
            terms = tp_exchange(partial)
        with jax.named_scope(f"grads_feedforward_{layer}"):
            pairs = [(in_hbm(normed_two), back_hidden), (back_chunks, *in_hbm([active]))]
            if layer == 1:
                grads_ff = whole_weight_grads(pairs)
                pieces["ff1"] = lax.psum_scatter(grads_ff, FC, scatter_dimension=0, tiled=True)
                tied = (grads_ff,)
            else:
                grads_ff = weight_grads(core, pairs)
                tied = (grads_ff[0],)
        with jax.named_scope(f"back_norm_two_{layer}"):
            back_middle, back_attn_own, rows_two = norm_back(
                terms,
                back,
                middle,
                vector[5:6],
                after=tied,
            )
            back_attn = tp_spread(back_attn_own)
        if layer == 0:
            with jax.named_scope("grads_feedforward_0"):
                chip_ff = chip_sum([grads_ff, grads_att], after=(back_attn_own,))
                column_ff = chips_all_to_all(chip_ff, ALONG_Y)
        with jax.named_scope(f"back_attend_{layer}"):
            back_query, part_own, part_beside, part_across, part_corner = run(
                "attend_back",
                attend_back_kernel,
                [((TOK, HW), bf16)] + [((TOK, 2 * HW), bf16)] * 4,
                [
                    meta,
                    slopes,
                    *in_hbm([queries]),
                    *back_attn,
                    *in_hbm([weight[0], *kv_blocks]),
                ],
                [SMEM, SMEM, full_spec(queries)]
                + [VMEM] * 4
                + [out_spec]
                + [full_spec(kv) for kv in kv_blocks],
                after=(chip_ff,) if layer == 0 else (),
            )
        with jax.named_scope(f"back_project_{layer}"):
            beside = move(part_beside, dc=1)
            far = move(pair_sum(part_across, move(part_corner, dc=1)), dx=2)
            if layer == 1:
                held = hold(last_partial[1:], after=(part_own,))
                (stream,) = join(
                    tp_exchange([last_partial[0], *held]), last_middle, last_vector, 7
                )
            else:
                output_chunks = tp_spread(hold([stream], after=(part_own,))[0])
            back_kv, qkv_row, *partial = run(
                "project_back",
                project_back_kernel,
                [((TOK, 2 * HW), bf16), ((1, 3 * HW), f32)] + CHUNKS,
                [back_query, part_own, beside, far, *in_hbm([weight[0]])],
                [VMEM] * 4 + [qkv_spec],
                after=(stream,) if layer == 1 else tuple(output_chunks[1:]),
            )
            terms = tp_exchange(partial)
        with jax.named_scope(f"grads_attention_{layer}"):
            normed = in_hbm(normed)
            grads = weight_grads(
                core,
                [(normed, back_query), (normed, back_kv), (back_attn, *in_hbm([mixed]))],
            )
            if layer == 1:
                grads_att = grads
            else:
                column_ff = quarter_sum(column_ff)
                pieces["ff0"] = chips_all_to_all(column_ff, ALONG_X)
                pieces["att0"] = core_sum(grads, spot)
        with jax.named_scope(f"back_norm_one_{layer}"):
            back, back_own, rows_one = norm_back(
                terms,
                back_middle,
                before,
                vector[0:1],
                after=(grads[0],) if layer == 1 else (pieces["att0"][0], column_ff),
            )
        vector_rows[layer] = (rows_one, rows_two, qkv_row, hidden_row, back_down_row)
        back_down_row = rows_one[2:3]
    with jax.named_scope("input_gradient"):
        input_gradient = assemble(tp_spread(back), spot)
    with jax.named_scope("block_output"):
        block_output = assemble(output_chunks, spot, after=(back_own,))
    with jax.named_scope("scatter_vectors"):
        vector_total = scatter_vectors(
            spot, vector_rows[0] + vector_rows[1], (pieces["ff0"],)
        )
    with jax.named_scope("grads_attention_0"):
        pieces["att0"] = [pieces["att0"][0], *hold(pieces["att0"][1:], after=(back_own,))]
    with jax.named_scope("adamw"):
        zero_terms = [pieces["ff0"].reshape(4, 32, 3 * D)]
        feedforward_out = matrix_adamw(
            "feedforward_adamw",
            feedforward_adamw_kernel,
            [*zero_terms, pieces["ff1"]],
            feedforward_weight,
            feedforward_first,
            feedforward_second,
        )
        attention_out = matrix_adamw(
            "attention_adamw",
            attention_adamw_kernel,
            [*x_terms(y_sum(pieces["att0"], spot, (vector_total,))), *zero_terms],
            attention_weight,
            attention_first,
            attention_second,
            after=(feedforward_out[0],),
        )
        vector_out = adamw_step(
            vector_weight, vector_first, vector_second, vector_total, vector_rate, 0.0
        )
    return (block_output, input_gradient, *attention_out, *feedforward_out, *vector_out)


def solution(mesh):
    tokens = P(FC, None)
    weights = P(None, FC, None, "tp")
    vectors = P(None, None, ("fsdp", "ctx", "tp"))
    in_specs = (tokens, tokens, P("fsdp", None)) + (weights,) * 6 + (vectors,) * 3
    out_specs = (tokens,) * 2 + (weights,) * 6 + (vectors,) * 3
    return jax.shard_map(body, mesh=mesh, in_specs=in_specs, out_specs=out_specs, check_vma=False)
```

```python
import jax
import jax.numpy as jnp
from jax import lax
from jax.experimental import pallas as pl
from jax.experimental.pallas import tpu as pltpu
from jax.sharding import PartitionSpec as P

H = 16
HD = 64
STEP = 10
FC = ("fsdp", "ctx")
NY = 4
NX = 4
TP = 4

norm_eps = 1e-05
gelu_factor = 0.7978845608028654
matrix_rate = 0.05
vector_rate = 0.3
weight_decay = 0.1

f32 = jnp.float32
bf16 = jnp.bfloat16
VMEM_LIMIT = 48 * 1024 * 1024


def place(y, x, core):
    return (y * 2 + (x & 1)) * 4 + (x >> 1) * 2 + core


def shift_perm(dy=0, dx=0, dc=0):
    return [
        (place(y, x, c), place((y + dy) % NY, (x + dx) % NX, (c + dc) % 2))
        for y in range(NY)
        for x in range(NX)
        for c in range(2)
    ]


CHIPS = [
    [place(y, x, core) for y in range(NY) for x in (0, 2, 1, 3)] for core in range(2)
]


ALONG_X = [[place(y, x, core) for x in (0, 2, 1, 3)] for y in range(NY) for core in range(2)]
ALONG_Y = [[place(y, x, core) for y in range(NY)] for x in range(NX) for core in range(2)]


def move(value, dy=0, dx=0, dc=0):
    return lax.ppermute(value, FC, shift_perm(dy, dx, dc))


def move_tp(value, k):
    return lax.ppermute(value, "tp", [(i, (i + k) % TP) for i in range(TP)])


def chips_all_to_all(value, groups=CHIPS):
    return lax.all_to_all(
        value, FC, split_axis=0, concat_axis=0, tiled=True, axis_index_groups=groups
    )


def tp_spread(own):
    return [own] + [move_tp(own, k) for k in (1, 2, 3)]


def tp_exchange(chunks):
    return [chunks[0]] + [move_tp(chunks[k], -k) for k in (1, 2, 3)]


def turn_rows(values, t):
    rows = values.shape[0] // TP
    return [lax.dynamic_slice_in_dim(values, ((t - k) & 3) * rows, rows, 0) for k in range(TP)]


def assemble_kernel(spot, p0, p1, p2, p3, out_ref):
    for k, ref in enumerate((p0, p1, p2, p3)):
        at = pl.multiple_of(((spot[3] - k) & 3) * ROWS, ROWS)
        out_ref[pl.ds(at, ROWS), :] = ref[...]


def assemble(chunks, spot, after=()):
    return run(
        "assemble",
        assemble_kernel,
        [((TOK, D), f32)],
        [spot, *chunks],
        [SMEM] + [VMEM] * 4,
        after=after,
    )[0]


def kv_gather(own):
    across = move(own, dx=2)
    beside = move(own, dc=1)
    return [own, beside, across, move(across, dc=1)]


SMEM = pl.BlockSpec(memory_space=pltpu.SMEM)
VMEM = pl.BlockSpec(memory_space=pltpu.VMEM)
ANY = pl.BlockSpec(memory_space=pl.ANY)
ROWS = 64
TOK = 256
D = 1024
HW = 256


def last_last(a, b):
    return lax.dot_general(a, b, (((1,), (1,)), ((), ())), preferred_element_type=f32)


def first_first(a, b):
    return lax.dot_general(a, b, (((0,), (0,)), ((), ())), preferred_element_type=f32)


def matmul(a, b):
    return jnp.dot(a, b, preferred_element_type=f32)


def whole_of(refs):
    return jnp.concatenate([ref[...] for ref in refs], axis=0)


FIRST_HBM = ("norm_back",)
OUT_HBM = ("weight_grads", "chip_sum")


def in_hbm(arrays):
    return [pltpu.with_memory_space_constraint(array, pltpu.HBM) for array in arrays]


def run(name, kernel, outs, args, specs, out_specs=None, grid=None, scratch=(), after=()):
    count = len(args)
    extra = len(after)

    def wrapped(*refs):
        kernel(*refs[:count], *refs[count + extra :])

    if grid is None and any(spec.block_shape is not None for spec in specs):
        grid = (1,)
    grid_args = {} if grid is None else {"grid": grid}
    return pl.pallas_call(
        wrapped,
        out_shape=[
            pltpu.HBM(shape, dtype)
            if name in OUT_HBM or (k == 0 and name in FIRST_HBM)
            else jax.ShapeDtypeStruct(shape, dtype)
            for k, (shape, dtype) in enumerate(outs)
        ],
        in_specs=list(specs) + [ANY] * extra,
        out_specs=[VMEM] * len(outs) if out_specs is None else out_specs,
        scratch_shapes=list(scratch),
        compiler_params=pltpu.CompilerParams(vmem_limit_bytes=VMEM_LIMIT),
        name=name,
        **grid_args,
    )(*args, *[in_hbm([a])[0] if a.size > 300000 else a for a in after])


def weight_spec(weight, width, column, stepped=False):
    array, slot, offset = weight
    if stepped:
        if slot is None:
            return pl.BlockSpec((D, width), lambda i: (0, offset // width + i))
        return pl.BlockSpec((None, D, width), lambda i: (slot, 0, offset // width + i))
    if slot is None:
        return pl.BlockSpec((D, width), lambda i: (0, column))
    return pl.BlockSpec((None, D, width), lambda i: (slot, 0, column))


def full_spec(array):
    return pl.BlockSpec(array.shape, lambda i: (0,) * array.ndim)


CHUNKS = [((ROWS, D), f32)] + [((ROWS, D), bf16)] * 3


def store_chunks(total, refs):
    for k, ref in enumerate(refs):
        ref[...] = total[k * ROWS : (k + 1) * ROWS].astype(ref.dtype)


def norm_parts(values):
    centre = values - jnp.mean(values, axis=-1, keepdims=True)
    spread = jnp.mean(centre * centre, axis=-1, keepdims=True)
    scale = lax.rsqrt(spread + norm_eps)
    return centre * scale, scale


def spread_first_kernel(t_ref, v0, v1, v2, v3, weight_ref, out_ref):
    group = lax.broadcasted_iota(jnp.int32, (24, 32), 1) >> 3
    columns = jnp.zeros((24, 32), f32)
    for k, part in enumerate((v0, v1, v2, v3)):
        tiled = jnp.concatenate([part[...]] * TP, axis=1)
        columns = jnp.where(group == ((t_ref[0] - k) & 3), tiled, columns)
    high = columns.astype(bf16)
    low = (columns - high.astype(f32)).astype(bf16)
    extra = jnp.concatenate(
        [
            jnp.concatenate([high.astype(f32), low.astype(f32), jnp.zeros((24, 64), f32)], axis=1),
            jnp.zeros((8, 128), f32),
        ],
        axis=0,
    ).astype(bf16)
    slots = [weight_ref[:, s, :].astype(bf16) for s in range(4)]
    for k in range(16):
        for s in range(4):
            out_ref[k, :, s * HW : (s + 1) * HW] = slots[s]
        out_ref[k, :, D:] = extra


def unpack_kernel(core_ref, own_ref, other_ref, weight_ref, vector_ref):
    core = core_ref[0]
    for k in range(16):
        weight_ref[k, core] = own_ref[k, :, :D]
        weight_ref[k, 1 - core] = other_ref[k, :, :D]
        sums = [
            ref[k, :, D : D + 32].astype(f32) + ref[k, :, D + 32 : D + 64].astype(f32)
            for ref in (own_ref, other_ref)
        ]
        even = jnp.where(core == 0, sums[0], sums[1])
        odd = jnp.where(core == 0, sums[1], sums[0])
        vector_ref[:, k * 64 : k * 64 + 32] = even
        vector_ref[:, k * 64 + 32 : k * 64 + 64] = odd


def gather_first(attention_weight, vector_parts, t, core, after):
    (spread,) = run(
        "spread_first",
        spread_first_kernel,
        [((16, 32, D + 128), bf16)],
        [t[None], *vector_parts, attention_weight],
        [SMEM] + [VMEM] * 4 + [pl.BlockSpec((None, 32, 4, HW), lambda i: (0, 0, 0, 0))],
        after=after,
    )
    mine = chips_all_to_all(spread.reshape(512, D + 128))
    other = move(mine, dc=1)
    weight, vector = run(
        "unpack",
        unpack_kernel,
        [((16, 2, 32, D), bf16), ((32, D), f32)],
        [core[None], mine.reshape(16, 32, D + 128), other.reshape(16, 32, D + 128)],
        [SMEM, VMEM, VMEM],
    )
    return weight.reshape(D, D), vector


def x_slot(x):
    return (x & 1) * 2 + (x >> 1)


def pack_kernel(attention_ref, feedforward_ref, out_ref):
    for s in range(2):
        out_ref[s] = feedforward_ref[0, :, s, :].astype(bf16)
        out_ref[3 + s] = feedforward_ref[1, :, s, :].astype(bf16)
    for s in range(4):
        out_ref[2, :, s * HW : (s + 1) * HW] = attention_ref[:, s, :].astype(bf16)


def gather_rest(attention_weight, feedforward_weight):
    (packed,) = run(
        "pack",
        pack_kernel,
        [((5, 32, D), bf16)],
        [attention_weight, feedforward_weight],
        [pl.BlockSpec((None, 32, 4, HW), lambda i: (1, 0, 0, 0)), VMEM],
    )
    return lax.all_gather(packed, FC, axis=1, tiled=True)


def first_kernel(x0, x1, x2, x3, vec, w_ref, bq, bv, n0, n1, n2, n3, kv_ref, q_ref):
    normed = []
    for x, n in zip((x0, x1, x2, x3), (n0, n1, n2, n3)):
        unit, _ = norm_parts(x[...].astype(f32))
        value = (unit * vec[0:1, :] + vec[1:2, :]).astype(bf16)
        n[...] = value
        normed.append(value)
    project(jnp.concatenate(normed, axis=0), w_ref, bq, bv, kv_ref, q_ref)


def project(normed, w_ref, bq, bv, kv_ref, q_ref):
    kv_ref[:, :HW] = matmul(normed, w_ref[:, HW : 2 * HW]).astype(bf16)
    kv_ref[:, HW:] = (matmul(normed, w_ref[:, 2 * HW : 3 * HW]) + bv[...]).astype(bf16)
    q_ref[...] = (matmul(normed, w_ref[:, :HW]) + bq[...]).astype(bf16)


def project_kernel(n0, n1, n2, n3, w_ref, bq, bv, kv_ref, q_ref):
    project(whole_of((n0, n1, n2, n3)), w_ref, bq, bv, kv_ref, q_ref)


def place_of(row, block, t):
    return block * 256 + (((t - (row >> 6)) & 3) << 6) + (row & 63)


def attend_kernel(meta, slopes, q_ref, kv0, kv1, kv2, kv3, w_ref, mixed_ref, *chunk_refs):
    c, t, s1, s2 = meta[0], meta[1], meta[2], meta[3]
    blocks = (kv0, kv1, kv2, kv3)
    row_place = place_of(lax.broadcasted_iota(jnp.int32, (256, 1), 0), c, t)
    row_segment = (row_place >= s1).astype(jnp.int32) + (row_place >= s2).astype(jnp.int32)
    distances = []
    for k in range(4):
        key_place = place_of(lax.broadcasted_iota(jnp.int32, (1, 256), 1), c ^ k, t)
        key_segment = (key_place >= s1).astype(jnp.int32) + (key_place >= s2).astype(jnp.int32)
        gap = row_place - key_place
        allowed = (gap >= 0) & (row_segment == key_segment)
        distances.append(jnp.where(allowed, gap, -1).astype(f32))
    mixed = []
    for h in range(4):
        cols = slice(h * HD, (h + 1) * HD)
        value_cols = slice(256 + h * HD, 256 + (h + 1) * HD)
        query = q_ref[:, cols]
        slope = slopes[h]
        scores = [
            jnp.where(d >= 0, last_last(query, kv[:, cols]) * 0.125 - slope * d, -1e30)
            for d, kv in zip(distances, blocks)
        ]
        top = jnp.maximum(
            jnp.maximum(scores[0], scores[1]), jnp.maximum(scores[2], scores[3])
        ).max(axis=-1, keepdims=True)
        exponent = [jnp.exp(s - top) for s in scores]
        total = (exponent[0] + exponent[1] + exponent[2] + exponent[3]).sum(axis=-1, keepdims=True)
        scale = 1.0 / total
        mixed.append(
            sum(
                matmul((e * scale).astype(bf16), kv[:, value_cols])
                for e, kv in zip(exponent, blocks)
            )
        )
    mixed = jnp.concatenate(mixed, axis=1).astype(bf16)
    mixed_ref[...] = mixed
    store_chunks(last_last(mixed, w_ref[...]), chunk_refs)


def attend_back_kernel(
    meta, slopes, q_ref, b0, b1, b2, b3, w_ref, kv0, kv1, kv2, kv3, dq_ref, dkv0, dkv1, dkv2, dkv3
):
    c, t, s1, s2 = meta[0], meta[1], meta[2], meta[3]
    blocks = (kv0, kv1, kv2, kv3)
    back_blocks = (dkv0, dkv1, dkv2, dkv3)
    back_mixed = matmul(whole_of((b0, b1, b2, b3)), w_ref[...]).astype(bf16)
    row_place = place_of(lax.broadcasted_iota(jnp.int32, (1, 256), 1), c, t)
    row_segment = (row_place >= s1).astype(jnp.int32) + (row_place >= s2).astype(jnp.int32)
    distances = []
    for k in range(4):
        key_place = place_of(lax.broadcasted_iota(jnp.int32, (256, 1), 0), c ^ k, t)
        key_segment = (key_place >= s1).astype(jnp.int32) + (key_place >= s2).astype(jnp.int32)
        gap = row_place - key_place
        allowed = (gap >= 0) & (row_segment == key_segment)
        distances.append(jnp.where(allowed, gap, -1).astype(f32))
    turned = [kv[:, :256].astype(f32).T.astype(bf16) for kv in blocks]
    back_query = []
    back_keys = [[] for _ in range(4)]
    back_values = [[] for _ in range(4)]
    for h in range(4):
        cols = slice(h * HD, (h + 1) * HD)
        value_cols = slice(256 + h * HD, 256 + (h + 1) * HD)
        query = q_ref[:, cols]
        back_rows = back_mixed[:, cols]
        slope = slopes[h]
        scores = [
            jnp.where(d >= 0, last_last(kv[:, cols], query) * 0.125 - slope * d, -1e30)
            for d, kv in zip(distances, blocks)
        ]
        top = jnp.maximum(
            jnp.maximum(scores[0], scores[1]), jnp.maximum(scores[2], scores[3])
        ).max(axis=0, keepdims=True)
        exponent = [jnp.exp(s - top) for s in scores]
        total = (exponent[0] + exponent[1] + exponent[2] + exponent[3]).sum(axis=0, keepdims=True)
        scale = 1.0 / total
        probs = [e * scale for e in exponent]
        back_probs = [last_last(kv[:, value_cols], back_rows) for kv in blocks]
        products = [p * b for p, b in zip(probs, back_probs)]
        delta = (products[0] + products[1] + products[2] + products[3]).sum(axis=0, keepdims=True)
        turned_query = None
        for k in range(4):
            back_scores = (probs[k] * (back_probs[k] - delta)).astype(bf16)
            part = matmul(turned[k][cols], back_scores)
            turned_query = part if turned_query is None else turned_query + part
            back_keys[k].append(matmul(back_scores, query) * 0.125)
            back_values[k].append(matmul(probs[k].astype(bf16), back_rows))
        back_query.append(turned_query)
    dq_ref[...] = (jnp.concatenate(back_query, axis=0) * 0.125).T.astype(bf16)
    for k in range(4):
        back_blocks[k][...] = jnp.concatenate(back_keys[k] + back_values[k], axis=1).astype(bf16)


def join_kernel(p0, p1, p2, p3, base, vec, out_ref, normed_ref, *, bias, gain, shift):
    value = base[...].astype(f32) + (
        (p0[...] + p1[...].astype(f32)) + (p2[...].astype(f32) + p3[...].astype(f32))
    )
    value = value + vec[bias : bias + 1, :]
    out_ref[...] = value
    if normed_ref is not None:
        unit, _ = norm_parts(value)
        normed_ref[...] = (unit * vec[gain : gain + 1, :] + vec[shift : shift + 1, :]).astype(bf16)


def join(terms, base, vec, bias, gain=None, shift=None, after=()):
    def kernel(*refs):
        join_kernel(
            *refs[:7],
            refs[7] if gain is not None else None,
            bias=bias,
            gain=gain,
            shift=shift,
        )

    outs = [((ROWS, D), f32)] + ([((ROWS, D), bf16)] if gain is not None else [])
    return run(
        "join",
        kernel,
        outs,
        [*terms, base, vec],
        [VMEM] * 6,
        after=after,
    )


def norm_back_kernel(p0, p1, p2, p3, base, before, gain, out_ref, low_ref, rows_ref):
    back = (p0[...] + p1[...].astype(f32)) + (p2[...].astype(f32) + p3[...].astype(f32))
    unit, scale = norm_parts(before[...].astype(f32))
    scaled = back * gain[...]
    inner = scaled - jnp.mean(scaled, axis=-1, keepdims=True)
    inner = inner - unit * jnp.mean(scaled * unit, axis=-1, keepdims=True)
    out = base[...].astype(f32) + inner * scale
    out_ref[...] = out
    low = out.astype(bf16)
    low_ref[...] = low
    rows_ref[0:1, :] = jnp.sum(back * unit, axis=0, keepdims=True)
    rows_ref[1:2, :] = jnp.sum(back, axis=0, keepdims=True)
    rows_ref[2:3, :] = jnp.sum(low.astype(f32), axis=0, keepdims=True)
    rows_ref[3:8, :] = jnp.zeros((5, D), f32)


def norm_back(terms, base, before, gain, after=()):
    return run(
        "norm_back",
        norm_back_kernel,
        [((ROWS, D), f32), ((ROWS, D), bf16), ((8, D), f32)],
        [*terms, *in_hbm([base, before]), gain],
        [VMEM] * 4 + [full_spec(base), full_spec(before), VMEM],
        after=after,
    )


def forward_kernel(n0, n1, n2, n3, up, down, bias, hidden_ref, active_ref, c0, c1, c2, c3, total):
    step = pl.program_id(0)
    hidden = matmul(whole_of((n0, n1, n2, n3)), up[...]) + bias[...]
    hidden_ref[...] = hidden
    inner = gelu_factor * (hidden + 0.044715 * hidden * hidden * hidden)
    active = (0.5 * hidden * (1.0 + jnp.tanh(inner))).astype(bf16)
    active_ref[...] = active
    part = last_last(active, down[...])

    @pl.when(step == 0)
    def _():
        total[...] = part

    @pl.when(step > 0)
    def _():
        total[...] += part

    @pl.when(step == pl.num_programs(0) - 1)
    def _():
        store_chunks(total[...], (c0, c1, c2, c3))


def chunk_specs():
    return [pl.BlockSpec((ROWS, D), lambda i: (0, 0))] * 4


BLOCK = 512


def feedforward(chunks, up, down, bias, after=()):
    hidden_spec = pl.BlockSpec((TOK, BLOCK), lambda i: (0, i))
    hidden, active, *partial = run(
        "feedforward",
        forward_kernel,
        [((TOK, D), f32), ((TOK, D), bf16)] + CHUNKS,
        [*chunks, up[0], down[0], bias],
        chunk_specs()
        + [
            weight_spec(up, BLOCK, 0, True),
            weight_spec(down, BLOCK, 0, True),
            pl.BlockSpec((1, BLOCK), lambda i: (0, i)),
        ],
        [hidden_spec, hidden_spec] + chunk_specs(),
        grid=(D // BLOCK,),
        scratch=[pltpu.VMEM((TOK, D), f32)],
        after=after,
    )
    return hidden, active, partial


def backward_kernel(b0, b1, b2, b3, up, down, hidden_ref, back_ref, row_ref, c0, c1, c2, c3, total):
    step = pl.program_id(0)
    back_active = matmul(whole_of((b0, b1, b2, b3)), down[...])
    u = hidden_ref[...]
    square = u * u
    bent = jnp.tanh(gelu_factor * (u + 0.044715 * square * u))
    slope = 0.5 * (1.0 + bent) + 0.5 * u * (1.0 - bent * bent) * gelu_factor * (
        1.0 + 3 * 0.044715 * square
    )
    back = (back_active * slope).astype(bf16)
    back_ref[...] = back
    row_ref[...] = jnp.sum(back.astype(f32), axis=0, keepdims=True)
    part = last_last(back, up[...])

    @pl.when(step == 0)
    def _():
        total[...] = part

    @pl.when(step > 0)
    def _():
        total[...] += part

    @pl.when(step == pl.num_programs(0) - 1)
    def _():
        store_chunks(total[...], (c0, c1, c2, c3))


def feedforward_back(chunks, up, down, hidden, after=()):
    hidden_spec = pl.BlockSpec((TOK, BLOCK), lambda i: (0, i))
    row_spec = pl.BlockSpec((1, BLOCK), lambda i: (0, i))
    back, row, *partial = run(
        "feedforward_back",
        backward_kernel,
        [((TOK, D), bf16), ((1, D), f32)] + CHUNKS,
        [*chunks, up[0], down[0], hidden],
        chunk_specs()
        + [weight_spec(up, BLOCK, 0, True), weight_spec(down, BLOCK, 0, True), hidden_spec],
        [hidden_spec, row_spec] + chunk_specs(),
        grid=(D // BLOCK,),
        scratch=[pltpu.VMEM((TOK, D), f32)],
        after=after,
    )
    return back, row, partial


def project_back_kernel(dq_ref, own, beside, far, w_ref, kv_ref, row_ref, *chunk_refs):
    back_kv = (
        (own[...].astype(f32) + beside[...].astype(f32)) + far[...].astype(f32)
    ).astype(bf16)
    kv_ref[...] = back_kv
    row_ref[:, :HW] = jnp.sum(dq_ref[...].astype(f32), axis=0, keepdims=True)
    row_ref[:, HW:] = jnp.sum(back_kv.astype(f32), axis=0, keepdims=True)
    total = last_last(dq_ref[...], w_ref[:, :HW]) + last_last(back_kv, w_ref[:, HW : 3 * HW])
    store_chunks(total, chunk_refs)


def whole_weight_grads(pairs, after=()):
    widths = [rhs.shape[1] for _, rhs in pairs]
    width = sum(widths)
    count = len(pairs)
    block = 256

    def kernel(*refs):
        out_ref = refs[5 * count]
        start = 0
        for i, columns in enumerate(widths):
            grads = first_first(whole_of(refs[4 * i : 4 * i + 4]), refs[4 * count + i][...])
            out_ref[:, start : start + columns] = grads.astype(bf16)
            start += columns

    (out,) = run(
        "weight_grads",
        kernel,
        [((D, width), bf16)],
        [chunk for lhs, _ in pairs for chunk in lhs] + [rhs for _, rhs in pairs],
        [pl.BlockSpec((ROWS, block), lambda i: (0, i))] * (4 * count)
        + [pl.BlockSpec((TOK, w), lambda i: (0, 0)) for w in widths],
        [pl.BlockSpec((block, width), lambda i: (i, 0))],
        grid=(D // block,),
        after=after,
    )
    return out


def weight_grads(core, pairs, after=()):
    widths = [rhs.shape[1] for _, rhs in pairs]
    width = sum(widths)
    count = len(pairs)
    block = 256

    def kernel(*refs):
        core_ref, rest = refs[0], refs[1:]
        mine_ref, other_ref = rest[5 * count], rest[5 * count + 1]
        first = core_ref[0] == 0
        start = 0
        for i, columns in enumerate(widths):
            grads = first_first(whole_of(rest[4 * i : 4 * i + 4]), rest[4 * count + i][...])
            grads = grads.astype(bf16)
            for j in range(block // 64):
                even = grads[64 * j : 64 * j + 32]
                odd = grads[64 * j + 32 : 64 * j + 64]
                at = (slice(32 * j, 32 * j + 32), slice(start, start + columns))
                mine_ref[at] = jnp.where(first, even, odd)
                other_ref[at] = jnp.where(first, odd, even)
            start += columns

    lhs_spec = pl.BlockSpec((ROWS, block), lambda i: (0, i))
    out_spec = pl.BlockSpec((block // 2, width), lambda i: (i, 0))
    return run(
        "weight_grads",
        kernel,
        [((D // 2, width), bf16)] * 2,
        [core[None]] + [chunk for lhs, _ in pairs for chunk in lhs] + [rhs for _, rhs in pairs],
        [SMEM]
        + [lhs_spec] * (4 * count)
        + [pl.BlockSpec((TOK, w), lambda i: (0, 0)) for w in widths],
        [out_spec, out_spec],
        grid=(D // block,),
        after=after,
    )


def summed(pieces):
    return jnp.sum(pieces.reshape(16, 32, -1), axis=0, dtype=f32)


def pair_kernel(a, b, out_ref):
    out_ref[...] = (a[...].astype(f32) + b[...].astype(f32)).astype(bf16)


def pair_sum(a, b):
    return run("pair_sum", pair_kernel, [(a.shape, bf16)], [a, b], [VMEM] * 2)[0]


def chip_sum(grads, after=()):
    args = [part for mine, other in grads for part in (mine, move(other, dc=1))]
    widths = [mine.shape[1] for mine, _ in grads]
    rows = D // 8

    def kernel(*refs):
        start = 0
        for i, width in enumerate(widths):
            total = refs[2 * i][...].astype(f32) + refs[2 * i + 1][...].astype(f32)
            refs[-1][:, start : start + width] = total.astype(bf16)
            start += width

    return run(
        "chip_sum",
        kernel,
        [((D // 2, sum(widths)), bf16)],
        args,
        [pl.BlockSpec((rows, a.shape[1]), lambda i: (i, 0)) for a in args],
        [pl.BlockSpec((rows, sum(widths)), lambda i: (i, 0))],
        grid=(4,),
        after=after,
    )[0]


def hold_kernel(*refs):
    count = len(refs) // 2
    for k in range(count):
        refs[count + k][...] = refs[k][...]


def hold(arrays, after):
    return run(
        "hold",
        hold_kernel,
        [(a.shape, a.dtype) for a in arrays],
        arrays,
        [VMEM] * len(arrays),
        after=after,
    )


def four(refs, cols):
    parts = [refs[k][..., cols].astype(f32) for k in range(4)]
    return (parts[0] + parts[1]) + (parts[2] + parts[3])


def feedforward_adamw_kernel(zero_ref, one_ref, weight, moment, second, m_ref, s_ref, w_ref):
    zero = four(zero_ref, slice(0, 2 * D))
    for layer, total in enumerate((zero, one_ref[...].astype(f32))):
        for s in range(2):
            at = (layer, slice(None), s, slice(None))
            m_ref[at], s_ref[at], w_ref[at] = adamw_step(
                weight[at],
                moment[at],
                second[at],
                total[:, s * D : (s + 1) * D],
                matrix_rate,
                weight_decay,
            )


def attention_adamw_kernel(
    a0, a1, a2, a3, zero_ref, weight, moment, second, m_ref, s_ref, w_ref
):
    zero = four((a0, a1, a2, a3), slice(0, D))
    one = four(zero_ref, slice(2 * D, 3 * D))
    for layer, total in enumerate((zero, one)):
        for s in range(4):
            at = (layer, slice(None), s, slice(None))
            m_ref[at], s_ref[at], w_ref[at] = adamw_step(
                weight[at],
                moment[at],
                second[at],
                total[:, s * HW : (s + 1) * HW],
                matrix_rate,
                weight_decay,
            )


def matrix_adamw(name, kernel, grads, weight, moment, second, after=()):
    return run(
        name,
        kernel,
        [(weight.shape, f32)] * 3,
        [*grads, weight, moment, second],
        [VMEM] * (len(grads) + 3),
        after=after,
    )


def core_sum_kernel(spot, mine, other, o0, o1, o2, o3):
    for k, ref in enumerate((o0, o1, o2, o3)):
        row = (spot[0] + k) & 3
        ref[0] = (mine[row, 0].astype(f32) + other[row, 0].astype(f32)).astype(bf16)


def core_sum(grads, spot, after=()):
    mine, other = (part.reshape(4, 4, 32, -1) for part in grads)
    other = move(other, dc=1)
    width = mine.shape[-1]
    whole_spec = pl.BlockSpec((4, 1, 32, width), lambda i: (0, i, 0, 0))
    part_spec = pl.BlockSpec((1, 32, width), lambda i: (i, 0, 0))
    return run(
        "core_sum",
        core_sum_kernel,
        [((4, 32, width), bf16)] * 4,
        [spot, mine, other],
        [SMEM, whole_spec, whole_spec],
        [part_spec] * 4,
        grid=(4,),
        after=after,
    )


def y_sum_kernel(spot, p0, p1, p2, p3, o0, o1, o2, o3):
    for k, ref in enumerate((o0, o1, o2, o3)):
        slot = x_slot((spot[1] + k) & 3)
        ref[...] = (
            (p0[slot].astype(f32) + p1[slot].astype(f32))
            + (p2[slot].astype(f32) + p3[slot].astype(f32))
        ).astype(bf16)


def quarter_kernel(p0, p1, p2, p3, out_ref):
    out_ref[...] = (
        (p0[...].astype(f32) + p1[...].astype(f32)) + (p2[...].astype(f32) + p3[...].astype(f32))
    ).astype(bf16)


def quarter_sum(pieces):
    rows, width = pieces.shape[0] // 4, pieces.shape[1]
    return run(
        "quarter_sum",
        quarter_kernel,
        [((rows, width), bf16)],
        [pieces] * 4,
        [pl.BlockSpec((rows // 4, width), lambda i, k=k: (4 * k + i, 0)) for k in range(4)],
        [pl.BlockSpec((rows // 4, width), lambda i: (i, 0))],
        grid=(4,),
    )[0]


def y_sum(parts, spot, after=()):
    terms = [parts[0]] + [move(parts[k], dy=k) for k in (1, 2, 3)]
    width = parts[0].shape[-1]
    return run(
        "y_sum",
        y_sum_kernel,
        [((32, width), bf16)] * 4,
        [spot, *terms],
        [SMEM] + [VMEM] * 4,
        after=after,
    )


def x_terms(parts):
    return [parts[0]] + [move(parts[k], dx=k) for k in (1, 2, 3)]


def vector_grads_kernel(spot, *refs):
    out_ref, whole = refs[-2], refs[-1]
    t = spot[3]
    whole[...] = jnp.zeros((32, D), f32)
    for layer in range(2):
        one, two, qkv, hidden, down = refs[5 * layer : 5 * layer + 5]
        at = 12 * layer
        whole[at : at + 2, :] = one[0:2, :]
        for s in range(4):
            cols = slice(s * HW, (s + 1) * HW)
            whole[at + 2 : at + 3, cols] = jnp.where(t == s, qkv[:, :HW], 0.0)
            whole[at + 3 : at + 4, cols] = jnp.where(t == s, qkv[:, 2 * HW :], 0.0)
            whole[at + 8 + s : at + 9 + s, :] = jnp.where(t == s, hidden[...], 0.0)
        whole[at + 4 : at + 5, :] = two[2:3, :]
        whole[at + 5 : at + 7, :] = two[0:2, :]
        whole[at + 7 : at + 8, :] = down[...]
    out_ref[...] = jnp.concatenate([whole[...], jnp.zeros((96, D), f32)], axis=0).T


def scatter_vectors(spot, rows, after):
    (partial,) = run(
        "vector_grads",
        vector_grads_kernel,
        [((D, 128), f32)],
        [spot, *rows[:5], *in_hbm(rows[5:])],
        [SMEM] + [full_spec(row) for row in rows],
        scratch=[pltpu.VMEM((32, D), f32)],
        after=after,
    )
    value = lax.all_to_all(
        partial, ("fsdp", "ctx", "tp"), split_axis=0, concat_axis=0, tiled=True
    )
    return jnp.sum(value.reshape(128, 8, 128), axis=0)[:, :24].T.reshape(2, 12, 8)


def adamw_step(weight, moment, second, gradient, step_rate, decay_rate):
    moment = 0.9 * moment + 0.1 * gradient
    second = 0.95 * second + 0.05 * gradient * gradient
    first_fix = 1.0 - 0.9**STEP
    second_fix = 1.0 - 0.95**STEP
    update = moment / first_fix / (jnp.sqrt(second / second_fix) + 1e-08) + decay_rate * weight
    return (moment, second, weight - step_rate * update)


def body(
    block_input,
    cotangent,
    sequence_starts,
    attention_weight,
    attention_first,
    attention_second,
    feedforward_weight,
    feedforward_first,
    feedforward_second,
    vector_weight,
    vector_first,
    vector_second,
):
    c = lax.axis_index("ctx")
    t = lax.axis_index("tp")
    core = (c & 1).astype(jnp.int32)
    meta = jnp.stack([c, t, sequence_starts[0, 0], sequence_starts[0, 1]]).astype(jnp.int32)
    slopes = jnp.exp2(-8.0 * ((t * 4 + jnp.arange(4, dtype=jnp.int32)).astype(f32) + 1.0) / H)

    fsdp = lax.axis_index("fsdp")
    spot = jnp.stack([fsdp >> 1, (fsdp & 1) + (c >> 1) * 2, c & 1, t]).astype(jnp.int32)
    with jax.named_scope("gather_rest"):
        rest = gather_rest(attention_weight, feedforward_weight)
    with jax.named_scope("gather_first"):
        vector_parts = tp_spread(vector_weight.reshape(24, 8))
        attention_zero, vectors = gather_first(
            attention_weight, vector_parts, t.astype(jnp.int32), core, (meta, slopes)
        )
    attention_of = ((attention_zero, None, 0), (rest, 2, 0))
    up_of = ((rest, 0, 0), (rest, 3, 0))
    down_of = ((rest, 1, 0), (rest, 4, 0))

    input_chunks = turn_rows(block_input, t)
    stream = input_chunks[0]
    kept = []
    normed_own = None
    for layer in range(2):
        vector = lax.slice_in_dim(vectors, 12 * layer, 12 * layer + 12, axis=0)
        bias_query = lax.dynamic_slice(vector, (2, t * HW), (1, HW))
        bias_value = lax.dynamic_slice(vector, (3, t * HW), (1, HW))
        bias_hidden = lax.dynamic_slice(vector, (8 + t, 0), (1, D))
        weight = attention_of[layer]
        qkv_spec = weight_spec(weight, 3 * HW, 0)
        out_spec = weight_spec(weight, HW, 3)
        with jax.named_scope(f"project_{layer}"):
            if layer == 0:
                *normed, kv_own, queries = run(
                    "first",
                    first_kernel,
                    [((ROWS, D), bf16)] * 4 + [((TOK, 2 * HW), bf16), ((TOK, HW), bf16)],
                    [*input_chunks, vector, weight[0], bias_query, bias_value],
                    [VMEM] * 5 + [qkv_spec, VMEM, VMEM],
                )
            else:
                normed = tp_spread(normed_own)
                kv_own, queries = run(
                    "project",
                    project_kernel,
                    [((TOK, 2 * HW), bf16), ((TOK, HW), bf16)],
                    [*normed, weight[0], bias_query, bias_value],
                    [VMEM] * 4 + [qkv_spec, VMEM, VMEM],
                )
            kv_blocks = kv_gather(kv_own)
        with jax.named_scope(f"attend_{layer}"):
            mixed, *partial = run(
                "attend",
                attend_kernel,
                [((TOK, HW), bf16)] + CHUNKS,
                [meta, slopes, queries, *kv_blocks, weight[0]],
                [SMEM, SMEM] + [VMEM] * 5 + [out_spec],
            )
        with jax.named_scope(f"join_attend_{layer}"):
            before = stream
            middle, normed_two_own = join(
                tp_exchange(partial),
                stream,
                vector,
                4,
                5,
                6,
            )
        with jax.named_scope(f"feedforward_{layer}"):
            normed_two = tp_spread(normed_two_own)
            hidden, active, partial = feedforward(
                normed_two, up_of[layer], down_of[layer], bias_hidden
            )
        with jax.named_scope(f"join_feedforward_{layer}"):
            if layer == 0:
                stream, normed_own = join(tp_exchange(partial), middle, vectors, 7, 12, 13)
            else:
                last_partial, last_vector, last_middle = partial, vector, middle
        kept.append(
            (before, normed, queries, kv_blocks, mixed, middle, normed_two, hidden, active)
        )
    back_chunks = turn_rows(cotangent, t)
    back = back_chunks[0]
    back_down_row = jnp.sum(back.astype(f32), axis=0, keepdims=True)
    vector_rows = [None, None]
    pieces = {}
    for layer in (1, 0):
        before, normed, queries, kv_blocks, mixed, middle, normed_two, hidden, active = kept[layer]
        vector = lax.slice_in_dim(vectors, 12 * layer, 12 * layer + 12, axis=0)
        weight = attention_of[layer]
        qkv_spec = weight_spec(weight, 3 * HW, 0)
        out_spec = weight_spec(weight, HW, 3)
        with jax.named_scope(f"back_feedforward_{layer}"):
            if layer == 0:
                back_chunks = tp_spread(back_own)
            back_hidden, hidden_row, partial = feedforward_back(
                back_chunks,
                up_of[layer],
                down_of[layer],
                hidden,
            )
            terms = tp_exchange(partial)
        with jax.named_scope(f"grads_feedforward_{layer}"):
            pairs = [(in_hbm(normed_two), back_hidden), (back_chunks, *in_hbm([active]))]
            if layer == 1:
                grads_ff = whole_weight_grads(pairs)
                pieces["ff1"] = lax.psum_scatter(grads_ff, FC, scatter_dimension=0, tiled=True)
                tied = (grads_ff,)
            else:
                grads_ff = weight_grads(core, pairs)
                tied = (grads_ff[0],)
        with jax.named_scope(f"back_norm_two_{layer}"):
            back_middle, back_attn_own, rows_two = norm_back(
                terms,
                back,
                middle,
                vector[5:6],
                after=tied,
            )
            back_attn = tp_spread(back_attn_own)
        if layer == 0:
            with jax.named_scope("grads_feedforward_0"):
                chip_ff = chip_sum([grads_ff, grads_att], after=(back_attn_own,))
                column_ff = chips_all_to_all(chip_ff, ALONG_Y)
        with jax.named_scope(f"back_attend_{layer}"):
            back_query, part_own, part_beside, part_across, part_corner = run(
                "attend_back",
                attend_back_kernel,
                [((TOK, HW), bf16)] + [((TOK, 2 * HW), bf16)] * 4,
                [
                    meta,
                    slopes,
                    *in_hbm([queries]),
                    *back_attn,
                    *in_hbm([weight[0], *kv_blocks]),
                ],
                [SMEM, SMEM, full_spec(queries)]
                + [VMEM] * 4
                + [out_spec]
                + [full_spec(kv) for kv in kv_blocks],
                after=(chip_ff,) if layer == 0 else (),
            )
        with jax.named_scope(f"back_project_{layer}"):
            beside = move(part_beside, dc=1)
            far = move(pair_sum(part_across, move(part_corner, dc=1)), dx=2)
            if layer == 1:
                held = hold(last_partial[1:], after=(part_own,))
                (stream,) = join(
                    tp_exchange([last_partial[0], *held]), last_middle, last_vector, 7
                )
            else:
                output_chunks = tp_spread(hold([stream], after=(part_own,))[0])
            back_kv, qkv_row, *partial = run(
                "project_back",
                project_back_kernel,
                [((TOK, 2 * HW), bf16), ((1, 3 * HW), f32)] + CHUNKS,
                [back_query, part_own, beside, far, *in_hbm([weight[0]])],
                [VMEM] * 4 + [qkv_spec],
                after=(stream,) if layer == 1 else tuple(output_chunks[1:]),
            )
            terms = tp_exchange(partial)
        with jax.named_scope(f"grads_attention_{layer}"):
            normed = in_hbm(normed)
            grads = weight_grads(
                core,
                [(normed, back_query), (normed, back_kv), (back_attn, *in_hbm([mixed]))],
            )
            if layer == 1:
                grads_att = grads
            else:
                column_ff = quarter_sum(column_ff)
                pieces["ff0"] = chips_all_to_all(column_ff, ALONG_X)
                pieces["att0"] = core_sum(grads, spot)
        with jax.named_scope(f"back_norm_one_{layer}"):
            back, back_own, rows_one = norm_back(
                terms,
                back_middle,
                before,
                vector[0:1],
                after=(grads[0],) if layer == 1 else (pieces["att0"][0], column_ff),
            )
        vector_rows[layer] = (rows_one, rows_two, qkv_row, hidden_row, back_down_row)
        back_down_row = rows_one[2:3]
    with jax.named_scope("input_gradient"):
        input_gradient = assemble(tp_spread(back), spot)
    with jax.named_scope("block_output"):
        block_output = assemble(output_chunks, spot, after=(back_own,))
    with jax.named_scope("scatter_vectors"):
        vector_total = scatter_vectors(
            spot, vector_rows[0] + vector_rows[1], (pieces["ff0"],)
        )
    with jax.named_scope("grads_attention_0"):
        pieces["att0"] = [pieces["att0"][0], *hold(pieces["att0"][1:], after=(back_own,))]
    with jax.named_scope("adamw"):
        zero_terms = [pieces["ff0"].reshape(4, 32, 3 * D)]
        feedforward_out = matrix_adamw(
            "feedforward_adamw",
            feedforward_adamw_kernel,
            [*zero_terms, pieces["ff1"]],
            feedforward_weight,
            feedforward_first,
            feedforward_second,
        )
        attention_out = matrix_adamw(
            "attention_adamw",
            attention_adamw_kernel,
            [*x_terms(y_sum(pieces["att0"], spot, (vector_total,))), *zero_terms],
            attention_weight,
            attention_first,
            attention_second,
            after=(feedforward_out[0],),
        )
        vector_out = adamw_step(
            vector_weight, vector_first, vector_second, vector_total, vector_rate, 0.0
        )
    return (block_output, input_gradient, *attention_out, *feedforward_out, *vector_out)


def solution(mesh):
    tokens = P(FC, None)
    weights = P(None, FC, None, "tp")
    vectors = P(None, None, ("fsdp", "ctx", "tp"))
    in_specs = (tokens, tokens, P("fsdp", None)) + (weights,) * 6 + (vectors,) * 3
    out_specs = (tokens,) * 2 + (weights,) * 6 + (vectors,) * 3
    return jax.shard_map(body, mesh=mesh, in_specs=in_specs, out_specs=out_specs, check_vma=False)
```
